32 devices in a mesh: tile: 16 (over z, y, core), group: 2 (over x).
Axes of the slice: x: 2, y: 2, z: 4, core: 2. Of those that a mesh axis runs over, the one named last changes fastest.
Arguments:
- latents: bfloat16 [192, 128, 1536], P(('tile', 'group')), may hold values from -6 to 6
- window_index: int32 [384], P(('tile', 'group')), may hold values from 0 to 2039
- window_len: int32 [384], P(('tile', 'group')), may hold values from 1 to 64
- live_blocks: int32 [32], P(('tile', 'group')), may hold values from 0 to 6, as said below
- norm_gain: float32 [1536], replicated, may hold values from 0.1 to 1.9
- w_qkv: bfloat16 [1536, 4608], P('group', 'tile'), may hold values from -0.15625 to 0.15625
- w_out: bfloat16 [1536, 1536], P('group', 'tile'), may hold values from -0.15625 to 0.15625
Outputs:
- refined: bfloat16 [192, 128, 1536], P(('tile', 'group'))
The draws below stay inside these ranges and needn't reach their ends.
Inputs may be any that keep to these rules, and one draw needn't show every extreme that they name: `live_blocks`: the device at tile index i and the device at tile index i + 8 in the same group form a pair; at most one of a pair holds more than 4 live blocks, the two hold at most 8 together, and in every draw some pair holds exactly 6 and 2.
All inputs are finite; a program needn't handle non-finite values.
Results may differ from the reference program's by a relative error of at most 0.0033.
Values may be sent and summed in bfloat16 or wider, within the bound.
No kernel may reach another device: no remote copies, remote signals or barrier semaphores. Data moves between devices by JAX's collectives and lax.ppermute only.
A program may use at most 128 MiB of HBM per device.

```python
import math
import jax
import jax.numpy as jnp
from jax import lax

D = 1536
HEADS = 24
HEAD_DIM = 64
WIN_SIDE = 8
WIN_ROWS = 34
WIN_COLS = 60
SLOTS = 6
CAP = 4
WIN_TOK = 64
BLOCK = 128
BLOCKS = 192
WINDOWS = 384
N_TILE = 16
N_GROUP = 2


def draw_window_len(key, part):
    key_full, key_part = jax.random.split(key, 2)
    full_pick = jax.random.randint(key_full, (WINDOWS,), 0, 5) < 3
    partial_len = jax.random.randint(key_part, (WINDOWS,), 1, WIN_TOK + 1)
    return jnp.where(full_pick, WIN_TOK, partial_len).astype(jnp.int32)


def draw_live_blocks(key, part):
    half_tiles = N_TILE // 2
    key_hot, key_cold, key_flip = jax.random.split(key, 3)
    heavy = jax.random.randint(key_hot, (half_tiles, N_GROUP), CAP, SLOTS + 1)
    heavy = heavy.at[0, 0].set(SLOTS)
    spare_room = 2 * CAP - heavy
    light = jax.random.randint(key_cold, (half_tiles, N_GROUP), 0, 1048576) % (spare_room + 1)
    light = light.at[0, 0].set(2 * CAP - SLOTS)
    flipped = jax.random.randint(key_flip, (half_tiles, N_GROUP), 0, 2) == 1
    lower = jnp.where(flipped, heavy, light)
    upper = jnp.where(flipped, light, heavy)
    return jnp.concatenate([lower, upper], axis=0).reshape(N_TILE * N_GROUP).astype(jnp.int32)


def set_ends(drawn, key, smallest, high):
    shape = drawn.shape
    place = [jax.random.randint(jax.random.fold_in(key, axis), (), 0, shape[axis]) for axis in range(len(shape))]
    drawn = drawn.at[tuple(place)].set(smallest)
    longest = shape.index(max(shape))
    place[longest] = (place[longest] + 1) % shape[longest]
    return drawn.at[tuple(place)].set(high)


def block_scale(stream_key, extent, cuts, low, top_value):
    def one(axis_at, shards_of):
        steps = jax.random.uniform(jax.random.fold_in(jax.random.fold_in(stream_key, 6), axis_at), (shards_of,), jnp.float32, low / len(cuts), top_value / len(cuts))
        return jnp.repeat(jnp.exp(steps), extent[axis_at] // shards_of).reshape((-1,) + (1,) * (len(extent) - axis_at - 1))

    level = one(*cuts[0])
    for cut in cuts[1:]:
        level = level * one(*cut)
    return level


def normal_values(stream_key, shape, deviation, reach, shards=(), kind=jnp.bfloat16):
    gain = block_scale(stream_key, shape, shards, -0.22, 0.18) if shards else 1.0
    result = jax.random.normal(stream_key, shape, jnp.float32) * deviation * gain
    return jnp.minimum(jnp.maximum(result, -reach), reach).astype(kind)


def setup_inputs(seed: int = 0) -> dict:
    seeds = jax.random.split(jax.random.key(seed), 8)
    return {
        "latents": normal_values(seeds[0], (BLOCKS, BLOCK, D), 1.0, 6.0, ((0, 32),)),
        "window_index": set_ends(jax.random.randint(seeds[1], (WINDOWS,), 0, WIN_ROWS * WIN_COLS), jax.random.fold_in(seeds[1], 1), 0, (WIN_ROWS * WIN_COLS) - 1).astype(jnp.int32),
        "window_len": draw_window_len(jax.random.fold_in(seeds[7], 71), 0),
        "live_blocks": draw_live_blocks(jax.random.fold_in(seeds[7], 71), 0),
        "norm_gain": jnp.clip(1.0 + 0.18 * jax.random.normal(seeds[4], (D,), jnp.float32), 0.1, 1.9),
        "w_qkv": normal_values(seeds[5], (D, 3 * D), D ** -0.5, 0.15625, ((0, 2), (1, 16))),
        "w_out": normal_values(seeds[6], (D, D), D ** -0.5, 0.15625, ((0, 2), (1, 16))),
    }


def position_table(window_ids):
    token_ids = jnp.arange(WIN_TOK, dtype=jnp.int32)
    row_pos = window_ids[:, None] // WIN_COLS * WIN_SIDE + token_ids[None, :] // WIN_SIDE
    col_pos = window_ids[:, None] % WIN_COLS * WIN_SIDE + token_ids[None, :] % WIN_SIDE
    quarter = D // 4
    frequency = jnp.exp(jnp.arange(quarter, dtype=jnp.float32) * (-math.log(10000.0) / quarter))
    row_angle = row_pos.astype(jnp.float32)[:, :, None] * frequency
    col_angle = col_pos.astype(jnp.float32)[:, :, None] * frequency
    return jnp.concatenate([jnp.sin(row_angle), jnp.cos(row_angle), jnp.sin(col_angle), jnp.cos(col_angle)], axis=-1)

def head_norm(values):
    return (values * lax.rsqrt(lax.optimization_barrier(jnp.mean(values * values, axis=-1, keepdims=True)) + 1e-06)).astype(jnp.bfloat16)

def window_layer(blocks_in, window_ids, window_lens, norm_gain, w_qkv, w_out):
    window_count = window_ids.shape[0]
    stream = blocks_in.reshape(window_count, WIN_TOK, D).astype(jnp.float32) + position_table(window_ids)
    scale = lax.rsqrt(lax.optimization_barrier(jnp.mean(stream * stream, axis=-1, keepdims=True)) + 1e-06)
    normed = (stream * scale * norm_gain.astype(jnp.float32)).astype(jnp.bfloat16).reshape(window_count * WIN_TOK, D)
    projected = jnp.dot(normed, w_qkv, preferred_element_type=jnp.float32)
    projected = projected.reshape(window_count, WIN_TOK, 3, HEADS, HEAD_DIM)
    queries = head_norm(projected[:, :, 0])
    keys = head_norm(projected[:, :, 1])
    values = projected[:, :, 2].astype(jnp.bfloat16)
    scores = jnp.einsum('wqhd,wkhd->whqk', queries.astype(jnp.float32), keys.astype(jnp.float32)) * HEAD_DIM ** (-0.5)
    key_mask = jnp.arange(WIN_TOK, dtype=jnp.int32)[None, :] < window_lens[:, None]
    weights = jnp.exp(scores) * key_mask[:, None, None, :].astype(jnp.float32)
    probs = (weights / lax.optimization_barrier(jnp.sum(weights, axis=-1, keepdims=True))).astype(jnp.bfloat16)
    attended = jnp.einsum('whqk,wkhd->wqhd', probs.astype(jnp.float32), values.astype(jnp.float32))
    attended = attended.astype(jnp.bfloat16).reshape(window_count * WIN_TOK, D)
    update = jnp.dot(attended, w_out, preferred_element_type=jnp.float32)
    base = blocks_in.reshape(window_count * WIN_TOK, D).astype(jnp.float32)
    token_live = key_mask.reshape(window_count * WIN_TOK)[:, None]
    return jnp.where(token_live, base + update, base).astype(jnp.bfloat16).reshape(blocks_in.shape)

def reference(latents, window_index, window_len, live_blocks, norm_gain, w_qkv, w_out):
    device_count = BLOCKS // SLOTS

    def one_device(inputs):
        blocks_in, window_ids, window_lens, live_count = inputs
        finished = window_layer(blocks_in, window_ids, window_lens, norm_gain, w_qkv, w_out)
        slot_live = jnp.arange(SLOTS, dtype=jnp.int32) < live_count
        return jnp.where(slot_live[:, None, None], finished, blocks_in)
    refined = lax.map(one_device, (latents.reshape(device_count, SLOTS, BLOCK, D), window_index.reshape(device_count, 2 * SLOTS), window_len.reshape(device_count, 2 * SLOTS), live_blocks))
    return refined.reshape(BLOCKS, BLOCK, D)
```

```python
import functools
import math

import jax
import jax.numpy as jnp
from jax import lax
from jax.experimental import pallas as pl
from jax.experimental.pallas import tpu as pltpu
from jax.sharding import PartitionSpec as P

HEAD_DIM = 64
WIN_SIDE = 8
WIN_COLS = 60
WIN_TOK = 64
EPS = 1e-06
BF = jnp.bfloat16
F32 = jnp.float32
LIMIT = 56 * 1024 * 1024


def position_table(window_ids, width):
    token_ids = jnp.arange(WIN_TOK, dtype=jnp.int32)
    row_pos = window_ids[:, None] // WIN_COLS * WIN_SIDE + token_ids[None, :] // WIN_SIDE
    col_pos = window_ids[:, None] % WIN_COLS * WIN_SIDE + token_ids[None, :] % WIN_SIDE
    quarter = width // 4
    frequency = jnp.exp(jnp.arange(quarter, dtype=F32) * (-math.log(10000.0) / quarter))
    row_angle = row_pos.astype(F32)[:, :, None] * frequency
    col_angle = col_pos.astype(F32)[:, :, None] * frequency
    return jnp.concatenate(
        [jnp.sin(row_angle), jnp.cos(row_angle), jnp.sin(col_angle), jnp.cos(col_angle)], axis=-1
    )


def head_norm(values):
    return (values * lax.rsqrt(jnp.mean(values * values, axis=-1, keepdims=True) + EPS)).astype(BF)


def window_layer(blocks_in, window_ids, window_lens, norm_gain, w_qkv, w_out):
    width = blocks_in.shape[-1]
    count = window_ids.shape[0]
    heads = width // HEAD_DIM
    stream = blocks_in.reshape(count, WIN_TOK, width).astype(F32) + position_table(window_ids, width)
    scale = lax.rsqrt(jnp.mean(stream * stream, axis=-1, keepdims=True) + EPS)
    normed = (stream * scale * norm_gain).astype(BF).reshape(count * WIN_TOK, width)
    full_rows = lax.all_gather(w_qkv, "group", axis=0, tiled=True)
    projected = jnp.dot(
        normed,
        lax.all_gather(full_rows, "tile", axis=1, tiled=True),
        preferred_element_type=F32,
    ).reshape(count, WIN_TOK, 3, heads, HEAD_DIM)
    queries = head_norm(projected[:, :, 0])
    keys = head_norm(projected[:, :, 1])
    values = projected[:, :, 2].astype(BF)
    scores = jnp.einsum("wqhd,wkhd->whqk", queries, keys, preferred_element_type=F32) * HEAD_DIM**-0.5
    key_mask = jnp.arange(WIN_TOK, dtype=jnp.int32)[None, :] < window_lens[:, None]
    weights = jnp.exp(scores) * key_mask[:, None, None, :].astype(F32)
    probs = (weights / jnp.sum(weights, axis=-1, keepdims=True)).astype(BF)
    attended = jnp.einsum("whqk,wkhd->wqhd", probs, values, preferred_element_type=F32)
    attended = attended.astype(BF).reshape(count * WIN_TOK, width)
    out_rows = lax.all_gather(w_out, "group", axis=0, tiled=True)
    update = jnp.dot(
        attended, lax.all_gather(out_rows, "tile", axis=1, tiled=True), preferred_element_type=F32
    )
    base = blocks_in.reshape(count * WIN_TOK, width).astype(F32)
    token_live = key_mask.reshape(count * WIN_TOK)[:, None]
    return jnp.where(token_live, base + update, base).astype(BF).reshape(blocks_in.shape)


def general(latents, window_index, window_len, live_blocks, norm_gain, w_qkv, w_out):
    slot_ids = jnp.arange(latents.shape[0], dtype=jnp.int32)
    live_mask = (slot_ids < live_blocks[0])[:, None, None]
    finished = window_layer(latents, window_index, window_len, norm_gain, w_qkv, w_out)
    return jnp.where(live_mask, finished, latents)


def anyspec():
    return pl.BlockSpec(memory_space=pl.ANY)


def vspec():
    return pl.BlockSpec(memory_space=pltpu.VMEM)


def sspec():
    return pl.BlockSpec(memory_space=pltpu.SMEM)


def params():
    return pltpu.CompilerParams(vmem_limit_bytes=LIMIT)


def cost(flops, moved):
    return pl.CostEstimate(flops=flops, bytes_accessed=moved, transcendentals=0)


def pack_kernel(wq_ref, wo_ref, unit_ref, a_ref, b_ref):
    half = wq_ref.shape[0] // 2
    nq = wq_ref.shape[1]
    for j, ref in enumerate((a_ref, b_ref)):
        wide = jnp.concatenate(
            [wq_ref[j * half : (j + 1) * half, :], wo_ref[j * half : (j + 1) * half, :]], axis=1
        )
        turned = wide.T
        ref[...] = turned
        unit_ref[j] = turned


def pack(w_qkv, w_out):
    depth, nq = w_qkv.shape
    both = nq + w_out.shape[1]
    return pl.pallas_call(
        pack_kernel,
        out_shape=(
            jax.ShapeDtypeStruct((2, both, depth // 2), BF),
            jax.ShapeDtypeStruct((both, depth // 2), BF),
            jax.ShapeDtypeStruct((both, depth // 2), BF),
        ),
        in_specs=[vspec()] * 2,
        out_specs=(vspec(),) * 3,
        compiler_params=params(),
        cost_estimate=cost(0, 4 * depth * both),
        name="pack_weights",
    )(w_qkv, w_out)


def norm_kernel(ids_ref, lat_ref, gain_ref, freq_ref, out_ref, pos_ref):
    blocks, _, width = lat_ref.shape
    quarter = width // 4
    freq = freq_ref[...]
    step = lax.broadcasted_iota(jnp.int32, (WIN_SIDE, quarter), 0).astype(F32) * freq
    sin_step, cos_step = jnp.sin(step), jnp.cos(step)
    gain = gain_ref[...]

    @pl.loop(0, blocks)
    def _(b):
        for w in range(2):
            place = ids_ref[2 * b + w]
            row = (place // WIN_COLS * WIN_SIDE).astype(F32)
            col = (place % WIN_COLS * WIN_SIDE).astype(F32)
            for at, start in ((0, row), (2 * quarter, col)):
                base = start * freq
                sin_base, cos_base = jnp.sin(base), jnp.cos(base)
                sines = sin_base * cos_step + cos_base * sin_step
                cosines = cos_base * cos_step - sin_base * sin_step
                for more, table in ((0, sines), (quarter, cosines)):
                    where = pl.ds(at + more, quarter)
                    for i in range(WIN_SIDE):
                        rows = pl.ds(w * WIN_TOK + i * WIN_SIDE, WIN_SIDE)
                        if at == 0:
                            pos_ref[rows, where] = jnp.broadcast_to(
                                table[i : i + 1, :], (WIN_SIDE, quarter)
                            )
                        else:
                            pos_ref[rows, where] = table
        stream = lat_ref[b].astype(F32) + pos_ref[...]
        scale = lax.rsqrt(jnp.mean(stream * stream, axis=-1, keepdims=True) + EPS)
        out_ref[b] = (stream * scale * gain).astype(BF).T


def normed_columns(latents, window_index, norm_gain):
    blocks, rows, width = latents.shape
    quarter = width // 4
    freq = jnp.exp(jnp.arange(quarter, dtype=F32) * (-math.log(10000.0) / quarter))
    return pl.pallas_call(
        norm_kernel,
        out_shape=jax.ShapeDtypeStruct((blocks, width, rows), BF),
        in_specs=[sspec(), vspec(), vspec(), vspec()],
        out_specs=vspec(),
        scratch_shapes=[pltpu.VMEM((rows, width), F32)],
        compiler_params=params(),
        cost_estimate=cost(40 * blocks * rows * width, 4 * blocks * rows * width),
        name="norm",
    )(window_index, latents, norm_gain.reshape(1, width), freq.reshape(1, quarter))


def pick_kernel(at_ref, near_b, near_c, far_d, far_e, qa, qb, oa, ob, sems):
    nq = qa.shape[1]
    no = oa.shape[1]

    def copies(second, third):
        out = []
        for s, src in ((0, second), (1, third)):
            for j, (q, o) in ((0, (qa, oa)), (1, (qb, ob))):
                out.append((src.at[j, pl.ds(0, nq)], q.at[s]))
                out.append((src.at[j, pl.ds(nq, no)], o.at[s]))
        return [pltpu.make_async_copy(x, y, sems.at[i]) for i, (x, y) in enumerate(out)]

    inner = at_ref[4] == 1

    @pl.when(inner)
    def _():
        for c in copies(near_b, near_c):
            c.start()
        for c in copies(near_b, near_c):
            c.wait()

    @pl.when(jnp.logical_not(inner))
    def _():
        for c in copies(far_d, far_e):
            c.start()
        for c in copies(far_d, far_e):
            c.wait()


def pick_far(place, b, c, d, e, nq):
    _, both, lanes = b.shape
    q = jax.ShapeDtypeStruct((2, nq, lanes), BF)
    o = jax.ShapeDtypeStruct((2, both - nq, lanes), BF)
    return pl.pallas_call(
        pick_kernel,
        out_shape=(q, q, o, o),
        in_specs=[sspec()] + [anyspec()] * 4,
        out_specs=(anyspec(),) * 4,
        scratch_shapes=[pltpu.SemaphoreType.DMA((8,))],
        compiler_params=params(),
        cost_estimate=cost(0, 8 * both * lanes * 2),
        name="pick_far",
    )(place, b, c, d, e)


def piece_copies(place, pieces, row0, rows, dst, sems):
    x, y, core = place
    lanes = dst.shape[2] // 4
    out = []
    for owner in range(2):
        c = core if owner == 0 else 1 - core
        aa, a2, bb, b2 = pieces[4 * owner : 4 * owner + 4]
        for i in range(2):
            xi = x if i == 0 else 1 - x
            yi = y if i == 0 else 1 - y
            for half, ref, px, py in (
                (0, aa, xi, y),
                (0, a2, xi, 1 - y),
                (1, bb, x, yi),
                (1, b2, 1 - x, yi),
            ):
                row = pl.multiple_of((2 * py + c) * rows, 16)
                lane = pl.multiple_of((2 * px + half) * lanes, 128)
                out.append(
                    pltpu.make_async_copy(
                        ref.at[i, :, pl.ds(row0, rows), :],
                        dst.at[:, pl.ds(row, rows), pl.ds(lane, lanes)],
                        sems.at[len(out)],
                    )
                )
    return out


def project_kernel(slots, nq, first_value, at_ref, planes_ref, n_ref, *rest):
    pieces, (out_ref, w_ref, sems) = rest[:8], rest[8:]
    copies = piece_copies((at_ref[0], at_ref[1], at_ref[2]), pieces, 0, nq, w_ref, sems)
    for c in copies:
        c.start()
    for c in copies:
        c.wait()
    plane_rows = w_ref.shape[1]
    blocks = n_ref.shape[0]
    chunk = plane_rows // 3
    heads = chunk // HEAD_DIM

    @pl.loop(0, slots * 3)
    def _(step):
        s = step // 3
        m = step % 3
        row = pl.multiple_of(m * chunk, 128)
        head0 = (planes_ref[s] * 3 + m) * heads
        w = w_ref[s, pl.ds(row, chunk), :]
        head = head0 + lax.broadcasted_iota(jnp.int32, (heads, 1, 1), 0)
        for b in range(0, blocks, 2):
            cols = jnp.concatenate([n_ref[b], n_ref[b + 1]], axis=1) if blocks > b + 1 else n_ref[b]
            got = jnp.dot(w, cols, preferred_element_type=F32)
            width = got.shape[1]
            got = got.reshape(heads, HEAD_DIM, width)
            ms = jnp.mean(got * got, axis=1, keepdims=True)
            scale = jnp.where(head < first_value, lax.rsqrt(ms + EPS), 1.0)
            out = (got * scale).astype(BF).reshape(chunk, width)
            out_ref[s, pl.ds(row, chunk), pl.ds(b * 128, width)] = out


def project(place, planes, normed, pieces, nq):
    blocks, width, rows = normed.shape
    slots = pieces[0].shape[1]
    plane_rows = 4 * nq
    return pl.pallas_call(
        functools.partial(project_kernel, slots, nq, 2 * width // HEAD_DIM),
        out_shape=jax.ShapeDtypeStruct((slots, plane_rows, blocks * rows), BF),
        in_specs=[sspec(), sspec(), vspec()] + [anyspec()] * 8,
        out_specs=vspec(),
        scratch_shapes=[
            pltpu.VMEM((slots, plane_rows, width), BF),
            pltpu.SemaphoreType.DMA((16,)),
        ],
        compiler_params=params(),
        cost_estimate=cost(
            2 * slots * plane_rows * width * blocks * rows,
            2 * (slots * plane_rows * width + 2 * blocks * rows * width),
        ),
        name="project",
    )(place, planes, normed, *pieces)


def attend_kernel(at_ref, planes_ref, lens_ref, p0, p1, p2, out_ref, t_ref, mask_ref, sems):
    plane_rows = p0.shape[1]
    copies = []
    for i, src in enumerate((p0.at[0], p1.at[0], p2.at[0], p2.at[1])):
        row = pl.multiple_of(planes_ref[i] * plane_rows, 128)
        copies.append(pltpu.make_async_copy(src, t_ref.at[pl.ds(row, plane_rows)], sems.at[i]))
    for c in copies:
        c.start()
    tokens, width = out_ref.shape
    blocks = tokens // 128
    key = lax.broadcasted_iota(jnp.int32, (128, 128), 0)
    query = lax.broadcasted_iota(jnp.int32, (128, 128), 1)
    for b in range(blocks):
        first = (key < WIN_TOK) & (query < WIN_TOK) & (key < lens_ref[2 * b])
        second = (key >= WIN_TOK) & (query >= WIN_TOK) & (key - WIN_TOK < lens_ref[2 * b + 1])
        mask_ref[b] = jnp.where(first | second, 1.0, 0.0).astype(F32)
    for c in copies:
        c.wait()
    ones = jnp.ones((16, 128), BF)

    @pl.loop(0, width // 128)
    def _(pair):
        for b in range(blocks):
            tok = pl.ds(b * 128, 128)
            done = []
            for i in range(2):
                row = pl.multiple_of(pair * 128, 128) + i * HEAD_DIM
                q = t_ref[pl.ds(row, HEAD_DIM), tok]
                k = t_ref[pl.ds(width + row, HEAD_DIM), tok]
                v = t_ref[pl.ds(2 * width + row, HEAD_DIM), tok]
                scores = lax.dot_general(k, q, (((0,), (0,)), ((), ())), preferred_element_type=F32)
                weights = (jnp.exp(scores * HEAD_DIM**-0.5) * mask_ref[b]).astype(BF)
                got = jnp.dot(jnp.concatenate([v, ones], axis=0), weights, preferred_element_type=F32)
                done.append(got[:HEAD_DIM] / got[HEAD_DIM : HEAD_DIM + 1])
            both = jnp.concatenate(done, axis=0)
            out_ref[tok, pl.ds(pl.multiple_of(pair * 128, 128), 128)] = both.T.astype(BF)


def attend(place, planes, window_len, parts, width):
    tokens = parts[0].shape[2]
    return pl.pallas_call(
        attend_kernel,
        out_shape=jax.ShapeDtypeStruct((tokens, width), BF),
        in_specs=[sspec()] * 3 + [anyspec()] * 3,
        out_specs=vspec(),
        scratch_shapes=[
            pltpu.VMEM((3 * width, tokens), BF),
            pltpu.VMEM((tokens // 128, 128, 128), F32),
            pltpu.SemaphoreType.DMA((4,)),
        ],
        compiler_params=params(),
        cost_estimate=cost(40 * 128 * tokens * width, 8 * tokens * width),
        name="attend",
    )(place, planes, window_len, *parts)


def output_kernel(row0, no, fresh, at_ref, planes_ref, lens_ref, live_ref, att_ref, lat_ref, *rest):
    pieces, rest = rest[:8], rest[8:]
    if not fresh:
        rest = rest[1:]
    out_ref, w_ref, base_ref, done_ref, sems, base_sems, out_sems = rest
    slots = w_ref.shape[0]
    cols = w_ref.shape[1]
    tokens = att_ref.shape[0]
    copies = piece_copies((at_ref[0], at_ref[1], at_ref[2]), pieces, row0, no, w_ref, sems)
    for c in copies:
        c.start()
    spots = [pl.ds(pl.multiple_of(planes_ref[s] * cols, 128), cols) for s in range(slots)]
    bases = [
        pltpu.make_async_copy(lat_ref.at[:, spots[s]], base_ref.at[s], base_sems.at[s])
        for s in range(slots)
    ]
    outs = [
        pltpu.make_async_copy(done_ref.at[s], out_ref.at[:, spots[s]], out_sems.at[s])
        for s in range(slots)
    ]
    for c in bases:
        c.start()
    for c in copies:
        c.wait()
    for c in bases:
        c.wait()
    for s in range(slots):

        @pl.loop(0, tokens // 128)
        def _(b):
            tok = pl.ds(pl.multiple_of(b * 128, 128), 128)
            update = lax.dot_general(
                att_ref[tok, :], w_ref[s], (((1,), (1,)), ((), ())), preferred_element_type=F32
            )
            base = base_ref[s, tok, :].astype(F32)
            row = lax.broadcasted_iota(jnp.int32, (128, 1), 0)
            alive = b < live_ref[0]
            first = jnp.where(alive, lens_ref[2 * b], 0)
            second = jnp.where(alive, lens_ref[2 * b + 1], 0) + WIN_TOK
            keep = (row < first) | ((row >= WIN_TOK) & (row < second))
            done_ref[s, tok, :] = jnp.where(keep, base + update, base).astype(BF)

        outs[s].start()
    for c in outs:
        c.wait()


def output(place, planes, lens, live, attended, latents, pieces, row0, no, before):
    tokens, width = attended.shape
    slots = pieces[0].shape[1]
    cols = 4 * no
    fresh = before is None
    return pl.pallas_call(
        functools.partial(output_kernel, row0, no, fresh),
        out_shape=jax.ShapeDtypeStruct((tokens, width), BF),
        in_specs=[sspec()] * 4 + [vspec()] + [anyspec()] * (9 if fresh else 10),
        out_specs=anyspec(),
        scratch_shapes=[
            pltpu.VMEM((slots, cols, width), BF),
            pltpu.VMEM((slots, tokens, cols), BF),
            pltpu.VMEM((slots, tokens, cols), BF),
            pltpu.SemaphoreType.DMA((16,)),
            pltpu.SemaphoreType.DMA((slots,)),
            pltpu.SemaphoreType.DMA((slots,)),
        ],
        input_output_aliases={} if fresh else {14: 0},
        compiler_params=params(),
        cost_estimate=cost(2 * slots * cols * width * tokens, 4 * slots * cols * (width + tokens)),
        name="output",
    )(place, planes, lens, live, attended, latents, *pieces, *(() if fresh else (before,)))


def neighbours(tile_count):
    inner_low, inner_high = range(4, 8), range(8, 12)
    return {
        "z": [(i, i ^ 4) for i in range(tile_count)],
        "mid": [(i, i + 4) for i in inner_low] + [(i, i - 4) for i in inner_high],
        "ends": [(i, i - 4) for i in inner_low] + [(i, i + 4) for i in inner_high],
        "y": [(i, i ^ 2) for i in range(tile_count)],
        "core": [(i, i ^ 1) for i in range(tile_count)],
    }


def spread(a, b, send):
    a1 = send["x"](a)
    b1 = send["y"](b)
    aa = jnp.stack([a, a1])
    bb = jnp.stack([b, b1])
    a2 = send["y"](aa)
    b2 = send["x"](bb)
    mine = [aa, a2, bb, b2]
    return mine + [send["core"](m) for m in mine]


def local(tile_count, latents, window_index, window_len, live_blocks, norm_gain, w_qkv, w_out):
    blocks, rows, width = latents.shape
    nq, no = w_qkv.shape[1], w_out.shape[1]
    send = {
        name: functools.partial(lax.ppermute, axis_name="tile", perm=pairs)
        for name, pairs in neighbours(tile_count).items()
    }
    send["x"] = functools.partial(lax.ppermute, axis_name="group", perm=[(0, 1), (1, 0)])
    t = lax.axis_index("tile")
    x = lax.axis_index("group")
    z = t // 4
    inner = ((z == 1) | (z == 2)).astype(jnp.int32)
    place = jnp.stack([x, t // 2 % 2, t % 2, z, inner]).astype(jnp.int32)
    second = jnp.where(inner == 1, 3 - z, z ^ 2)
    planes = jnp.stack([z, z ^ 1, second, second ^ 1]).astype(jnp.int32)

    unit, a, b = pack(w_qkv, w_out)
    swapped = send["z"](unit)
    near_b = send["mid"](unit)
    g0 = spread(a[None], b[None], send)
    normed = normed_columns(latents, window_index, norm_gain)
    near_c = send["mid"](swapped)
    far_d = send["ends"](near_b)
    g1 = spread(swapped[0][None], swapped[1][None], send)
    p0 = project(place, planes[0:1], normed, g0, nq)
    far_e = send["ends"](near_c)
    qa, qb, oa, ob = pick_far(place, near_b, near_c, far_d, far_e, nq)
    g2 = spread(qa, qb, send)
    p1 = project(place, planes[1:2], normed, g1, nq)
    go = spread(oa, ob, send)
    p2 = project(place, planes[2:4], normed, g2, nq)
    attended = attend(place, planes, window_len, (p0, p1, p2), width)
    flat = latents.reshape(blocks * rows, width)
    args = (window_len, live_blocks, attended, flat)
    out = output(place, planes[0:1], *args, g0, nq, no, None)
    out = output(place, planes[1:2], *args, g1, nq, no, out)
    out = output(place, planes[2:4], *args, go, 0, no, out)
    return out.reshape(latents.shape)


def solution(mesh):
    in_specs = (
        P(("tile", "group"), None, None),
        P(("tile", "group")),
        P(("tile", "group")),
        P(("tile", "group")),
        P(),
        P("group", "tile"),
        P("group", "tile"),
    )
    out_specs = P(("tile", "group"), None, None)
    planes, chips, cores = 4, 2, 2
    if mesh.shape["group"] == 2 and mesh.shape["tile"] == planes * chips * cores:
        body = functools.partial(local, mesh.shape["tile"])
    else:
        body = general
    return jax.shard_map(body, mesh=mesh, in_specs=in_specs, out_specs=out_specs, check_vma=False)
```

```python
import functools
import math

import jax
import jax.numpy as jnp
from jax import lax
from jax.experimental import pallas as pl
from jax.experimental.pallas import tpu as pltpu
from jax.sharding import PartitionSpec as P

HEAD_DIM = 64
WIN_SIDE = 8
WIN_COLS = 60
WIN_TOK = 64
EPS = 1e-06
BF = jnp.bfloat16
F32 = jnp.float32


def position_table(window_ids, width):
    token_ids = jnp.arange(WIN_TOK, dtype=jnp.int32)
    row_pos = window_ids[:, None] // WIN_COLS * WIN_SIDE + token_ids[None, :] // WIN_SIDE
    col_pos = window_ids[:, None] % WIN_COLS * WIN_SIDE + token_ids[None, :] % WIN_SIDE
    quarter = width // 4
    frequency = jnp.exp(jnp.arange(quarter, dtype=F32) * (-math.log(10000.0) / quarter))
    row_angle = row_pos.astype(F32)[:, :, None] * frequency
    col_angle = col_pos.astype(F32)[:, :, None] * frequency
    return jnp.concatenate(
        [jnp.sin(row_angle), jnp.cos(row_angle), jnp.sin(col_angle), jnp.cos(col_angle)], axis=-1
    )


def head_norm(values):
    return (values * lax.rsqrt(jnp.mean(values * values, axis=-1, keepdims=True) + EPS)).astype(BF)


def window_layer(blocks_in, window_ids, window_lens, norm_gain, w_qkv, w_out):
    width = blocks_in.shape[-1]
    count = window_ids.shape[0]
    heads = width // HEAD_DIM
    stream = blocks_in.reshape(count, WIN_TOK, width).astype(F32) + position_table(window_ids, width)
    scale = lax.rsqrt(jnp.mean(stream * stream, axis=-1, keepdims=True) + EPS)
    normed = (stream * scale * norm_gain).astype(BF).reshape(count * WIN_TOK, width)
    full_rows = lax.all_gather(w_qkv, "group", axis=0, tiled=True)
    projected = jnp.dot(
        normed,
        lax.all_gather(full_rows, "tile", axis=1, tiled=True),
        preferred_element_type=F32,
    ).reshape(count, WIN_TOK, 3, heads, HEAD_DIM)
    queries = head_norm(projected[:, :, 0])
    keys = head_norm(projected[:, :, 1])
    values = projected[:, :, 2].astype(BF)
    scores = jnp.einsum("wqhd,wkhd->whqk", queries, keys, preferred_element_type=F32) * HEAD_DIM**-0.5
    key_mask = jnp.arange(WIN_TOK, dtype=jnp.int32)[None, :] < window_lens[:, None]
    weights = jnp.exp(scores) * key_mask[:, None, None, :].astype(F32)
    probs = (weights / jnp.sum(weights, axis=-1, keepdims=True)).astype(BF)
    attended = jnp.einsum("whqk,wkhd->wqhd", probs, values, preferred_element_type=F32)
    attended = attended.astype(BF).reshape(count * WIN_TOK, width)
    out_rows = lax.all_gather(w_out, "group", axis=0, tiled=True)
    update = jnp.dot(
        attended, lax.all_gather(out_rows, "tile", axis=1, tiled=True), preferred_element_type=F32
    )
    base = blocks_in.reshape(count * WIN_TOK, width).astype(F32)
    token_live = key_mask.reshape(count * WIN_TOK)[:, None]
    return jnp.where(token_live, base + update, base).astype(BF).reshape(blocks_in.shape)


def general(latents, window_index, window_len, live_blocks, norm_gain, w_qkv, w_out):
    slot_ids = jnp.arange(latents.shape[0], dtype=jnp.int32)
    live_mask = (slot_ids < live_blocks[0])[:, None, None]
    finished = window_layer(latents, window_index, window_len, norm_gain, w_qkv, w_out)
    return jnp.where(live_mask, finished, latents)


def anyspec():
    return pl.BlockSpec(memory_space=pl.ANY)


def vspec():
    return pl.BlockSpec(memory_space=pltpu.VMEM)


def sspec():
    return pl.BlockSpec(memory_space=pltpu.SMEM)


def params(mib):
    return pltpu.CompilerParams(vmem_limit_bytes=mib * 1024 * 1024)


def cost(flops, moved):
    return pl.CostEstimate(flops=flops, bytes_accessed=moved, transcendentals=0)


def norm_kernel(ids_ref, lat_ref, gain_ref, freq_ref, out_ref, pos_ref):
    blocks, _, width = lat_ref.shape
    quarter = width // 4
    freq = freq_ref[...]
    step = lax.broadcasted_iota(jnp.int32, (WIN_SIDE, quarter), 0).astype(F32) * freq
    sin_step, cos_step = jnp.sin(step), jnp.cos(step)
    gain = gain_ref[...]

    @pl.loop(0, blocks)
    def _(b):
        for w in range(2):
            place = ids_ref[2 * b + w]
            row = (place // WIN_COLS * WIN_SIDE).astype(F32)
            col = (place % WIN_COLS * WIN_SIDE).astype(F32)
            for at, start in ((0, row), (2 * quarter, col)):
                base = start * freq
                sin_base, cos_base = jnp.sin(base), jnp.cos(base)
                sines = sin_base * cos_step + cos_base * sin_step
                cosines = cos_base * cos_step - sin_base * sin_step
                for more, table in ((0, sines), (quarter, cosines)):
                    where = pl.ds(at + more, quarter)
                    for i in range(WIN_SIDE):
                        rows = pl.ds(w * WIN_TOK + i * WIN_SIDE, WIN_SIDE)
                        if at == 0:
                            pos_ref[rows, where] = jnp.broadcast_to(
                                table[i : i + 1, :], (WIN_SIDE, quarter)
                            )
                        else:
                            pos_ref[rows, where] = table
        stream = lat_ref[b].astype(F32) + pos_ref[...]
        scale = lax.rsqrt(jnp.mean(stream * stream, axis=-1, keepdims=True) + EPS)
        normed = (stream * scale * gain).astype(BF)
        out_ref[:, pl.ds(pl.multiple_of(b * 128, 128), 128)] = normed.T


def normed_columns(latents, window_index, norm_gain):
    blocks, rows, width = latents.shape
    quarter = width // 4
    freq = jnp.exp(jnp.arange(quarter, dtype=F32) * (-math.log(10000.0) / quarter))
    return pl.pallas_call(
        norm_kernel,
        out_shape=jax.ShapeDtypeStruct((width, blocks * rows), BF),
        in_specs=[sspec(), vspec(), vspec(), vspec()],
        out_specs=vspec(),
        scratch_shapes=[pltpu.VMEM((rows, width), F32)],
        compiler_params=params(24),
        cost_estimate=cost(40 * blocks * rows * width, 4 * blocks * rows * width),
        name="norm",
    )(window_index, latents, norm_gain.reshape(1, width), freq.reshape(1, quarter))


def project_kernel(key_chunk, value_chunk, at_ref, plane_ref, n_ref, *rest):
    pieces, (p_ref, k_ref, w_ref, sems) = rest[:8], rest[8:]
    x, y, core = at_ref[0], at_ref[1], at_ref[2]
    rows, lanes = pieces[0].shape
    copies = []
    for owner in range(2):
        c = core if owner == 0 else 1 - core
        for i, (px, py) in enumerate(((x, y), (1 - x, y), (x, 1 - y), (1 - x, 1 - y))):
            row = pl.multiple_of((2 * py + c) * rows, 16)
            lane = pl.multiple_of(px * lanes, 128)
            copies.append(
                pltpu.make_async_copy(
                    pieces[4 * owner + i],
                    w_ref.at[pl.ds(row, rows), pl.ds(lane, lanes)],
                    sems.at[len(copies)],
                )
            )
    for c in copies:
        c.start()
    for c in copies:
        c.wait()
    count, chunk, tokens = p_ref.shape
    cols = n_ref[...]

    @pl.loop(0, count)
    def _(m):
        which = plane_ref[0] * count + m
        w = w_ref[pl.ds(pl.multiple_of(m * chunk, 128), chunk), :]
        got = jnp.dot(w, cols, preferred_element_type=F32)
        got = got.reshape(chunk // HEAD_DIM, HEAD_DIM, tokens)
        ms = jnp.mean(got * got, axis=1, keepdims=True)
        scale = jnp.where(which < value_chunk, lax.rsqrt(ms + EPS), 1.0)
        out = (got * scale).astype(BF).reshape(chunk, tokens)
        is_key = (which >= key_chunk) & (which < value_chunk)

        @pl.when(is_key)
        def _():
            k_ref[m] = out.T

        @pl.when(jnp.logical_not(is_key))
        def _():
            p_ref[m] = out


def project(place, plane, normed, pieces):
    width, tokens = normed.shape
    rows = 4 * pieces[0].shape[0]
    chunk = width // 4
    count = rows // chunk
    return pl.pallas_call(
        functools.partial(project_kernel, 4, 8),
        out_shape=(
            jax.ShapeDtypeStruct((count, chunk, tokens), BF),
            jax.ShapeDtypeStruct((count, tokens, chunk), BF),
        ),
        in_specs=[sspec(), sspec(), vspec()] + [anyspec()] * 8,
        out_specs=(vspec(), vspec()),
        scratch_shapes=[pltpu.VMEM((rows, width), BF), pltpu.SemaphoreType.DMA((8,))],
        compiler_params=params(24),
        cost_estimate=cost(2 * rows * width * tokens, 2 * (rows + tokens) * width),
        name="project",
    )(place, plane, normed, *pieces)


def attend_kernel(
    planes_ref, lens_ref, p0, k0, p1, k1, p2, k2, p3, k3, out_ref, q_ref, k_ref, v_ref, mask_ref, sems
):
    count, chunk, tokens = p0.shape
    for s, (p, k) in enumerate(((p0, k0), (p1, k1), (p2, k2), (p3, k3))):
        for m in range(count):
            which = planes_ref[s] * count + m
            sem = sems.at[s * count + m]

            @pl.when(which < 4)
            def _():
                pltpu.make_async_copy(p.at[m], q_ref.at[jnp.minimum(which, 3)], sem).start()

            @pl.when((which >= 4) & (which < 8))
            def _():
                to = k_ref.at[jnp.clip(which - 4, 0, 3)]
                pltpu.make_async_copy(k.at[m], to, sem).start()

            @pl.when(which >= 8)
            def _():
                to = v_ref.at[jnp.clip(which - 8, 0, 3)]
                pltpu.make_async_copy(p.at[m], to, sem).start()

    blocks = tokens // 128
    key = lax.broadcasted_iota(jnp.int32, (128, 256), 0)
    query = lax.broadcasted_iota(jnp.int32, (128, 256), 1) % 128
    for b in range(blocks):
        first = (key < WIN_TOK) & (query < WIN_TOK) & (key < lens_ref[2 * b])
        second = (key >= WIN_TOK) & (query >= WIN_TOK) & (key - WIN_TOK < lens_ref[2 * b + 1])
        mask_ref[b] = jnp.where(first | second, 1.0, 0.0).astype(F32)
    for i in range(4 * count):
        pltpu.make_async_copy(p0.at[0], q_ref.at[0], sems.at[i]).wait()
    ones = jnp.ones((16, 128), BF)
    blank = jnp.zeros((HEAD_DIM, 128), BF)
    pairs = chunk // 128

    @pl.loop(0, 4 * pairs)
    def _(pair):
        part = pair // pairs
        at = pl.ds(pl.multiple_of(pair % pairs * 128, 128), 128)
        out_at = pl.ds(pl.multiple_of(pair * 128, 128), 128)
        for b in range(blocks):
            tok = pl.ds(b * 128, 128)
            q = q_ref[part, at, tok]
            k = k_ref[part, tok, at]
            v = v_ref[part, at, tok]
            q0 = jnp.concatenate([q[:HEAD_DIM], blank], axis=0)
            q1 = jnp.concatenate([blank, q[HEAD_DIM:]], axis=0)
            scores = jnp.dot(k, jnp.concatenate([q0, q1], axis=1), preferred_element_type=F32)
            weights = (jnp.exp(scores * HEAD_DIM**-0.5) * mask_ref[b]).astype(BF)
            got = jnp.dot(jnp.concatenate([v, ones], axis=0), weights, preferred_element_type=F32)
            o0 = got[:HEAD_DIM, :128] / got[128:129, :128]
            o1 = got[HEAD_DIM:128, 128:] / got[128:129, 128:]
            out_ref[tok, out_at] = jnp.concatenate([o0, o1], axis=0).T.astype(BF)


def attend(planes, window_len, parts):
    count, chunk, tokens = parts[0][0].shape
    width = 4 * chunk
    return pl.pallas_call(
        attend_kernel,
        out_shape=jax.ShapeDtypeStruct((tokens, width), BF),
        in_specs=[sspec()] * 2 + [anyspec()] * 8,
        out_specs=vspec(),
        scratch_shapes=[
            pltpu.VMEM((4, chunk, tokens), BF),
            pltpu.VMEM((4, tokens, chunk), BF),
            pltpu.VMEM((4, chunk, tokens), BF),
            pltpu.VMEM((tokens // 128, 128, 256), F32),
            pltpu.SemaphoreType.DMA((4 * count,)),
        ],
        compiler_params=params(24),
        cost_estimate=cost(40 * 128 * tokens * width, 8 * tokens * width),
        name="attend",
    )(planes, window_len, *[a for pair in parts for a in pair])


def output_kernel(at_ref, planes_ref, lens_ref, live_ref, att_ref, lat_ref, *rest):
    pieces, (out_ref, w_ref, sems) = rest[:10], rest[10:]
    x, y, core = at_ref[0], at_ref[1], at_ref[2]
    slots, rows, lanes = pieces[0].shape
    copies = []
    for owner in range(2):
        c = core if owner == 0 else 1 - core
        own, xs, ys, da, db = pieces[5 * owner : 5 * owner + 5]
        for s in range(slots):
            diagonal = da.at[s] if s < slots // 2 else db.at[s - slots // 2]
            for ref, px, py in (
                (own.at[s], x, y),
                (xs.at[s], 1 - x, y),
                (ys.at[s], x, 1 - y),
                (diagonal, 1 - x, 1 - y),
            ):
                row = pl.multiple_of((planes_ref[s] * 4 + 2 * py + c) * rows, 16)
                lane = pl.multiple_of(px * lanes, 128)
                copies.append(
                    pltpu.make_async_copy(
                        ref, w_ref.at[pl.ds(row, rows), pl.ds(lane, lanes)], sems.at[len(copies)]
                    )
                )
    for c in copies:
        c.start()
    for c in copies:
        c.wait()
    tokens, width = att_ref.shape
    cols = 4 * rows
    att = att_ref[...]
    token = lax.broadcasted_iota(jnp.int32, (tokens, 1), 0)
    stop = jnp.zeros((tokens, 1), jnp.int32)
    for w in range(tokens // WIN_TOK):
        length = jnp.where(w // 2 < live_ref[0], lens_ref[w], 0)
        stop = jnp.where(token // WIN_TOK == w, length + w * WIN_TOK, stop)
    keep = token < stop

    @pl.loop(0, slots)
    def _(s):
        spot = pl.ds(pl.multiple_of(s * cols, 128), cols)
        update = lax.dot_general(
            att, w_ref[spot, :], (((1,), (1,)), ((), ())), preferred_element_type=F32
        )
        base = lat_ref[:, spot].astype(F32)
        out_ref[:, spot] = jnp.where(keep, base + update, base).astype(BF)


def output(place, planes, lens, live, attended, latents, pieces):
    tokens, width = attended.shape
    return pl.pallas_call(
        output_kernel,
        out_shape=jax.ShapeDtypeStruct((tokens, width), BF),
        in_specs=[sspec()] * 4 + [vspec()] * 2 + [anyspec()] * 10,
        out_specs=vspec(),
        scratch_shapes=[pltpu.VMEM((width, width), BF), pltpu.SemaphoreType.DMA((32,))],
        compiler_params=params(32),
        cost_estimate=cost(2 * width * width * tokens, 2 * width * (width + 3 * tokens)),
        name="output",
    )(place, planes, lens, live, attended, latents, *pieces)


def after(value, *earlier):
    return lax.optimization_barrier((value, *earlier))[0]


def local(tile_count, latents, window_index, window_len, live_blocks, norm_gain, w_qkv, w_out):
    blocks, rows, width = latents.shape

    def along(bit):
        pairs = [(i, i ^ bit) for i in range(tile_count)]
        return functools.partial(lax.ppermute, axis_name="tile", perm=pairs)

    core, ys, z1, z2, z3 = along(1), along(2), along(4), along(8), along(12)
    xs = functools.partial(lax.ppermute, axis_name="group", perm=[(0, 1), (1, 0)])
    t = lax.axis_index("tile")
    x = lax.axis_index("group")
    z = t // 4
    place = jnp.stack([x, t // 2 % 2, t % 2]).astype(jnp.int32)
    planes = jnp.stack([z, z ^ 1, z ^ 2, z ^ 3]).astype(jnp.int32)

    u0 = w_qkv.T
    o0 = w_out.T
    u1, x0, y0 = z1(u0), xs(u0), ys(u0)
    u2 = z2(u0)
    normed = normed_columns(latents, window_index, norm_gain)
    y0, normed = lax.optimization_barrier((y0, normed))
    d0 = xs(y0)
    y1 = ys(u1)
    u3 = z3(after(u0, u2, y0))
    x2, y2 = xs(after(u2, d0)), ys(u2)
    d1 = z1(d0)
    s0 = [u0, x0, y0, d0]
    p0 = project(place, planes[0:1], normed, s0 + [core(a) for a in s0])
    d2 = ys(after(x2, p0[0]))
    x1 = xs(after(u1, x2))
    s1 = [u1, x1, y1, d1]
    p1 = project(place, planes[1:2], normed, s1 + [core(a) for a in s1])
    y3, x3 = ys(after(u3, d2)), xs(after(u3, x1))
    d3 = z1(d2)
    o1, o2, o3 = (f(after(o0, u3)) for f in (z1, z2, z3))
    s2 = [u2, x2, y2, d2]
    p2 = project(place, planes[2:3], normed, s2 + [core(a) for a in s2])
    o4 = after(jnp.stack([o0, o1, o2, o3]), p1[0])
    xo, yo = xs(o4), ys(o4)
    s3 = [u3, x3, y3, d3]
    p3 = project(place, planes[3:4], normed, s3 + [core(a) for a in s3])
    half = o4.shape[0] // 2
    da, db = xs(after(yo[:half], p3[0])), ys(xo[half:])
    so = [o4, xo, yo, da, db]
    so = so + [core(a) for a in so]
    attended = attend(planes, window_len, (p0, p1, p2, p3))
    flat = latents.reshape(blocks * rows, width)
    out = output(place, planes, window_len, live_blocks, attended, flat, so)
    return out.reshape(latents.shape)


def solution(mesh):
    in_specs = (
        P(("tile", "group"), None, None),
        P(("tile", "group")),
        P(("tile", "group")),
        P(("tile", "group")),
        P(),
        P("group", "tile"),
        P("group", "tile"),
    )
    out_specs = P(("tile", "group"), None, None)
    planes, chips, cores = 4, 2, 2
    if mesh.shape["group"] == 2 and mesh.shape["tile"] == planes * chips * cores:
        body = functools.partial(local, mesh.shape["tile"])
    else:
        body = general
    return jax.shard_map(body, mesh=mesh, in_specs=in_specs, out_specs=out_specs, check_vma=False)
```

```python
import functools
import math

import jax
import jax.numpy as jnp
from jax import lax
from jax.experimental import pallas as pl
from jax.experimental.pallas import tpu as pltpu
from jax.sharding import PartitionSpec as P

HEAD_DIM = 64
WIN_SIDE = 8
WIN_COLS = 60
WIN_TOK = 64
EPS = 1e-06
BF = jnp.bfloat16
F32 = jnp.float32


def position_table(window_ids, width):
    token_ids = jnp.arange(WIN_TOK, dtype=jnp.int32)
    row_pos = window_ids[:, None] // WIN_COLS * WIN_SIDE + token_ids[None, :] // WIN_SIDE
    col_pos = window_ids[:, None] % WIN_COLS * WIN_SIDE + token_ids[None, :] % WIN_SIDE
    quarter = width // 4
    frequency = jnp.exp(jnp.arange(quarter, dtype=F32) * (-math.log(10000.0) / quarter))
    row_angle = row_pos.astype(F32)[:, :, None] * frequency
    col_angle = col_pos.astype(F32)[:, :, None] * frequency
    return jnp.concatenate(
        [jnp.sin(row_angle), jnp.cos(row_angle), jnp.sin(col_angle), jnp.cos(col_angle)], axis=-1
    )


def head_norm(values):
    return (values * lax.rsqrt(jnp.mean(values * values, axis=-1, keepdims=True) + EPS)).astype(BF)


def window_layer(blocks_in, window_ids, window_lens, norm_gain, w_qkv, w_out):
    width = blocks_in.shape[-1]
    count = window_ids.shape[0]
    heads = width // HEAD_DIM
    stream = blocks_in.reshape(count, WIN_TOK, width).astype(F32) + position_table(window_ids, width)
    scale = lax.rsqrt(jnp.mean(stream * stream, axis=-1, keepdims=True) + EPS)
    normed = (stream * scale * norm_gain).astype(BF).reshape(count * WIN_TOK, width)
    full_rows = lax.all_gather(w_qkv, "group", axis=0, tiled=True)
    projected = jnp.dot(
        normed,
        lax.all_gather(full_rows, "tile", axis=1, tiled=True),
        preferred_element_type=F32,
    ).reshape(count, WIN_TOK, 3, heads, HEAD_DIM)
    queries = head_norm(projected[:, :, 0])
    keys = head_norm(projected[:, :, 1])
    values = projected[:, :, 2].astype(BF)
    scores = jnp.einsum("wqhd,wkhd->whqk", queries, keys, preferred_element_type=F32) * HEAD_DIM**-0.5
    key_mask = jnp.arange(WIN_TOK, dtype=jnp.int32)[None, :] < window_lens[:, None]
    weights = jnp.exp(scores) * key_mask[:, None, None, :].astype(F32)
    probs = (weights / jnp.sum(weights, axis=-1, keepdims=True)).astype(BF)
    attended = jnp.einsum("whqk,wkhd->wqhd", probs, values, preferred_element_type=F32)
    attended = attended.astype(BF).reshape(count * WIN_TOK, width)
    out_rows = lax.all_gather(w_out, "group", axis=0, tiled=True)
    update = jnp.dot(
        attended, lax.all_gather(out_rows, "tile", axis=1, tiled=True), preferred_element_type=F32
    )
    base = blocks_in.reshape(count * WIN_TOK, width).astype(F32)
    token_live = key_mask.reshape(count * WIN_TOK)[:, None]
    return jnp.where(token_live, base + update, base).astype(BF).reshape(blocks_in.shape)


def general(latents, window_index, window_len, live_blocks, norm_gain, w_qkv, w_out):
    slot_ids = jnp.arange(latents.shape[0], dtype=jnp.int32)
    live_mask = (slot_ids < live_blocks[0])[:, None, None]
    finished = window_layer(latents, window_index, window_len, norm_gain, w_qkv, w_out)
    return jnp.where(live_mask, finished, latents)


def hspec():
    return pl.BlockSpec(memory_space=pltpu.HBM)


def vspec():
    return pl.BlockSpec(memory_space=pltpu.VMEM)


def sspec():
    return pl.BlockSpec(memory_space=pltpu.SMEM)


def params(mib):
    return pltpu.CompilerParams(vmem_limit_bytes=mib * 1024 * 1024)


def far(value):
    return pltpu.with_memory_space_constraint(value, pltpu.HBM)


def cost(flops, moved):
    return pl.CostEstimate(flops=flops, bytes_accessed=moved, transcendentals=0)


def norm_kernel(ids_ref, lat_ref, gain_ref, freq_ref, out_ref, pos_ref):
    blocks, _, width = lat_ref.shape
    quarter = width // 4
    freq = freq_ref[...]
    step = lax.broadcasted_iota(jnp.int32, (WIN_SIDE, quarter), 0).astype(F32) * freq
    sin_step, cos_step = jnp.sin(step), jnp.cos(step)
    gain = gain_ref[...]

    @pl.loop(0, blocks)
    def _(b):
        for w in range(2):
            place = ids_ref[2 * b + w]
            row = (place // WIN_COLS * WIN_SIDE).astype(F32)
            col = (place % WIN_COLS * WIN_SIDE).astype(F32)
            for at, start in ((0, row), (2 * quarter, col)):
                base = start * freq
                sin_base, cos_base = jnp.sin(base), jnp.cos(base)
                sines = sin_base * cos_step + cos_base * sin_step
                cosines = cos_base * cos_step - sin_base * sin_step
                for more, table in ((0, sines), (quarter, cosines)):
                    where = pl.ds(at + more, quarter)
                    for i in range(WIN_SIDE):
                        rows = pl.ds(w * WIN_TOK + i * WIN_SIDE, WIN_SIDE)
                        if at == 0:
                            pos_ref[rows, where] = jnp.broadcast_to(
                                table[i : i + 1, :], (WIN_SIDE, quarter)
                            )
                        else:
                            pos_ref[rows, where] = table
        stream = lat_ref[b].astype(F32) + pos_ref[...]
        scale = lax.rsqrt(jnp.mean(stream * stream, axis=-1, keepdims=True) + EPS)
        normed = (stream * scale * gain).astype(BF)
        out_ref[:, pl.ds(pl.multiple_of(b * 128, 128), 128)] = normed.T


def normed_columns(latents, window_index, norm_gain):
    blocks, rows, width = latents.shape
    quarter = width // 4
    freq = jnp.exp(jnp.arange(quarter, dtype=F32) * (-math.log(10000.0) / quarter))
    return pl.pallas_call(
        norm_kernel,
        out_shape=jax.ShapeDtypeStruct((width, blocks * rows), BF),
        in_specs=[sspec(), vspec(), vspec(), vspec()],
        out_specs=vspec(),
        scratch_shapes=[pltpu.VMEM((rows, width), F32)],
        compiler_params=params(24),
        cost_estimate=cost(40 * blocks * rows * width, 4 * blocks * rows * width),
        name="norm",
    )(window_index, latents, norm_gain.reshape(1, width), freq.reshape(1, quarter))


def project_kernel(key_chunk, value_chunk, at_ref, plane_ref, n_ref, *rest):
    pieces, (p_ref, k_ref, w_ref, sems) = rest[:8], rest[8:]
    x, y, core = at_ref[0], at_ref[1], at_ref[2]
    rows, lanes = pieces[0].shape
    copies = []
    for owner in range(2):
        c = core if owner == 0 else 1 - core
        for i, (px, py) in enumerate(((x, y), (1 - x, y), (x, 1 - y), (1 - x, 1 - y))):
            row = pl.multiple_of((2 * py + c) * rows, 16)
            lane = pl.multiple_of(px * lanes, 128)
            copies.append(
                pltpu.make_async_copy(
                    pieces[4 * owner + i],
                    w_ref.at[pl.ds(row, rows), pl.ds(lane, lanes)],
                    sems.at[len(copies)],
                )
            )
    for c in copies:
        c.start()
    for c in copies:
        c.wait()
    count, chunk, tokens = p_ref.shape
    cols = n_ref[...]

    @pl.loop(0, count)
    def _(m):
        which = plane_ref[0] * count + m
        w = w_ref[pl.ds(pl.multiple_of(m * chunk, 128), chunk), :]
        got = jnp.dot(w, cols, preferred_element_type=F32)
        got = got.reshape(chunk // HEAD_DIM, HEAD_DIM, tokens)
        ms = jnp.mean(got * got, axis=1, keepdims=True)
        scale = jnp.where(which < value_chunk, lax.rsqrt(ms + EPS), 1.0)
        out = (got * scale).astype(BF).reshape(chunk, tokens)
        is_key = (which >= key_chunk) & (which < value_chunk)

        @pl.when(is_key)
        def _():
            k_ref[m] = out.T

        @pl.when(jnp.logical_not(is_key))
        def _():
            p_ref[m] = out


def project(place, plane, normed, pieces):
    width, tokens = normed.shape
    rows = 4 * pieces[0].shape[0]
    chunk = width // 4
    count = rows // chunk
    return pl.pallas_call(
        functools.partial(project_kernel, 4, 8),
        out_shape=(
            jax.ShapeDtypeStruct((count, chunk, tokens), BF),
            jax.ShapeDtypeStruct((count, tokens, chunk), BF),
        ),
        in_specs=[sspec(), sspec(), vspec()] + [hspec()] * 8,
        out_specs=(vspec(), vspec()),
        scratch_shapes=[pltpu.VMEM((rows, width), BF), pltpu.SemaphoreType.DMA((8,))],
        compiler_params=params(24),
        cost_estimate=cost(2 * rows * width * tokens, 2 * (rows + tokens) * width),
        name="project",
    )(place, plane, normed, *map(far, pieces))


def attend_kernel(
    planes_ref, lens_ref, p0, k0, p1, k1, p2, k2, p3, k3, out_ref, q_ref, k_ref, v_ref, mask_ref, sems
):
    count, chunk, tokens = p0.shape
    for s, (p, k) in enumerate(((p0, k0), (p1, k1), (p2, k2), (p3, k3))):
        for m in range(count):
            which = planes_ref[s] * count + m
            sem = sems.at[s * count + m]

            @pl.when(which < 4)
            def _():
                pltpu.make_async_copy(p.at[m], q_ref.at[jnp.minimum(which, 3)], sem).start()

            @pl.when((which >= 4) & (which < 8))
            def _():
                to = k_ref.at[jnp.clip(which - 4, 0, 3)]
                pltpu.make_async_copy(k.at[m], to, sem).start()

            @pl.when(which >= 8)
            def _():
                to = v_ref.at[jnp.clip(which - 8, 0, 3)]
                pltpu.make_async_copy(p.at[m], to, sem).start()

    blocks = tokens // 128
    key = lax.broadcasted_iota(jnp.int32, (128, 256), 0)
    query = lax.broadcasted_iota(jnp.int32, (128, 256), 1) % 128
    for b in range(blocks):
        first = (key < WIN_TOK) & (query < WIN_TOK) & (key < lens_ref[2 * b])
        second = (key >= WIN_TOK) & (query >= WIN_TOK) & (key - WIN_TOK < lens_ref[2 * b + 1])
        mask_ref[b] = jnp.where(first | second, 1.0, 0.0).astype(F32)
    for i in range(4 * count):
        pltpu.make_async_copy(p0.at[0], q_ref.at[0], sems.at[i]).wait()
    ones = jnp.ones((16, 128), BF)
    blank = jnp.zeros((HEAD_DIM, 128), BF)
    pairs = chunk // 128

    @pl.loop(0, 4 * pairs)
    def _(pair):
        part = pair // pairs
        at = pl.ds(pl.multiple_of(pair % pairs * 128, 128), 128)
        out_at = pl.ds(pl.multiple_of(pair * 128, 128), 128)
        for b in range(blocks):
            tok = pl.ds(b * 128, 128)
            q = q_ref[part, at, tok]
            k = k_ref[part, tok, at]
            v = v_ref[part, at, tok]
            q0 = jnp.concatenate([q[:HEAD_DIM], blank], axis=0)
            q1 = jnp.concatenate([blank, q[HEAD_DIM:]], axis=0)
            scores = jnp.dot(k, jnp.concatenate([q0, q1], axis=1), preferred_element_type=F32)
            weights = (jnp.exp(scores * HEAD_DIM**-0.5) * mask_ref[b]).astype(BF)
            got = jnp.dot(jnp.concatenate([v, ones], axis=0), weights, preferred_element_type=F32)
            o0 = got[:HEAD_DIM, :128] / got[128:129, :128]
            o1 = got[HEAD_DIM:128, 128:] / got[128:129, 128:]
            out_ref[tok, out_at] = jnp.concatenate([o0, o1], axis=0).T.astype(BF)


def attend(planes, window_len, parts):
    count, chunk, tokens = parts[0][0].shape
    width = 4 * chunk
    return pl.pallas_call(
        attend_kernel,
        out_shape=jax.ShapeDtypeStruct((tokens, width), BF),
        in_specs=[sspec()] * 2 + [hspec()] * 8,
        out_specs=vspec(),
        scratch_shapes=[
            pltpu.VMEM((4, chunk, tokens), BF),
            pltpu.VMEM((4, tokens, chunk), BF),
            pltpu.VMEM((4, chunk, tokens), BF),
            pltpu.VMEM((tokens // 128, 128, 256), F32),
            pltpu.SemaphoreType.DMA((4 * count,)),
        ],
        compiler_params=params(24),
        cost_estimate=cost(40 * 128 * tokens * width, 8 * tokens * width),
        name="attend",
    )(planes, window_len, *[far(a) for pair in parts for a in pair])


def output_kernel(at_ref, planes_ref, lens_ref, live_ref, att_ref, lat_ref, *rest):
    pieces, (out_ref, w_ref, sems) = rest[:10], rest[10:]
    x, y, core = at_ref[0], at_ref[1], at_ref[2]
    slots, rows, lanes = pieces[0].shape
    copies = []
    for owner in range(2):
        c = core if owner == 0 else 1 - core
        own, xs, ys, da, db = pieces[5 * owner : 5 * owner + 5]
        for s in range(slots):
            diagonal = da.at[s] if s < slots // 2 else db.at[s - slots // 2]
            for ref, px, py in (
                (own.at[s], x, y),
                (xs.at[s], 1 - x, y),
                (ys.at[s], x, 1 - y),
                (diagonal, 1 - x, 1 - y),
            ):
                row = pl.multiple_of((planes_ref[s] * 4 + 2 * py + c) * rows, 16)
                lane = pl.multiple_of(px * lanes, 128)
                copies.append(
                    pltpu.make_async_copy(
                        ref, w_ref.at[pl.ds(row, rows), pl.ds(lane, lanes)], sems.at[len(copies)]
                    )
                )
    for c in copies:
        c.start()
    for c in copies:
        c.wait()
    tokens, width = att_ref.shape
    cols = 4 * rows
    att = att_ref[...]
    token = lax.broadcasted_iota(jnp.int32, (tokens, 1), 0)
    stop = jnp.zeros((tokens, 1), jnp.int32)
    for w in range(tokens // WIN_TOK):
        length = jnp.where(w // 2 < live_ref[0], lens_ref[w], 0)
        stop = jnp.where(token // WIN_TOK == w, length + w * WIN_TOK, stop)
    keep = token < stop

    @pl.loop(0, slots)
    def _(s):
        spot = pl.ds(pl.multiple_of(s * cols, 128), cols)
        update = lax.dot_general(
            att, w_ref[spot, :], (((1,), (1,)), ((), ())), preferred_element_type=F32
        )
        base = lat_ref[:, spot].astype(F32)
        out_ref[:, spot] = jnp.where(keep, base + update, base).astype(BF)


def output(place, planes, lens, live, attended, latents, pieces):
    tokens, width = attended.shape
    return pl.pallas_call(
        output_kernel,
        out_shape=jax.ShapeDtypeStruct((tokens, width), BF),
        in_specs=[sspec()] * 4 + [vspec()] * 2 + [hspec()] * 10,
        out_specs=vspec(),
        scratch_shapes=[pltpu.VMEM((width, width), BF), pltpu.SemaphoreType.DMA((32,))],
        compiler_params=params(32),
        cost_estimate=cost(2 * width * width * tokens, 2 * width * (width + 3 * tokens)),
        name="output",
    )(place, planes, lens, live, attended, latents, *map(far, pieces))


def after(value, *earlier):
    return lax.optimization_barrier((value, *earlier))[0]


def local(tile_count, latents, window_index, window_len, live_blocks, norm_gain, w_qkv, w_out):
    blocks, rows, width = latents.shape

    def along(bit):
        pairs = [(i, i ^ bit) for i in range(tile_count)]
        return functools.partial(lax.ppermute, axis_name="tile", perm=pairs)

    core, ys, z1, z2, z3 = along(1), along(2), along(4), along(8), along(12)
    xs = functools.partial(lax.ppermute, axis_name="group", perm=[(0, 1), (1, 0)])
    t = lax.axis_index("tile")
    x = lax.axis_index("group")
    z = t // 4
    place = jnp.stack([x, t // 2 % 2, t % 2]).astype(jnp.int32)
    planes = jnp.stack([z, z ^ 1, z ^ 2, z ^ 3]).astype(jnp.int32)

    u0 = w_qkv.T
    o0 = w_out.T
    u1, x0, y0, u2 = z1(u0), xs(u0), ys(u0), z2(u0)
    o1, o2 = z1(after(o0, x0)), z2(after(o0, x0))
    normed = normed_columns(latents, window_index, norm_gain)
    d0 = xs(after(y0, normed))
    y1 = ys(u1)
    x2, y2, u3 = xs(u2), ys(u2), z1(u2)
    x1 = xs(after(u1, d0))
    d1 = z1(d0)
    o3 = z1(after(o2, d0))
    s0 = [u0, x0, y0, d0]
    p0 = project(place, planes[0:1], normed, s0 + [core(a) for a in s0])
    d2 = ys(after(x2, p0[0]))
    x3, y3 = xs(u3), ys(u3)
    o4 = jnp.stack([after(o0, u3), o1, o2, o3])
    xo, yo = xs(o4), ys(o4)
    s1 = [u1, x1, y1, d1]
    p1 = project(place, planes[1:2], normed, s1 + [core(a) for a in s1])
    d3 = z1(d2)
    s2 = [u2, x2, y2, d2]
    p2 = project(place, planes[2:3], normed, s2 + [core(a) for a in s2])
    s3 = [u3, after(x3, p1[0]), after(y3, p2[0]), d3]
    p3 = project(place, planes[3:4], normed, s3 + [core(a) for a in s3])
    half = o4.shape[0] // 2
    da, db = xs(yo[:half]), ys(xo[half:])
    so = [o4, xo, yo, da, db]
    so = so + [core(a) for a in so]
    attended = attend(planes, after(window_len, xo, yo), (p0, p1, p2, p3))
    flat = latents.reshape(blocks * rows, width)
    out = output(place, planes, window_len, live_blocks, attended, flat, so)
    return out.reshape(latents.shape)


def solution(mesh):
    in_specs = (
        P(("tile", "group"), None, None),
        P(("tile", "group")),
        P(("tile", "group")),
        P(("tile", "group")),
        P(),
        P("group", "tile"),
        P("group", "tile"),
    )
    out_specs = P(("tile", "group"), None, None)
    planes, chips, cores = 4, 2, 2
    if mesh.shape["group"] == 2 and mesh.shape["tile"] == planes * chips * cores:
        body = functools.partial(local, mesh.shape["tile"])
    else:
        body = general
    return jax.shard_map(body, mesh=mesh, in_specs=in_specs, out_specs=out_specs, check_vma=False)
```

```python
import functools
import math

import jax
import jax.numpy as jnp
from jax import lax
from jax.experimental import pallas as pl
from jax.experimental.pallas import tpu as pltpu
from jax.sharding import PartitionSpec as P

HEAD_DIM = 64
WIN_SIDE = 8
WIN_COLS = 60
WIN_TOK = 64
EPS = 1e-06
BF = jnp.bfloat16
F32 = jnp.float32


def position_table(window_ids, width):
    token_ids = jnp.arange(WIN_TOK, dtype=jnp.int32)
    row_pos = window_ids[:, None] // WIN_COLS * WIN_SIDE + token_ids[None, :] // WIN_SIDE
    col_pos = window_ids[:, None] % WIN_COLS * WIN_SIDE + token_ids[None, :] % WIN_SIDE
    quarter = width // 4
    frequency = jnp.exp(jnp.arange(quarter, dtype=F32) * (-math.log(10000.0) / quarter))
    row_angle = row_pos.astype(F32)[:, :, None] * frequency
    col_angle = col_pos.astype(F32)[:, :, None] * frequency
    return jnp.concatenate(
        [jnp.sin(row_angle), jnp.cos(row_angle), jnp.sin(col_angle), jnp.cos(col_angle)], axis=-1
    )


def head_norm(values):
    return (values * lax.rsqrt(jnp.mean(values * values, axis=-1, keepdims=True) + EPS)).astype(BF)


def window_layer(blocks_in, window_ids, window_lens, norm_gain, w_qkv, w_out):
    width = blocks_in.shape[-1]
    count = window_ids.shape[0]
    heads = width // HEAD_DIM
    stream = blocks_in.reshape(count, WIN_TOK, width).astype(F32) + position_table(window_ids, width)
    scale = lax.rsqrt(jnp.mean(stream * stream, axis=-1, keepdims=True) + EPS)
    normed = (stream * scale * norm_gain).astype(BF).reshape(count * WIN_TOK, width)
    full_rows = lax.all_gather(w_qkv, "group", axis=0, tiled=True)
    projected = jnp.dot(
        normed,
        lax.all_gather(full_rows, "tile", axis=1, tiled=True),
        preferred_element_type=F32,
    ).reshape(count, WIN_TOK, 3, heads, HEAD_DIM)
    queries = head_norm(projected[:, :, 0])
    keys = head_norm(projected[:, :, 1])
    values = projected[:, :, 2].astype(BF)
    scores = jnp.einsum("wqhd,wkhd->whqk", queries, keys, preferred_element_type=F32) * HEAD_DIM**-0.5
    key_mask = jnp.arange(WIN_TOK, dtype=jnp.int32)[None, :] < window_lens[:, None]
    weights = jnp.exp(scores) * key_mask[:, None, None, :].astype(F32)
    probs = (weights / jnp.sum(weights, axis=-1, keepdims=True)).astype(BF)
    attended = jnp.einsum("whqk,wkhd->wqhd", probs, values, preferred_element_type=F32)
    attended = attended.astype(BF).reshape(count * WIN_TOK, width)
    out_rows = lax.all_gather(w_out, "group", axis=0, tiled=True)
    update = jnp.dot(
        attended, lax.all_gather(out_rows, "tile", axis=1, tiled=True), preferred_element_type=F32
    )
    base = blocks_in.reshape(count * WIN_TOK, width).astype(F32)
    token_live = key_mask.reshape(count * WIN_TOK)[:, None]
    return jnp.where(token_live, base + update, base).astype(BF).reshape(blocks_in.shape)


def general(latents, window_index, window_len, live_blocks, norm_gain, w_qkv, w_out):
    slot_ids = jnp.arange(latents.shape[0], dtype=jnp.int32)
    live_mask = (slot_ids < live_blocks[0])[:, None, None]
    finished = window_layer(latents, window_index, window_len, norm_gain, w_qkv, w_out)
    return jnp.where(live_mask, finished, latents)


def hspec():
    return pl.BlockSpec(memory_space=pltpu.HBM)


def vspec():
    return pl.BlockSpec(memory_space=pltpu.VMEM)


def sspec():
    return pl.BlockSpec(memory_space=pltpu.SMEM)


def params(mib):
    return pltpu.CompilerParams(vmem_limit_bytes=mib * 1024 * 1024)


def far(value):
    return pltpu.with_memory_space_constraint(value, pltpu.HBM)


def cost(flops, moved):
    return pl.CostEstimate(flops=flops, bytes_accessed=moved, transcendentals=0)


def norm_kernel(ids_ref, lat_ref, gain_ref, freq_ref, out_ref, pos_ref):
    blocks, _, width = lat_ref.shape
    quarter = width // 4
    freq = freq_ref[...]
    step = lax.broadcasted_iota(jnp.int32, (WIN_SIDE, quarter), 0).astype(F32) * freq
    sin_step, cos_step = jnp.sin(step), jnp.cos(step)
    gain = gain_ref[...]

    @pl.loop(0, blocks)
    def _(b):
        for w in range(2):
            place = ids_ref[2 * b + w]
            row = (place // WIN_COLS * WIN_SIDE).astype(F32)
            col = (place % WIN_COLS * WIN_SIDE).astype(F32)
            for at, start in ((0, row), (2 * quarter, col)):
                base = start * freq
                sin_base, cos_base = jnp.sin(base), jnp.cos(base)
                sines = sin_base * cos_step + cos_base * sin_step
                cosines = cos_base * cos_step - sin_base * sin_step
                for more, table in ((0, sines), (quarter, cosines)):
                    where = pl.ds(at + more, quarter)
                    for i in range(WIN_SIDE):
                        rows = pl.ds(w * WIN_TOK + i * WIN_SIDE, WIN_SIDE)
                        if at == 0:
                            pos_ref[rows, where] = jnp.broadcast_to(
                                table[i : i + 1, :], (WIN_SIDE, quarter)
                            )
                        else:
                            pos_ref[rows, where] = table
        stream = lat_ref[b].astype(F32) + pos_ref[...]
        scale = lax.rsqrt(jnp.mean(stream * stream, axis=-1, keepdims=True) + EPS)
        normed = (stream * scale * gain).astype(BF)
        out_ref[:, pl.ds(pl.multiple_of(b * 128, 128), 128)] = normed.T


def normed_columns(latents, window_index, norm_gain):
    blocks, rows, width = latents.shape
    quarter = width // 4
    freq = jnp.exp(jnp.arange(quarter, dtype=F32) * (-math.log(10000.0) / quarter))
    return pl.pallas_call(
        norm_kernel,
        out_shape=jax.ShapeDtypeStruct((width, blocks * rows), BF),
        in_specs=[sspec(), vspec(), vspec(), vspec()],
        out_specs=vspec(),
        scratch_shapes=[pltpu.VMEM((rows, width), F32)],
        compiler_params=params(24),
        cost_estimate=cost(40 * blocks * rows * width, 4 * blocks * rows * width),
        name="norm",
    )(window_index, latents, norm_gain.reshape(1, width), freq.reshape(1, quarter))


def places(x, y):
    return ((x, y), (1 - x, y), (x, 1 - y), (1 - x, 1 - y))


def project_kernel(key_chunk, value_chunk, at_ref, plane_ref, n_ref, *rest):
    pieces, (p_ref, k_ref, w_ref, rows_ref, cols_ref, sems, out_sems) = rest[:8], rest[8:]
    x, y, core = at_ref[0], at_ref[1], at_ref[2]
    rows, lanes = w_ref.shape[0] // 4, w_ref.shape[1] // 2
    for i, (px, py) in enumerate(places(x, y)):
        for owner, c in ((0, core), (1, 1 - core)):
            row = pl.multiple_of((2 * py + c) * rows, 16)
            lane = pl.multiple_of(px * lanes, 128)
            pltpu.make_async_copy(
                pieces[4 * owner + i].at[pl.ds(0, rows), :],
                w_ref.at[pl.ds(row, rows), pl.ds(lane, lanes)],
                sems.at[py * 4 + 2 * owner + i % 2],
            ).start()
    count, chunk, tokens = p_ref.shape

    def landed(which):
        for i in range(4):
            pltpu.make_async_copy(
                pieces[0].at[pl.ds(0, rows), :],
                w_ref.at[pl.ds(0, rows), pl.ds(0, lanes)],
                sems.at[4 * which + i],
            ).wait()

    for m in range(count):
        if m < 2:
            landed(m)
        which = plane_ref[0] * count + m
        got = jnp.dot(w_ref[m * chunk : (m + 1) * chunk, :], n_ref[...], preferred_element_type=F32)
        got = got.reshape(chunk // HEAD_DIM, HEAD_DIM, tokens)
        ms = jnp.mean(got * got, axis=1, keepdims=True)
        scale = jnp.where(which < value_chunk, lax.rsqrt(ms + EPS), 1.0)
        scale = jnp.where(which < key_chunk, scale * HEAD_DIM**-0.5, scale)
        out = (got * scale).astype(BF).reshape(chunk, tokens)
        rows_ref[m] = out
        cols_ref[m] = out.T
        is_key = (which >= key_chunk) & (which < value_chunk)

        @pl.when(is_key)
        def _():
            pltpu.make_async_copy(cols_ref.at[m], k_ref.at[m], out_sems.at[m]).start()

        @pl.when(jnp.logical_not(is_key))
        def _():
            pltpu.make_async_copy(rows_ref.at[m], p_ref.at[m], out_sems.at[m]).start()

    for m in range(count):
        pltpu.make_async_copy(rows_ref.at[m], p_ref.at[m], out_sems.at[m]).wait()


def project(place, plane, normed, pieces, rows):
    width, tokens = normed.shape
    chunk = width // 4
    count = 4 * rows // chunk
    return pl.pallas_call(
        functools.partial(project_kernel, 4, 8),
        out_shape=(
            pltpu.HBM((count, chunk, tokens), BF),
            pltpu.HBM((count, tokens, chunk), BF),
        ),
        in_specs=[sspec(), sspec(), vspec()] + [hspec()] * 8,
        out_specs=(hspec(), hspec()),
        scratch_shapes=[
            pltpu.VMEM((4 * rows, width), BF),
            pltpu.VMEM((count, chunk, tokens), BF),
            pltpu.VMEM((count, tokens, chunk), BF),
            pltpu.SemaphoreType.DMA((8,)),
            pltpu.SemaphoreType.DMA((count,)),
        ],
        compiler_params=params(24),
        cost_estimate=cost(8 * rows * width * tokens, 2 * (4 * rows + tokens) * width),
        name="project",
    )(place, plane, normed, *map(far, pieces))


def attend_kernel(
    planes_ref, lens_ref, p0, k0, p1, k1, p2, k2, p3, k3, out_ref, q_ref, k_ref, v_ref, mask_ref, sems
):
    count, chunk, tokens = p0.shape
    for s, (p, k) in enumerate(((p0, k0), (p1, k1), (p2, k2), (p3, k3))):
        for m in range(count):
            which = planes_ref[s] * count + m
            sem = sems.at[which]

            @pl.when(which < 4)
            def _():
                pltpu.make_async_copy(p.at[m], q_ref.at[jnp.minimum(which, 3)], sem).start()

            @pl.when((which >= 4) & (which < 8))
            def _():
                to = k_ref.at[jnp.clip(which - 4, 0, 3)]
                pltpu.make_async_copy(k.at[m], to, sem).start()

            @pl.when(which >= 8)
            def _():
                to = v_ref.at[jnp.clip(which - 8, 0, 3)]
                pltpu.make_async_copy(p.at[m], to, sem).start()

    blocks = tokens // 128
    key = lax.broadcasted_iota(jnp.int32, (128, 256), 0)
    query = lax.broadcasted_iota(jnp.int32, (128, 256), 1) % 128
    for b in range(blocks):
        first = (key < WIN_TOK) & (query < WIN_TOK) & (key < lens_ref[2 * b])
        second = (key >= WIN_TOK) & (query >= WIN_TOK) & (key - WIN_TOK < lens_ref[2 * b + 1])
        mask_ref[b] = jnp.where(first | second, 1.0, 0.0).astype(F32)
    ones = jnp.ones((16, 128), BF)
    blank = jnp.zeros((HEAD_DIM, 128), BF)
    pairs = chunk // 128

    @pl.loop(0, 4)
    def _(part):
        for kind in range(3):
            pltpu.make_async_copy(p0.at[0], q_ref.at[0], sems.at[4 * kind + part]).wait()

        @pl.loop(0, pairs)
        def _(i):
            at = pl.ds(pl.multiple_of(i * 128, 128), 128)
            out_at = pl.ds(pl.multiple_of(part * chunk + i * 128, 128), 128)
            for b in range(blocks):
                tok = pl.ds(b * 128, 128)
                q = q_ref[part, at, tok]
                k = k_ref[part, tok, at]
                v = v_ref[part, at, tok]
                q0 = jnp.concatenate([q[:HEAD_DIM], blank], axis=0)
                q1 = jnp.concatenate([blank, q[HEAD_DIM:]], axis=0)
                scores = jnp.dot(k, jnp.concatenate([q0, q1], axis=1), preferred_element_type=F32)
                weights = (jnp.exp(scores) * mask_ref[b]).astype(BF)
                got = jnp.dot(
                    jnp.concatenate([v, ones], axis=0), weights, preferred_element_type=F32
                )
                share = 1.0 / got[128:129, :]
                o0 = got[:HEAD_DIM, :128] * share[:, :128]
                o1 = got[HEAD_DIM:128, 128:] * share[:, 128:]
                out_ref[tok, out_at] = jnp.concatenate([o0, o1], axis=0).astype(BF).T


def attend(planes, window_len, parts):
    count, chunk, tokens = parts[0][0].shape
    width = 4 * chunk
    return pl.pallas_call(
        attend_kernel,
        out_shape=jax.ShapeDtypeStruct((tokens, width), BF),
        in_specs=[sspec()] * 2 + [hspec()] * 8,
        out_specs=vspec(),
        scratch_shapes=[
            pltpu.VMEM((4, chunk, tokens), BF),
            pltpu.VMEM((4, tokens, chunk), BF),
            pltpu.VMEM((4, chunk, tokens), BF),
            pltpu.VMEM((tokens // 128, 128, 256), F32),
            pltpu.SemaphoreType.DMA((4 * count,)),
        ],
        compiler_params=params(24),
        cost_estimate=cost(40 * 128 * tokens * width, 8 * tokens * width),
        name="attend",
    )(planes, window_len, *[far(a) for pair in parts for a in pair])


def output_kernel(at_ref, planes_ref, lens_ref, live_ref, att_ref, lat_ref, *rest):
    pieces, (out_ref, w_ref, done_ref, sems, out_sems) = rest[:-5], rest[-5:]
    x, y, core = at_ref[0], at_ref[1], at_ref[2]
    slots = len(pieces) // 8
    tokens, width = att_ref.shape
    rows, lanes = width // (4 * slots), width // 2
    skip = pieces[0].shape[0] - rows
    copies = []
    for s in range(slots):
        for owner, c in ((0, core), (1, 1 - core)):
            for i, (px, py) in enumerate(places(x, y)):
                src = pieces[8 * s + 4 * owner + i].at[pl.ds(skip, rows), :]
                row = pl.multiple_of((2 * py + c) * rows, 16)
                lane = pl.multiple_of(px * lanes, 128)
                copies.append(
                    pltpu.make_async_copy(
                        src, w_ref.at[s, pl.ds(row, rows), pl.ds(lane, lanes)], sems.at[len(copies)]
                    )
                )
    for c in copies:
        c.start()
    cols = 4 * rows
    token = lax.broadcasted_iota(jnp.int32, (tokens, 1), 0)
    stop = jnp.zeros((tokens, 1), jnp.int32)
    for w in range(tokens // WIN_TOK):
        length = jnp.where(w // 2 < live_ref[0], lens_ref[w], 0)
        stop = jnp.where(token // WIN_TOK == w, length + w * WIN_TOK, stop)
    keep = token < stop
    outs = []
    for s in range(slots):
        for c in copies[8 * s : 8 * s + 8]:
            c.wait()
        spot = pl.ds(pl.multiple_of(planes_ref[s] * cols, 128), cols)
        update = lax.dot_general(
            att_ref[...], w_ref[s], (((1,), (1,)), ((), ())), preferred_element_type=F32
        )
        base = lat_ref[:, spot].astype(F32)
        done_ref[s] = jnp.where(keep, base + update, base).astype(BF)
        outs.append(pltpu.make_async_copy(done_ref.at[s], out_ref.at[:, spot], out_sems.at[s]))
        outs[s].start()
    for c in outs:
        c.wait()


def output(place, planes, lens, live, attended, latents, pieces):
    tokens, width = attended.shape
    return pl.pallas_call(
        output_kernel,
        out_shape=jax.ShapeDtypeStruct((tokens, width), BF),
        in_specs=[sspec()] * 4 + [vspec()] * 2 + [hspec()] * len(pieces),
        out_specs=hspec(),
        scratch_shapes=[
            pltpu.VMEM((4, width // 4, width), BF),
            pltpu.VMEM((4, tokens, width // 4), BF),
            pltpu.SemaphoreType.DMA((len(pieces),)),
            pltpu.SemaphoreType.DMA((4,)),
        ],
        compiler_params=params(32),
        cost_estimate=cost(2 * width * width * tokens, 2 * width * (width + 3 * tokens)),
        name="output",
    )(place, planes, lens, live, attended, latents, *map(far, pieces))


def local(tile_count, latents, window_index, window_len, live_blocks, norm_gain, w_qkv, w_out):
    blocks, rows, width = latents.shape

    def along(axis, pairs):
        def move(value, name):
            with jax.named_scope(name):
                return lax.ppermute(value, axis, pairs)

        return move

    def across(bit):
        return along("tile", [(i, i ^ bit) for i in range(tile_count)])

    core, ys, z1 = across(1), across(2), across(4)
    xs = along("group", [(0, 1), (1, 0)])
    low, high = range(tile_count // 4, tile_count // 2), range(tile_count // 2, 3 * tile_count // 4)
    step = tile_count // 4
    mid = along("tile", [(i, i + step) for i in low] + [(i, i - step) for i in high])
    ends = along("tile", [(i, i - step) for i in low] + [(i, i + step) for i in high])
    t = lax.axis_index("tile")
    x = lax.axis_index("group")
    z = t // 4
    place = jnp.stack([x, t // 2 % 2, t % 2]).astype(jnp.int32)
    planes = jnp.stack([z, z ^ 1, z ^ 2, z ^ 3]).astype(jnp.int32)

    nq = w_qkv.shape[1]

    def sync(*values):
        return lax.optimization_barrier(values)

    def share(**values):
        shared = []
        for name, value in values.items():
            if shared:
                value = sync(value, shared[-1])[0]
            shared.append(core(value, f"core_{name}"))
        return shared

    u0 = jnp.concatenate([w_qkv.T, w_out.T], axis=0)
    u1, near, x0, y0 = z1(u0, "u1"), mid(u0, "near2"), xs(u0, "x0"), ys(u0, "y0")
    normed = normed_columns(latents, window_index, norm_gain)
    cu0, = share(u0=u0)
    u1, near, x0, y0, normed, cu0 = sync(u1, near, x0, y0, normed, cu0)
    far2, near3, d0, y1 = ends(near, "far2"), mid(u1, "near3"), xs(y0, "d0"), ys(u1, "y1")
    cx0, cy0 = share(x0=x0, y0=y0)
    far2, near3, d0, y1, cx0, cy0, near, u1 = sync(far2, near3, d0, y1, cx0, cy0, near, u1)
    u2 = near3 + far2
    x2, y2, far3 = xs(u2, "x2"), ys(u2, "y2"), ends(near3, "far3")
    cd0, cy1, cu1 = share(d0=d0, y1=y1, u1=u1)
    x2, y2, far3, cd0, cy1, cu1, u1, u2, d0, near = sync(x2, y2, far3, cd0, cy1, cu1, u1, u2, d0, near)
    x1, d2, d1 = xs(u1, "x1"), ys(x2, "d2"), z1(d0, "d1")
    u3 = near + far3
    s0 = [u0, x0, y0, d0, cu0, cx0, cy0, cd0]
    p0 = project(place, planes[0:1], normed, s0, nq)
    cu2, cx2, cy2 = share(u2=u2, x2=x2, y2=y2)
    x1, d2, d1, u3, cu2, cx2, cy2, *p0 = sync(x1, d2, d1, u3, cu2, cx2, cy2, *p0)
    x3, y3, d3 = xs(u3, "x3"), ys(u3, "y3"), z1(d2, "d3")
    cx1, cd1, cd2, cu3 = share(x1=x1, d1=d1, d2=d2, u3=u3)
    s1 = [u1, x1, y1, d1, cu1, cx1, cy1, cd1]
    p1 = project(place, planes[1:2], normed, s1, nq)
    s2 = [u2, x2, y2, d2, cu2, cx2, cy2, cd2]
    p2 = project(place, planes[2:3], normed, s2, nq)
    x3, y3, d3, cu3, p1, p2 = sync(x3, y3, d3, cu3, p1, p2)
    cx3, cy3, cd3 = (share(**{name: value})[0] for name, value in (("x3", x3), ("y3", y3), ("d3", d3)))
    s3 = [u3, x3, y3, d3, cu3, cx3, cy3, cd3]
    p3 = project(place, planes[3:4], normed, s3, nq)
    attended = attend(planes, window_len, (p0, p1, p2, p3))
    so = s0 + s1 + s2 + s3
    flat = latents.reshape(blocks * rows, width)
    out = output(place, planes, window_len, live_blocks, attended, flat, so)
    return out.reshape(latents.shape)


def solution(mesh):
    in_specs = (
        P(("tile", "group"), None, None),
        P(("tile", "group")),
        P(("tile", "group")),
        P(("tile", "group")),
        P(),
        P("group", "tile"),
        P("group", "tile"),
    )
    out_specs = P(("tile", "group"), None, None)
    planes, chips, cores = 4, 2, 2
    if mesh.shape["group"] == 2 and mesh.shape["tile"] == planes * chips * cores:
        body = functools.partial(local, mesh.shape["tile"])
    else:
        body = general
    return jax.shard_map(body, mesh=mesh, in_specs=in_specs, out_specs=out_specs, check_vma=False)
```

```python
import functools
import math

import jax
import jax.numpy as jnp
from jax import lax
from jax.experimental import pallas as pl
from jax.experimental.pallas import tpu as pltpu
from jax.sharding import PartitionSpec as P

HEAD_DIM = 64
WIN_SIDE = 8
WIN_COLS = 60
WIN_TOK = 64
EPS = 1e-06
BF = jnp.bfloat16
F32 = jnp.float32


def position_table(window_ids, width):
    token_ids = jnp.arange(WIN_TOK, dtype=jnp.int32)
    row_pos = window_ids[:, None] // WIN_COLS * WIN_SIDE + token_ids[None, :] // WIN_SIDE
    col_pos = window_ids[:, None] % WIN_COLS * WIN_SIDE + token_ids[None, :] % WIN_SIDE
    quarter = width // 4
    frequency = jnp.exp(jnp.arange(quarter, dtype=F32) * (-math.log(10000.0) / quarter))
    row_angle = row_pos.astype(F32)[:, :, None] * frequency
    col_angle = col_pos.astype(F32)[:, :, None] * frequency
    return jnp.concatenate(
        [jnp.sin(row_angle), jnp.cos(row_angle), jnp.sin(col_angle), jnp.cos(col_angle)], axis=-1
    )


def head_norm(values):
    return (values * lax.rsqrt(jnp.mean(values * values, axis=-1, keepdims=True) + EPS)).astype(BF)


def window_layer(blocks_in, window_ids, window_lens, norm_gain, w_qkv, w_out):
    width = blocks_in.shape[-1]
    count = window_ids.shape[0]
    heads = width // HEAD_DIM
    stream = blocks_in.reshape(count, WIN_TOK, width).astype(F32) + position_table(window_ids, width)
    scale = lax.rsqrt(jnp.mean(stream * stream, axis=-1, keepdims=True) + EPS)
    normed = (stream * scale * norm_gain).astype(BF).reshape(count * WIN_TOK, width)
    full_rows = lax.all_gather(w_qkv, "group", axis=0, tiled=True)
    projected = jnp.dot(
        normed,
        lax.all_gather(full_rows, "tile", axis=1, tiled=True),
        preferred_element_type=F32,
    ).reshape(count, WIN_TOK, 3, heads, HEAD_DIM)
    queries = head_norm(projected[:, :, 0])
    keys = head_norm(projected[:, :, 1])
    values = projected[:, :, 2].astype(BF)
    scores = jnp.einsum("wqhd,wkhd->whqk", queries, keys, preferred_element_type=F32) * HEAD_DIM**-0.5
    key_mask = jnp.arange(WIN_TOK, dtype=jnp.int32)[None, :] < window_lens[:, None]
    weights = jnp.exp(scores) * key_mask[:, None, None, :].astype(F32)
    probs = (weights / jnp.sum(weights, axis=-1, keepdims=True)).astype(BF)
    attended = jnp.einsum("whqk,wkhd->wqhd", probs, values, preferred_element_type=F32)
    attended = attended.astype(BF).reshape(count * WIN_TOK, width)
    out_rows = lax.all_gather(w_out, "group", axis=0, tiled=True)
    update = jnp.dot(
        attended, lax.all_gather(out_rows, "tile", axis=1, tiled=True), preferred_element_type=F32
    )
    base = blocks_in.reshape(count * WIN_TOK, width).astype(F32)
    token_live = key_mask.reshape(count * WIN_TOK)[:, None]
    return jnp.where(token_live, base + update, base).astype(BF).reshape(blocks_in.shape)


def general(latents, window_index, window_len, live_blocks, norm_gain, w_qkv, w_out):
    slot_ids = jnp.arange(latents.shape[0], dtype=jnp.int32)
    live_mask = (slot_ids < live_blocks[0])[:, None, None]
    finished = window_layer(latents, window_index, window_len, norm_gain, w_qkv, w_out)
    return jnp.where(live_mask, finished, latents)


def hspec():
    return pl.BlockSpec(memory_space=pltpu.HBM)


def vspec():
    return pl.BlockSpec(memory_space=pltpu.VMEM)


def sspec():
    return pl.BlockSpec(memory_space=pltpu.SMEM)


def params(mib):
    return pltpu.CompilerParams(vmem_limit_bytes=mib * 1024 * 1024)


def far(value):
    return pltpu.with_memory_space_constraint(value, pltpu.HBM)


def cost(flops, moved):
    return pl.CostEstimate(flops=flops, bytes_accessed=moved, transcendentals=0)


def norm_kernel(ids_ref, lat_ref, gain_ref, freq_ref, out_ref, pos_ref):
    blocks, _, width = lat_ref.shape
    quarter = width // 4
    freq = freq_ref[...]
    step = lax.broadcasted_iota(jnp.int32, (WIN_SIDE, quarter), 0).astype(F32) * freq
    sin_step, cos_step = jnp.sin(step), jnp.cos(step)
    gain = gain_ref[...]

    @pl.loop(0, blocks)
    def _(b):
        for w in range(2):
            place = ids_ref[2 * b + w]
            row = (place // WIN_COLS * WIN_SIDE).astype(F32)
            col = (place % WIN_COLS * WIN_SIDE).astype(F32)
            for at, start in ((0, row), (2 * quarter, col)):
                base = start * freq
                sin_base, cos_base = jnp.sin(base), jnp.cos(base)
                sines = sin_base * cos_step + cos_base * sin_step
                cosines = cos_base * cos_step - sin_base * sin_step
                for more, table in ((0, sines), (quarter, cosines)):
                    where = pl.ds(at + more, quarter)
                    for i in range(WIN_SIDE):
                        rows = pl.ds(w * WIN_TOK + i * WIN_SIDE, WIN_SIDE)
                        if at == 0:
                            pos_ref[rows, where] = jnp.broadcast_to(
                                table[i : i + 1, :], (WIN_SIDE, quarter)
                            )
                        else:
                            pos_ref[rows, where] = table
        stream = lat_ref[b].astype(F32) + pos_ref[...]
        scale = lax.rsqrt(jnp.mean(stream * stream, axis=-1, keepdims=True) + EPS)
        normed = (stream * scale * gain).astype(BF)
        out_ref[:, pl.ds(pl.multiple_of(b * 128, 128), 128)] = normed.T


def normed_columns(latents, window_index, norm_gain):
    blocks, rows, width = latents.shape
    quarter = width // 4
    freq = jnp.exp(jnp.arange(quarter, dtype=F32) * (-math.log(10000.0) / quarter))
    return pl.pallas_call(
        norm_kernel,
        out_shape=jax.ShapeDtypeStruct((width, blocks * rows), BF),
        in_specs=[sspec(), vspec(), vspec(), vspec()],
        out_specs=vspec(),
        scratch_shapes=[pltpu.VMEM((rows, width), F32)],
        compiler_params=params(24),
        cost_estimate=cost(40 * blocks * rows * width, 4 * blocks * rows * width),
        name="norm",
    )(window_index, latents, norm_gain.reshape(1, width), freq.reshape(1, quarter))


def places(x, y):
    return ((x, y), (1 - x, y), (x, 1 - y), (1 - x, 1 - y))


def piece_rows(ref, spot, start, rows):
    part = pl.ds(start, rows)
    return ref.at[part, :] if spot is None else ref.at[spot, part, :]


def start_columns(at_ref, pieces, spots, rows, w_ref, sems):
    x, y, core = at_ref[0], at_ref[1], at_ref[2]
    lanes = w_ref.shape[1] // 2
    for i, (px, py) in enumerate(places(x, y)):
        for owner, c in ((0, core), (1, 1 - core)):
            row = pl.multiple_of((2 * py + c) * rows, 16)
            lane = pl.multiple_of(px * lanes, 128)
            pltpu.make_async_copy(
                piece_rows(pieces[4 * owner + i], spots[4 * owner + i], 0, rows),
                w_ref.at[pl.ds(row, rows), pl.ds(lane, lanes)],
                sems.at[py * 4 + 2 * owner + i % 2],
            ).start()


def wait_columns(half, pieces, spots, rows, w_ref, sems):
    lanes = w_ref.shape[1] // 2
    for i in range(4):
        pltpu.make_async_copy(
            piece_rows(pieces[0], spots[0], 0, rows),
            w_ref.at[pl.ds(0, rows), pl.ds(0, lanes)],
            sems.at[4 * half + i],
        ).wait()


def project_chunk(m, which, parts, w_ref, n_ref):
    tokens = n_ref.shape[1]
    chunk = n_ref.shape[0] // parts
    got = jnp.dot(w_ref[m * chunk : (m + 1) * chunk, :], n_ref[...], preferred_element_type=F32)
    got = got.reshape(chunk // HEAD_DIM, HEAD_DIM, tokens)
    ms = jnp.mean(got * got, axis=1, keepdims=True)
    scale = jnp.where(which < 2 * parts, lax.rsqrt(ms + EPS), 1.0)
    scale = jnp.where(which < parts, scale * HEAD_DIM**-0.5, scale)
    return (got * scale).astype(BF).reshape(chunk, tokens)


def project_kernel(spots, parts, at_ref, plane_ref, n_ref, *rest):
    pieces, (p_ref, k_ref, w_ref, rows_ref, cols_ref, sems, out_sems) = rest[:8], rest[8:]
    rows = w_ref.shape[0] // 4
    start_columns(at_ref, pieces, spots, rows, w_ref, sems)
    count = p_ref.shape[0]
    for m in range(count):
        if m < 2:
            wait_columns(m, pieces, spots, rows, w_ref, sems)
        which = plane_ref[0] * count + m
        out = project_chunk(m, which, parts, w_ref, n_ref)
        rows_ref[m] = out
        cols_ref[m] = out.T
        is_key = (which >= parts) & (which < 2 * parts)

        @pl.when(is_key)
        def _():
            pltpu.make_async_copy(cols_ref.at[m], k_ref.at[m], out_sems.at[m]).start()

        @pl.when(jnp.logical_not(is_key))
        def _():
            pltpu.make_async_copy(rows_ref.at[m], p_ref.at[m], out_sems.at[m]).start()

    for m in range(count):
        pltpu.make_async_copy(rows_ref.at[m], p_ref.at[m], out_sems.at[m]).wait()


def project(place, plane, normed, pieces, rows):
    width, tokens = normed.shape
    parts = 4
    chunk = width // parts
    count = 4 * rows // chunk
    return pl.pallas_call(
        functools.partial(project_kernel, [spot for _, spot in pieces], parts),
        out_shape=(
            pltpu.HBM((count, chunk, tokens), BF),
            pltpu.HBM((count, tokens, chunk), BF),
        ),
        in_specs=[sspec(), sspec(), vspec()] + [hspec()] * 8,
        out_specs=(hspec(), hspec()),
        scratch_shapes=[
            pltpu.VMEM((4 * rows, width), BF),
            pltpu.VMEM((count, chunk, tokens), BF),
            pltpu.VMEM((count, tokens, chunk), BF),
            pltpu.SemaphoreType.DMA((8,)),
            pltpu.SemaphoreType.DMA((count,)),
        ],
        compiler_params=params(24),
        cost_estimate=cost(8 * rows * width * tokens, 2 * (4 * rows + tokens) * width),
        name="project",
    )(place, plane, normed, *[far(value) for value, _ in pieces])


def finish_kernel(
    spots, rows, at_ref, planes_ref, lens_ref, live_ref, n_ref, lat_ref, p0, k0, p1, k1, p2, k2, *rest
):
    pieces, rest = rest[:-15], rest[-15:]
    out_ref, w_ref, q_ref, k_ref, v_ref, mask_ref, e_ref, att_ref, wo_ref, done_ref = rest[:10]
    w_sems, part_sems, wo_sems, out_sems, base_sems = rest[10:]
    parts, chunk, tokens = q_ref.shape
    count = p0.shape[0]
    slots = wo_ref.shape[0]
    last = slots - 1
    x, y, core = at_ref[0], at_ref[1], at_ref[2]

    start_columns(at_ref, pieces[8 * last :], spots[8 * last :], rows, w_ref, w_sems)
    for part in range(parts):
        for kind, to in ((0, q_ref), (1, k_ref), (2, v_ref)):
            which = parts * kind + part
            for s, (p, k) in enumerate(((p0, k0), (p1, k1), (p2, k2))):

                @pl.when(planes_ref[which // count] == s)
                def _():
                    src = (k if kind == 1 else p).at[which % count]
                    pltpu.make_async_copy(src, to.at[part], part_sems.at[which]).start()

    cols, lanes = wo_ref.shape[1], wo_ref.shape[2] // 2
    ours = cols // 4
    skip = pieces[0].shape[-2] - ours
    copies = []
    for s in range(slots):
        for owner, c in ((0, core), (1, 1 - core)):
            for i, (px, py) in enumerate(places(x, y)):
                at = 8 * s + 4 * owner + i
                row = pl.multiple_of((2 * py + c) * ours, 16)
                lane = pl.multiple_of(px * lanes, 128)
                copies.append(
                    pltpu.make_async_copy(
                        piece_rows(pieces[at], spots[at], skip, ours),
                        wo_ref.at[s, pl.ds(row, ours), pl.ds(lane, lanes)],
                        wo_sems.at[at],
                    )
                )
    bases = []
    for s in range(slots):
        spot = pl.ds(pl.multiple_of(planes_ref[s] * cols, 128), cols)
        bases.append(pltpu.make_async_copy(lat_ref.at[:, spot], done_ref.at[s], base_sems.at[s]))
    for c in copies + bases:
        c.start()

    blocks = tokens // 128
    key = lax.broadcasted_iota(jnp.int32, (128, 256), 0)
    query = lax.broadcasted_iota(jnp.int32, (128, 256), 1) % 128
    for b in range(blocks):
        first = (key < WIN_TOK) & (query < WIN_TOK) & (key < lens_ref[2 * b])
        second = (key >= WIN_TOK) & (query >= WIN_TOK) & (key - WIN_TOK < lens_ref[2 * b + 1])
        mask_ref[b] = jnp.where(first | second, 1.0, 0.0).astype(F32)

    for m in range(count):
        if m < 2:
            wait_columns(m, pieces[8 * last :], spots[8 * last :], rows, w_ref, w_sems)
        which = planes_ref[last] * count + m
        out = project_chunk(m, which, parts, w_ref, n_ref)
        for kind, to in ((0, q_ref), (1, k_ref), (2, v_ref)):

            @pl.when(which // parts == kind)
            def _():
                to[which % parts] = out.T if kind == 1 else out

    ones = jnp.ones((16, 128), BF)
    blank = jnp.zeros((HEAD_DIM, 128), BF)
    pairs = chunk // 128

    @pl.loop(0, parts)
    def _(part):
        for kind in range(3):
            which = parts * kind + part

            @pl.when(planes_ref[which // count] != last)
            def _():
                pltpu.make_async_copy(p0.at[0], q_ref.at[0], part_sems.at[which]).wait()

        @pl.loop(0, pairs)
        def _(i):
            at = pl.ds(pl.multiple_of(i * 128, 128), 128)
            out_at = pl.ds(pl.multiple_of(part * chunk + i * 128, 128), 128)
            for b in range(blocks):
                tok = pl.ds(b * 128, 128)
                q = q_ref[part, at, tok]
                k = k_ref[part, tok, at]
                q0 = jnp.concatenate([q[:HEAD_DIM], blank], axis=0)
                q1 = jnp.concatenate([blank, q[HEAD_DIM:]], axis=0)
                scores = jnp.dot(k, jnp.concatenate([q0, q1], axis=1), preferred_element_type=F32)
                e_ref[b] = (jnp.exp(scores) * mask_ref[b]).astype(BF)
            for b in range(blocks):
                tok = pl.ds(b * 128, 128)
                v = v_ref[part, at, tok]
                got = jnp.dot(
                    jnp.concatenate([v, ones], axis=0), e_ref[b], preferred_element_type=F32
                )
                token = lax.broadcasted_iota(jnp.int32, (1, 256), 1) % 128
                first = (token < WIN_TOK) & (token < lens_ref[2 * b])
                second = (token >= WIN_TOK) & (token - WIN_TOK < lens_ref[2 * b + 1])
                keep = (first | second) & (b < live_ref[0])
                share = jnp.where(keep, 1.0 / got[128:129, :], 0.0)
                o0 = got[:HEAD_DIM, :128] * share[:, :128]
                o1 = got[HEAD_DIM:128, 128:] * share[:, 128:]
                att_ref[tok, out_at] = jnp.concatenate([o0, o1], axis=0).astype(BF).T

    outs = []
    for s in range(slots):
        for c in copies[8 * s : 8 * s + 8] + [bases[s]]:
            c.wait()
        spot = pl.ds(pl.multiple_of(planes_ref[s] * cols, 128), cols)
        update = lax.dot_general(
            att_ref[...], wo_ref[s], (((1,), (1,)), ((), ())), preferred_element_type=F32
        )
        done_ref[s] = (done_ref[s].astype(F32) + update).astype(BF)
        outs.append(pltpu.make_async_copy(done_ref.at[s], out_ref.at[:, spot], out_sems.at[s]))
        outs[s].start()
    for c in outs:
        c.wait()


def finish(place, planes, window_len, live_blocks, normed, latents, parts, pieces, rows):
    count, chunk, tokens = parts[0][0].shape
    width = normed.shape[0]
    slots = len(pieces) // 8
    return pl.pallas_call(
        functools.partial(finish_kernel, [spot for _, spot in pieces], rows),
        out_shape=jax.ShapeDtypeStruct((tokens, width), BF),
        in_specs=[sspec()] * 4 + [vspec()] + [hspec()] * (7 + len(pieces)),
        out_specs=hspec(),
        scratch_shapes=[
            pltpu.VMEM((4 * rows, width), BF),
            pltpu.VMEM((4, chunk, tokens), BF),
            pltpu.VMEM((4, tokens, chunk), BF),
            pltpu.VMEM((4, chunk, tokens), BF),
            pltpu.VMEM((tokens // 128, 128, 256), F32),
            pltpu.VMEM((tokens // 128, 128, 256), BF),
            pltpu.VMEM((tokens, width), BF),
            pltpu.VMEM((slots, width // slots, width), BF),
            pltpu.VMEM((slots, tokens, width // slots), BF),
            pltpu.SemaphoreType.DMA((8,)),
            pltpu.SemaphoreType.DMA((4 * count,)),
            pltpu.SemaphoreType.DMA((len(pieces),)),
            pltpu.SemaphoreType.DMA((slots,)),
            pltpu.SemaphoreType.DMA((slots,)),
        ],
        compiler_params=params(44),
        cost_estimate=cost(6 * width * width * tokens, 8 * width * tokens),
        name="finish",
    )(
        place,
        planes,
        window_len,
        live_blocks,
        normed,
        far(latents),
        *[far(a) for pair in parts for a in pair],
        *[far(value) for value, _ in pieces],
    )


def local(tile_count, latents, window_index, window_len, live_blocks, norm_gain, w_qkv, w_out):
    blocks, rows, width = latents.shape

    def along(axis, pairs):
        def move(value, name):
            with jax.named_scope(name):
                return lax.ppermute(value, axis, pairs)

        return move

    def across(bit):
        return along("tile", [(i, i ^ bit) for i in range(tile_count)])

    core, ys, z1, z2 = across(1), across(2), across(4), across(8)
    xs = along("group", [(0, 1), (1, 0)])
    xy = along(
        ("tile", "group"),
        [(2 * i + g, 2 * (i ^ 2) + 1 - g) for i in range(tile_count) for g in range(2)],
    )
    t = lax.axis_index("tile")
    x = lax.axis_index("group")
    z = t // 4
    place = jnp.stack([x, t // 2 % 2, t % 2]).astype(jnp.int32)
    planes = jnp.stack([z, z ^ 1, z ^ 2, z ^ 3]).astype(jnp.int32)

    nq = w_qkv.shape[1]

    def sync(*values):
        return lax.optimization_barrier(values)

    def share(**values):
        shared = []
        for name, value in values.items():
            if shared:
                value = sync(value, shared[-1])[0]
            shared.append(core(value, f"core_{name}"))
        return shared

    def slot(index, *values):
        return [(value, index if value.ndim == 3 else None) for value in values]

    u0 = jnp.concatenate([w_qkv.T, w_out.T], axis=0)
    u1, d0, x0, y0, u2 = z1(u0, "u1"), xy(u0, "d0"), xs(u0, "x0"), ys(u0, "y0"), z2(u0, "u2")
    normed = normed_columns(latents, window_index, norm_gain)
    cu0 = core(u0, "core_u0")
    u1, d0, x0, y0, u2, normed, cu0 = sync(u1, d0, x0, y0, u2, normed, cu0)
    u12 = jnp.stack([u1, u2])
    x2, y12, u3, d1 = xs(u2, "x2"), ys(u12, "y12"), z1(u2, "u3"), z1(d0, "d1")
    cx0, cy0 = share(x0=x0, y0=y0)
    x2, y12, u3, d1, cx0, cy0, u12 = sync(x2, y12, u3, d1, cx0, cy0, u12)
    x1, d2 = xs(u1, "x1"), ys(x2, "d2")
    cd0, cx2, cy12 = core(d0, "core_d0"), core(x2, "core_x2"), core(y12, "core_y12")
    s0 = slot(0, u0, x0, y0, d0, cu0, cx0, cy0, cd0)
    p0 = project(place, planes[0:1], normed, s0, nq)
    x1, d2, cx2, cy12, d1, u3, p0, u12 = sync(x1, d2, cx2, cy12, d1, u3, p0, u12)
    x3, y3, d3 = xs(u3, "x3"), ys(u3, "y3"), z1(d2, "d3")
    cu12, cx1 = share(u12=u12, x1=x1)
    cd2, cd1 = share(d2=d2, d1=d1)
    s2 = slot(1, u12, x2, y12, d2, cu12, cx2, cy12, cd2)
    p2 = project(place, planes[2:3], normed, s2, nq)
    x3, y3, d3, u3, p2, cx1, cd1 = sync(x3, y3, d3, u3, p2, cx1, cd1)
    cu3, cx3, cy3, cd3 = core(u3, "core_u3"), core(x3, "core_x3"), core(y3, "core_y3"), core(d3, "core_d3")
    s1 = slot(0, u12, x1, y12, d1, cu12, cx1, cy12, cd1)
    p1 = project(place, planes[1:2], normed, s1, nq)
    s3 = slot(0, u3, x3, y3, d3, cu3, cx3, cy3, cd3)
    flat = latents.reshape(blocks * rows, width)
    so = s0 + s1 + s2 + s3
    out = finish(place, planes, window_len, live_blocks, normed, flat, (p0, p1, p2), so, nq)
    return out.reshape(latents.shape)


def solution(mesh):
    in_specs = (
        P(("tile", "group"), None, None),
        P(("tile", "group")),
        P(("tile", "group")),
        P(("tile", "group")),
        P(),
        P("group", "tile"),
        P("group", "tile"),
    )
    out_specs = P(("tile", "group"), None, None)
    planes, chips, cores = 4, 2, 2
    if mesh.shape["group"] == 2 and mesh.shape["tile"] == planes * chips * cores:
        body = functools.partial(local, mesh.shape["tile"])
    else:
        body = general
    return jax.shard_map(body, mesh=mesh, in_specs=in_specs, out_specs=out_specs, check_vma=False)
```

```python
import functools
import math

import jax
import jax.numpy as jnp
from jax import lax
from jax.experimental import pallas as pl
from jax.experimental.pallas import tpu as pltpu
from jax.sharding import PartitionSpec as P

HEAD_DIM = 64
WIN_SIDE = 8
WIN_COLS = 60
WIN_TOK = 64
EPS = 1e-06
BF = jnp.bfloat16
F32 = jnp.float32


def position_table(window_ids, width):
    token_ids = jnp.arange(WIN_TOK, dtype=jnp.int32)
    row_pos = window_ids[:, None] // WIN_COLS * WIN_SIDE + token_ids[None, :] // WIN_SIDE
    col_pos = window_ids[:, None] % WIN_COLS * WIN_SIDE + token_ids[None, :] % WIN_SIDE
    quarter = width // 4
    frequency = jnp.exp(jnp.arange(quarter, dtype=F32) * (-math.log(10000.0) / quarter))
    row_angle = row_pos.astype(F32)[:, :, None] * frequency
    col_angle = col_pos.astype(F32)[:, :, None] * frequency
    return jnp.concatenate(
        [jnp.sin(row_angle), jnp.cos(row_angle), jnp.sin(col_angle), jnp.cos(col_angle)], axis=-1
    )


def head_norm(values):
    return (values * lax.rsqrt(jnp.mean(values * values, axis=-1, keepdims=True) + EPS)).astype(BF)


def window_layer(blocks_in, window_ids, window_lens, norm_gain, w_qkv, w_out):
    width = blocks_in.shape[-1]
    count = window_ids.shape[0]
    heads = width // HEAD_DIM
    stream = blocks_in.reshape(count, WIN_TOK, width).astype(F32) + position_table(window_ids, width)
    scale = lax.rsqrt(jnp.mean(stream * stream, axis=-1, keepdims=True) + EPS)
    normed = (stream * scale * norm_gain).astype(BF).reshape(count * WIN_TOK, width)
    full_rows = lax.all_gather(w_qkv, "group", axis=0, tiled=True)
    projected = jnp.dot(
        normed,
        lax.all_gather(full_rows, "tile", axis=1, tiled=True),
        preferred_element_type=F32,
    ).reshape(count, WIN_TOK, 3, heads, HEAD_DIM)
    queries = head_norm(projected[:, :, 0])
    keys = head_norm(projected[:, :, 1])
    values = projected[:, :, 2].astype(BF)
    scores = jnp.einsum("wqhd,wkhd->whqk", queries, keys, preferred_element_type=F32) * HEAD_DIM**-0.5
    key_mask = jnp.arange(WIN_TOK, dtype=jnp.int32)[None, :] < window_lens[:, None]
    weights = jnp.exp(scores) * key_mask[:, None, None, :].astype(F32)
    probs = (weights / jnp.sum(weights, axis=-1, keepdims=True)).astype(BF)
    attended = jnp.einsum("whqk,wkhd->wqhd", probs, values, preferred_element_type=F32)
    attended = attended.astype(BF).reshape(count * WIN_TOK, width)
    out_rows = lax.all_gather(w_out, "group", axis=0, tiled=True)
    update = jnp.dot(
        attended, lax.all_gather(out_rows, "tile", axis=1, tiled=True), preferred_element_type=F32
    )
    base = blocks_in.reshape(count * WIN_TOK, width).astype(F32)
    token_live = key_mask.reshape(count * WIN_TOK)[:, None]
    return jnp.where(token_live, base + update, base).astype(BF).reshape(blocks_in.shape)


def general(latents, window_index, window_len, live_blocks, norm_gain, w_qkv, w_out):
    slot_ids = jnp.arange(latents.shape[0], dtype=jnp.int32)
    live_mask = (slot_ids < live_blocks[0])[:, None, None]
    finished = window_layer(latents, window_index, window_len, norm_gain, w_qkv, w_out)
    return jnp.where(live_mask, finished, latents)


def hspec():
    return pl.BlockSpec(memory_space=pltpu.HBM)


def vspec():
    return pl.BlockSpec(memory_space=pltpu.VMEM)


def sspec():
    return pl.BlockSpec(memory_space=pltpu.SMEM)


def params(mib):
    return pltpu.CompilerParams(vmem_limit_bytes=mib * 1024 * 1024)


def far(value):
    return pltpu.with_memory_space_constraint(value, pltpu.HBM)


def cost(flops, moved):
    return pl.CostEstimate(flops=flops, bytes_accessed=moved, transcendentals=0)


def norm_kernel(ids_ref, lat_ref, gain_ref, freq_ref, out_ref, pos_ref):
    blocks, _, width = lat_ref.shape
    quarter = width // 4
    freq = freq_ref[...]
    step = lax.broadcasted_iota(jnp.int32, (WIN_SIDE, quarter), 0).astype(F32) * freq
    sin_step, cos_step = jnp.sin(step), jnp.cos(step)
    gain = gain_ref[...]

    @pl.loop(0, blocks)
    def _(b):
        for w in range(2):
            place = ids_ref[2 * b + w]
            row = (place // WIN_COLS * WIN_SIDE).astype(F32)
            col = (place % WIN_COLS * WIN_SIDE).astype(F32)
            for at, start in ((0, row), (2 * quarter, col)):
                base = start * freq
                sin_base, cos_base = jnp.sin(base), jnp.cos(base)
                sines = sin_base * cos_step + cos_base * sin_step
                cosines = cos_base * cos_step - sin_base * sin_step
                for more, table in ((0, sines), (quarter, cosines)):
                    where = pl.ds(at + more, quarter)
                    for i in range(WIN_SIDE):
                        rows = pl.ds(w * WIN_TOK + i * WIN_SIDE, WIN_SIDE)
                        if at == 0:
                            pos_ref[rows, where] = jnp.broadcast_to(
                                table[i : i + 1, :], (WIN_SIDE, quarter)
                            )
                        else:
                            pos_ref[rows, where] = table
        stream = lat_ref[b].astype(F32) + pos_ref[...]
        scale = lax.rsqrt(jnp.mean(stream * stream, axis=-1, keepdims=True) + EPS)
        normed = (stream * scale * gain).astype(BF)
        out_ref[:, pl.ds(pl.multiple_of(b * 128, 128), 128)] = normed.T


def normed_columns(latents, window_index, norm_gain):
    blocks, rows, width = latents.shape
    quarter = width // 4
    freq = jnp.exp(jnp.arange(quarter, dtype=F32) * (-math.log(10000.0) / quarter))
    return pl.pallas_call(
        norm_kernel,
        out_shape=jax.ShapeDtypeStruct((width, blocks * rows), BF),
        in_specs=[sspec(), vspec(), vspec(), vspec()],
        out_specs=vspec(),
        scratch_shapes=[pltpu.VMEM((rows, width), F32)],
        compiler_params=params(24),
        cost_estimate=cost(40 * blocks * rows * width, 4 * blocks * rows * width),
        name="norm",
    )(window_index, latents, norm_gain.reshape(1, width), freq.reshape(1, quarter))


def places(x, y):
    return ((x, y), (1 - x, y), (x, 1 - y), (1 - x, 1 - y))


def piece_rows(ref, spot, start, rows):
    part = pl.ds(start, rows)
    return ref.at[part, :] if spot is None else ref.at[spot, part, :]


def start_columns(at_ref, pieces, spots, rows, w_ref, sems):
    x, y, core = at_ref[0], at_ref[1], at_ref[2]
    lanes = w_ref.shape[1] // 2
    for i, (px, py) in enumerate(places(x, y)):
        for owner, c in ((0, core), (1, 1 - core)):
            row = pl.multiple_of((2 * py + c) * rows, 16)
            lane = pl.multiple_of(px * lanes, 128)
            pltpu.make_async_copy(
                piece_rows(pieces[4 * owner + i], spots[4 * owner + i], 0, rows),
                w_ref.at[pl.ds(row, rows), pl.ds(lane, lanes)],
                sems.at[py * 4 + 2 * owner + i % 2],
            ).start()


def wait_columns(half, pieces, spots, rows, w_ref, sems):
    lanes = w_ref.shape[1] // 2
    for i in range(4):
        pltpu.make_async_copy(
            piece_rows(pieces[0], spots[0], 0, rows),
            w_ref.at[pl.ds(0, rows), pl.ds(0, lanes)],
            sems.at[4 * half + i],
        ).wait()


def project_chunk(m, which, parts, w_ref, n_ref):
    tokens = n_ref.shape[1]
    chunk = n_ref.shape[0] // parts
    got = jnp.dot(w_ref[m * chunk : (m + 1) * chunk, :], n_ref[...], preferred_element_type=F32)
    got = got.reshape(chunk // HEAD_DIM, HEAD_DIM, tokens)
    ms = jnp.mean(got * got, axis=1, keepdims=True)
    scale = jnp.where(which < 2 * parts, lax.rsqrt(ms + EPS), 1.0)
    scale = jnp.where(which < parts, scale * HEAD_DIM**-0.5, scale)
    return (got * scale).astype(BF).reshape(chunk, tokens)


def project_kernel(spots, parts, at_ref, plane_ref, n_ref, *rest):
    pieces, (p_ref, k_ref, w_ref, rows_ref, cols_ref, sems, out_sems) = rest[:8], rest[8:]
    rows = w_ref.shape[0] // 4
    start_columns(at_ref, pieces, spots, rows, w_ref, sems)
    count = p_ref.shape[0]
    for m in range(count):
        if m < 2:
            wait_columns(m, pieces, spots, rows, w_ref, sems)
        which = plane_ref[0] * count + m
        out = project_chunk(m, which, parts, w_ref, n_ref)
        rows_ref[m] = out
        cols_ref[m] = out.T
        is_key = (which >= parts) & (which < 2 * parts)

        @pl.when(is_key)
        def _():
            pltpu.make_async_copy(cols_ref.at[m], k_ref.at[m], out_sems.at[m]).start()

        @pl.when(jnp.logical_not(is_key))
        def _():
            pltpu.make_async_copy(rows_ref.at[m], p_ref.at[m], out_sems.at[m]).start()

    for m in range(count):
        pltpu.make_async_copy(rows_ref.at[m], p_ref.at[m], out_sems.at[m]).wait()


def project(place, plane, normed, pieces, rows):
    width, tokens = normed.shape
    parts = 4
    chunk = width // parts
    count = 4 * rows // chunk
    return pl.pallas_call(
        functools.partial(project_kernel, [spot for _, spot in pieces], parts),
        out_shape=(
            pltpu.HBM((count, chunk, tokens), BF),
            pltpu.HBM((count, tokens, chunk), BF),
        ),
        in_specs=[sspec(), sspec(), vspec()] + [hspec()] * 8,
        out_specs=(hspec(), hspec()),
        scratch_shapes=[
            pltpu.VMEM((4 * rows, width), BF),
            pltpu.VMEM((count, chunk, tokens), BF),
            pltpu.VMEM((count, tokens, chunk), BF),
            pltpu.SemaphoreType.DMA((8,)),
            pltpu.SemaphoreType.DMA((count,)),
        ],
        compiler_params=params(24),
        cost_estimate=cost(8 * rows * width * tokens, 2 * (4 * rows + tokens) * width),
        name="project",
    )(place, plane, normed, *[far(value) for value, _ in pieces])


def finish_kernel(
    spots, rows, at_ref, planes_ref, lens_ref, live_ref, n_ref, lat_ref, p0, k0, p1, k1, p2, k2, *rest
):
    pieces, rest = rest[:-15], rest[-15:]
    out_ref, w_ref, q_ref, k_ref, v_ref, mask_ref, e_ref, att_ref, wo_ref, done_ref = rest[:10]
    w_sems, part_sems, wo_sems, out_sems, base_sems = rest[10:]
    parts, chunk, tokens = q_ref.shape
    count = p0.shape[0]
    slots = wo_ref.shape[0]
    last = slots - 1
    x, y, core = at_ref[0], at_ref[1], at_ref[2]

    start_columns(at_ref, pieces[8 * last :], spots[8 * last :], rows, w_ref, w_sems)
    for part in range(parts):
        for kind, to in ((0, q_ref), (1, k_ref), (2, v_ref)):
            which = parts * kind + part
            for s, (p, k) in enumerate(((p0, k0), (p1, k1), (p2, k2))):

                @pl.when(planes_ref[which // count] == s)
                def _():
                    src = (k if kind == 1 else p).at[which % count]
                    pltpu.make_async_copy(src, to.at[part], part_sems.at[which]).start()

    cols, lanes = wo_ref.shape[1], wo_ref.shape[2] // 2
    ours = cols // 4
    skip = pieces[0].shape[-2] - ours
    copies = []
    for s in range(slots):
        for owner, c in ((0, core), (1, 1 - core)):
            for i, (px, py) in enumerate(places(x, y)):
                at = 8 * s + 4 * owner + i
                row = pl.multiple_of((2 * py + c) * ours, 16)
                lane = pl.multiple_of(px * lanes, 128)
                copies.append(
                    pltpu.make_async_copy(
                        piece_rows(pieces[at], spots[at], skip, ours),
                        wo_ref.at[s, pl.ds(row, ours), pl.ds(lane, lanes)],
                        wo_sems.at[at],
                    )
                )
    bases = []
    for s in range(slots):
        spot = pl.ds(pl.multiple_of(planes_ref[s] * cols, 128), cols)
        bases.append(pltpu.make_async_copy(lat_ref.at[:, spot], done_ref.at[s], base_sems.at[s]))
    for c in copies + bases:
        c.start()

    blocks = tokens // 128
    key = lax.broadcasted_iota(jnp.int32, (128, 256), 0)
    query = lax.broadcasted_iota(jnp.int32, (128, 256), 1) % 128
    for b in range(blocks):
        first = (key < WIN_TOK) & (query < WIN_TOK) & (key < lens_ref[2 * b])
        second = (key >= WIN_TOK) & (query >= WIN_TOK) & (key - WIN_TOK < lens_ref[2 * b + 1])
        mask_ref[b] = jnp.where(first | second, 1.0, 0.0).astype(F32)

    for m in range(count):
        if m < 2:
            wait_columns(m, pieces[8 * last :], spots[8 * last :], rows, w_ref, w_sems)
        which = planes_ref[last] * count + m
        out = project_chunk(m, which, parts, w_ref, n_ref)
        for kind, to in ((0, q_ref), (1, k_ref), (2, v_ref)):

            @pl.when(which // parts == kind)
            def _():
                to[which % parts] = out.T if kind == 1 else out

    ones = jnp.ones((16, 128), BF)
    blank = jnp.zeros((HEAD_DIM, 128), BF)
    pairs = chunk // 128

    @pl.loop(0, parts)
    def _(part):
        for kind in range(3):
            which = parts * kind + part

            @pl.when(planes_ref[which // count] != last)
            def _():
                pltpu.make_async_copy(p0.at[0], q_ref.at[0], part_sems.at[which]).wait()

        @pl.loop(0, pairs)
        def _(i):
            at = pl.ds(pl.multiple_of(i * 128, 128), 128)
            out_at = pl.ds(pl.multiple_of(part * chunk + i * 128, 128), 128)
            for b in range(blocks):
                tok = pl.ds(b * 128, 128)
                q = q_ref[part, at, tok]
                k = k_ref[part, tok, at]
                q0 = jnp.concatenate([q[:HEAD_DIM], blank], axis=0)
                q1 = jnp.concatenate([blank, q[HEAD_DIM:]], axis=0)
                scores = jnp.dot(k, jnp.concatenate([q0, q1], axis=1), preferred_element_type=F32)
                e_ref[b] = (jnp.exp(scores) * mask_ref[b]).astype(BF)
            for b in range(blocks):
                tok = pl.ds(b * 128, 128)
                v = v_ref[part, at, tok]
                got = jnp.dot(
                    jnp.concatenate([v, ones], axis=0), e_ref[b], preferred_element_type=F32
                )
                token = lax.broadcasted_iota(jnp.int32, (1, 256), 1) % 128
                first = (token < WIN_TOK) & (token < lens_ref[2 * b])
                second = (token >= WIN_TOK) & (token - WIN_TOK < lens_ref[2 * b + 1])
                keep = (first | second) & (b < live_ref[0])
                share = jnp.where(keep, 1.0 / got[128:129, :], 0.0)
                o0 = got[:HEAD_DIM, :128] * share[:, :128]
                o1 = got[HEAD_DIM:128, 128:] * share[:, 128:]
                att_ref[tok, out_at] = jnp.concatenate([o0, o1], axis=0).astype(BF).T

    outs = []
    for s in range(slots):
        for c in copies[8 * s : 8 * s + 8] + [bases[s]]:
            c.wait()
        spot = pl.ds(pl.multiple_of(planes_ref[s] * cols, 128), cols)
        update = lax.dot_general(
            att_ref[...], wo_ref[s], (((1,), (1,)), ((), ())), preferred_element_type=F32
        )
        done_ref[s] = (done_ref[s].astype(F32) + update).astype(BF)
        outs.append(pltpu.make_async_copy(done_ref.at[s], out_ref.at[:, spot], out_sems.at[s]))
        outs[s].start()
    for c in outs:
        c.wait()


def finish(place, planes, window_len, live_blocks, normed, latents, parts, pieces, rows):
    count, chunk, tokens = parts[0][0].shape
    width = normed.shape[0]
    slots = len(pieces) // 8
    return pl.pallas_call(
        functools.partial(finish_kernel, [spot for _, spot in pieces], rows),
        out_shape=jax.ShapeDtypeStruct((tokens, width), BF),
        in_specs=[sspec()] * 4 + [vspec()] + [hspec()] * (7 + len(pieces)),
        out_specs=hspec(),
        scratch_shapes=[
            pltpu.VMEM((4 * rows, width), BF),
            pltpu.VMEM((4, chunk, tokens), BF),
            pltpu.VMEM((4, tokens, chunk), BF),
            pltpu.VMEM((4, chunk, tokens), BF),
            pltpu.VMEM((tokens // 128, 128, 256), F32),
            pltpu.VMEM((tokens // 128, 128, 256), BF),
            pltpu.VMEM((tokens, width), BF),
            pltpu.VMEM((slots, width // slots, width), BF),
            pltpu.VMEM((slots, tokens, width // slots), BF),
            pltpu.SemaphoreType.DMA((8,)),
            pltpu.SemaphoreType.DMA((4 * count,)),
            pltpu.SemaphoreType.DMA((len(pieces),)),
            pltpu.SemaphoreType.DMA((slots,)),
            pltpu.SemaphoreType.DMA((slots,)),
        ],
        compiler_params=params(44),
        cost_estimate=cost(6 * width * width * tokens, 8 * width * tokens),
        name="finish",
    )(
        place,
        planes,
        window_len,
        live_blocks,
        normed,
        far(latents),
        *[far(a) for pair in parts for a in pair],
        *[far(value) for value, _ in pieces[:-8]],
        *[value for value, _ in pieces[-8:]],
    )


def local(tile_count, latents, window_index, window_len, live_blocks, norm_gain, w_qkv, w_out):
    blocks, rows, width = latents.shape

    def along(axis, pairs):
        def move(value, name):
            with jax.named_scope(name):
                return lax.ppermute(value, axis, pairs)

        return move

    def across(bit):
        return along("tile", [(i, i ^ bit) for i in range(tile_count)])

    core, ys, z1, z2 = across(1), across(2), across(4), across(8)
    xs = along("group", [(0, 1), (1, 0)])
    xy = along(
        ("tile", "group"),
        [(2 * i + g, 2 * (i ^ 2) + 1 - g) for i in range(tile_count) for g in range(2)],
    )
    t = lax.axis_index("tile")
    x = lax.axis_index("group")
    z = t // 4
    place = jnp.stack([x, t // 2 % 2, t % 2]).astype(jnp.int32)
    planes = jnp.stack([z, z ^ 1, z ^ 2, z ^ 3]).astype(jnp.int32)

    nq = w_qkv.shape[1]

    def sync(*values):
        return lax.optimization_barrier(values)

    def share(**values):
        shared = []
        for name, value in values.items():
            if shared:
                value = sync(value, shared[-1])[0]
            shared.append(core(value, f"core_{name}"))
        return shared

    def slot(index, *values):
        return [(value, index if value.ndim == 3 else None) for value in values]

    u0 = jnp.concatenate([w_qkv.T, w_out.T], axis=0)
    u1, d0, x0, y0, u2 = z1(u0, "u1"), xy(u0, "d0"), xs(u0, "x0"), ys(u0, "y0"), z2(u0, "u2")
    normed = normed_columns(latents, window_index, norm_gain)
    cu0 = core(u0, "core_u0")
    u1, d0, x0, y0, u2, normed, cu0 = sync(u1, d0, x0, y0, u2, normed, cu0)
    u12 = jnp.stack([u1, u2])
    x2, y12, u3, d1 = xs(u2, "x2"), ys(u12, "y12"), z1(u2, "u3"), z1(d0, "d1")
    cx0, cy0 = share(x0=x0, y0=y0)
    x2, y12, u3, d1, cx0, cy0, u12 = sync(x2, y12, u3, d1, cx0, cy0, u12)
    x1, d2 = xs(u1, "x1"), ys(x2, "d2")
    cd0, cx2, cy12, cu12 = (
        core(value, name) for value, name in ((d0, "core_d0"), (x2, "core_x2"), (y12, "core_y12"), (u12, "core_u12"))
    )
    s0 = slot(0, u0, x0, y0, d0, cu0, cx0, cy0, cd0)
    p0 = project(place, planes[0:1], normed, s0, nq)
    x1, d2, cx2, cy12, cu12, d1, u3, p0 = sync(x1, d2, cx2, cy12, cu12, d1, u3, p0)
    x3, y3, d3 = xs(u3, "x3"), ys(u3, "y3"), z1(d2, "d3")
    cd2, cx1, cd1 = core(d2, "core_d2"), core(x1, "core_x1"), core(d1, "core_d1")
    s2 = slot(1, u12, x2, y12, d2, cu12, cx2, cy12, cd2)
    p2 = project(place, planes[2:3], normed, s2, nq)
    s1 = slot(0, u12, x1, y12, d1, cu12, cx1, cy12, cd1)
    p1 = project(place, planes[1:2], normed, s1, nq)
    x3, y3, d3, u3, p2, p1 = sync(x3, y3, d3, u3, p2, p1)
    cu3, cx3, cy3, cd3 = core(u3, "core_u3"), core(x3, "core_x3"), core(y3, "core_y3"), core(d3, "core_d3")
    s3 = slot(0, u3, x3, y3, d3, cu3, cx3, cy3, cd3)
    flat = latents.reshape(blocks * rows, width)
    so = s0 + s1 + s2 + s3
    out = finish(place, planes, window_len, live_blocks, normed, flat, (p0, p1, p2), so, nq)
    return out.reshape(latents.shape)


def solution(mesh):
    in_specs = (
        P(("tile", "group"), None, None),
        P(("tile", "group")),
        P(("tile", "group")),
        P(("tile", "group")),
        P(),
        P("group", "tile"),
        P("group", "tile"),
    )
    out_specs = P(("tile", "group"), None, None)
    planes, chips, cores = 4, 2, 2
    if mesh.shape["group"] == 2 and mesh.shape["tile"] == planes * chips * cores:
        body = functools.partial(local, mesh.shape["tile"])
    else:
        body = general
    return jax.shard_map(body, mesh=mesh, in_specs=in_specs, out_specs=out_specs, check_vma=False)
```

```python
import functools
import math

import jax
import jax.numpy as jnp
from jax import lax
from jax.experimental import pallas as pl
from jax.experimental.pallas import tpu as pltpu
from jax.sharding import PartitionSpec as P

HEAD_DIM = 64
WIN_SIDE = 8
WIN_COLS = 60
WIN_TOK = 64
EPS = 1e-06
BF = jnp.bfloat16
F32 = jnp.float32


def position_table(window_ids, width):
    token_ids = jnp.arange(WIN_TOK, dtype=jnp.int32)
    row_pos = window_ids[:, None] // WIN_COLS * WIN_SIDE + token_ids[None, :] // WIN_SIDE
    col_pos = window_ids[:, None] % WIN_COLS * WIN_SIDE + token_ids[None, :] % WIN_SIDE
    quarter = width // 4
    frequency = jnp.exp(jnp.arange(quarter, dtype=F32) * (-math.log(10000.0) / quarter))
    row_angle = row_pos.astype(F32)[:, :, None] * frequency
    col_angle = col_pos.astype(F32)[:, :, None] * frequency
    return jnp.concatenate(
        [jnp.sin(row_angle), jnp.cos(row_angle), jnp.sin(col_angle), jnp.cos(col_angle)], axis=-1
    )


def head_norm(values):
    return (values * lax.rsqrt(jnp.mean(values * values, axis=-1, keepdims=True) + EPS)).astype(BF)


def window_layer(blocks_in, window_ids, window_lens, norm_gain, w_qkv, w_out):
    width = blocks_in.shape[-1]
    count = window_ids.shape[0]
    heads = width // HEAD_DIM
    stream = blocks_in.reshape(count, WIN_TOK, width).astype(F32) + position_table(window_ids, width)
    scale = lax.rsqrt(jnp.mean(stream * stream, axis=-1, keepdims=True) + EPS)
    normed = (stream * scale * norm_gain).astype(BF).reshape(count * WIN_TOK, width)
    full_rows = lax.all_gather(w_qkv, "group", axis=0, tiled=True)
    projected = jnp.dot(
        normed,
        lax.all_gather(full_rows, "tile", axis=1, tiled=True),
        preferred_element_type=F32,
    ).reshape(count, WIN_TOK, 3, heads, HEAD_DIM)
    queries = head_norm(projected[:, :, 0])
    keys = head_norm(projected[:, :, 1])
    values = projected[:, :, 2].astype(BF)
    scores = jnp.einsum("wqhd,wkhd->whqk", queries, keys, preferred_element_type=F32) * HEAD_DIM**-0.5
    key_mask = jnp.arange(WIN_TOK, dtype=jnp.int32)[None, :] < window_lens[:, None]
    weights = jnp.exp(scores) * key_mask[:, None, None, :].astype(F32)
    probs = (weights / jnp.sum(weights, axis=-1, keepdims=True)).astype(BF)
    attended = jnp.einsum("whqk,wkhd->wqhd", probs, values, preferred_element_type=F32)
    attended = attended.astype(BF).reshape(count * WIN_TOK, width)
    out_rows = lax.all_gather(w_out, "group", axis=0, tiled=True)
    update = jnp.dot(
        attended, lax.all_gather(out_rows, "tile", axis=1, tiled=True), preferred_element_type=F32
    )
    base = blocks_in.reshape(count * WIN_TOK, width).astype(F32)
    token_live = key_mask.reshape(count * WIN_TOK)[:, None]
    return jnp.where(token_live, base + update, base).astype(BF).reshape(blocks_in.shape)


def general(latents, window_index, window_len, live_blocks, norm_gain, w_qkv, w_out):
    slot_ids = jnp.arange(latents.shape[0], dtype=jnp.int32)
    live_mask = (slot_ids < live_blocks[0])[:, None, None]
    finished = window_layer(latents, window_index, window_len, norm_gain, w_qkv, w_out)
    return jnp.where(live_mask, finished, latents)


def hspec():
    return pl.BlockSpec(memory_space=pltpu.HBM)


def vspec():
    return pl.BlockSpec(memory_space=pltpu.VMEM)


def sspec():
    return pl.BlockSpec(memory_space=pltpu.SMEM)


def params(mib):
    return pltpu.CompilerParams(vmem_limit_bytes=mib * 1024 * 1024)


def far(value):
    return pltpu.with_memory_space_constraint(value, pltpu.HBM)


def cost(flops, moved):
    return pl.CostEstimate(flops=flops, bytes_accessed=moved, transcendentals=0)


def norm_kernel(ids_ref, lat_ref, gain_ref, freq_ref, out_ref, pos_ref):
    blocks, _, width = lat_ref.shape
    quarter = width // 4
    freq = freq_ref[...]
    step = lax.broadcasted_iota(jnp.int32, (WIN_SIDE, quarter), 0).astype(F32) * freq
    sin_step, cos_step = jnp.sin(step), jnp.cos(step)
    gain = gain_ref[...]

    @pl.loop(0, blocks)
    def _(b):
        for w in range(2):
            place = ids_ref[2 * b + w]
            row = (place // WIN_COLS * WIN_SIDE).astype(F32)
            col = (place % WIN_COLS * WIN_SIDE).astype(F32)
            for at, start in ((0, row), (2 * quarter, col)):
                base = start * freq
                sin_base, cos_base = jnp.sin(base), jnp.cos(base)
                sines = sin_base * cos_step + cos_base * sin_step
                cosines = cos_base * cos_step - sin_base * sin_step
                for more, table in ((0, sines), (quarter, cosines)):
                    where = pl.ds(at + more, quarter)
                    for i in range(WIN_SIDE):
                        rows = pl.ds(w * WIN_TOK + i * WIN_SIDE, WIN_SIDE)
                        if at == 0:
                            pos_ref[rows, where] = jnp.broadcast_to(
                                table[i : i + 1, :], (WIN_SIDE, quarter)
                            )
                        else:
                            pos_ref[rows, where] = table
        stream = lat_ref[b].astype(F32) + pos_ref[...]
        scale = lax.rsqrt(jnp.mean(stream * stream, axis=-1, keepdims=True) + EPS)
        normed = (stream * scale * gain).astype(BF)
        out_ref[:, pl.ds(pl.multiple_of(b * 128, 128), 128)] = normed.T


def normed_columns(latents, window_index, norm_gain):
    blocks, rows, width = latents.shape
    quarter = width // 4
    freq = jnp.exp(jnp.arange(quarter, dtype=F32) * (-math.log(10000.0) / quarter))
    return pl.pallas_call(
        norm_kernel,
        out_shape=jax.ShapeDtypeStruct((width, blocks * rows), BF),
        in_specs=[sspec(), vspec(), vspec(), vspec()],
        out_specs=vspec(),
        scratch_shapes=[pltpu.VMEM((rows, width), F32)],
        compiler_params=params(24),
        cost_estimate=cost(40 * blocks * rows * width, 4 * blocks * rows * width),
        name="norm",
    )(window_index, latents, norm_gain.reshape(1, width), freq.reshape(1, quarter))


def places(x, y):
    return ((x, y), (1 - x, y), (x, 1 - y), (1 - x, 1 - y))


def piece_rows(ref, spot, start, rows):
    part = pl.ds(start, rows)
    return ref.at[part, :] if spot is None else ref.at[spot, part, :]


def start_columns(at_ref, pieces, spots, rows, w_ref, sems):
    x, y, core = at_ref[0], at_ref[1], at_ref[2]
    lanes = w_ref.shape[1] // 2
    for i, (px, py) in enumerate(places(x, y)):
        for owner, c in ((0, core), (1, 1 - core)):
            row = pl.multiple_of((2 * py + c) * rows, 16)
            lane = pl.multiple_of(px * lanes, 128)
            pltpu.make_async_copy(
                piece_rows(pieces[4 * owner + i], spots[4 * owner + i], 0, rows),
                w_ref.at[pl.ds(row, rows), pl.ds(lane, lanes)],
                sems.at[py * 4 + 2 * owner + i % 2],
            ).start()


def wait_columns(half, pieces, spots, rows, w_ref, sems):
    lanes = w_ref.shape[1] // 2
    for i in range(4):
        pltpu.make_async_copy(
            piece_rows(pieces[0], spots[0], 0, rows),
            w_ref.at[pl.ds(0, rows), pl.ds(0, lanes)],
            sems.at[4 * half + i],
        ).wait()


def project_chunk(m, which, parts, w_ref, n_ref):
    tokens = n_ref.shape[1]
    chunk = n_ref.shape[0] // parts
    got = jnp.dot(w_ref[m * chunk : (m + 1) * chunk, :], n_ref[...], preferred_element_type=F32)
    got = got.reshape(chunk // HEAD_DIM, HEAD_DIM, tokens)
    ms = jnp.mean(got * got, axis=1, keepdims=True)
    scale = jnp.where(which < 2 * parts, lax.rsqrt(ms + EPS), 1.0)
    scale = jnp.where(which < parts, scale * HEAD_DIM**-0.5, scale)
    return (got * scale).astype(BF).reshape(chunk, tokens)


def project_kernel(spots, parts, at_ref, plane_ref, n_ref, *rest):
    pieces, (p_ref, k_ref, w_ref, rows_ref, cols_ref, sems, out_sems) = rest[:8], rest[8:]
    rows = w_ref.shape[0] // 4
    start_columns(at_ref, pieces, spots, rows, w_ref, sems)
    count = p_ref.shape[0]
    for m in range(count):
        if m < 2:
            wait_columns(m, pieces, spots, rows, w_ref, sems)
        which = plane_ref[0] * count + m
        out = project_chunk(m, which, parts, w_ref, n_ref)
        rows_ref[m] = out
        cols_ref[m] = out.T
        is_key = (which >= parts) & (which < 2 * parts)

        @pl.when(is_key)
        def _():
            pltpu.make_async_copy(cols_ref.at[m], k_ref.at[m], out_sems.at[m]).start()

        @pl.when(jnp.logical_not(is_key))
        def _():
            pltpu.make_async_copy(rows_ref.at[m], p_ref.at[m], out_sems.at[m]).start()

    for m in range(count):
        pltpu.make_async_copy(rows_ref.at[m], p_ref.at[m], out_sems.at[m]).wait()


def project(place, plane, normed, pieces, rows):
    width, tokens = normed.shape
    parts = 4
    chunk = width // parts
    count = 4 * rows // chunk
    return pl.pallas_call(
        functools.partial(project_kernel, [spot for _, spot in pieces], parts),
        out_shape=(
            pltpu.HBM((count, chunk, tokens), BF),
            pltpu.HBM((count, tokens, chunk), BF),
        ),
        in_specs=[sspec(), sspec(), vspec()] + [hspec()] * 8,
        out_specs=(hspec(), hspec()),
        scratch_shapes=[
            pltpu.VMEM((4 * rows, width), BF),
            pltpu.VMEM((count, chunk, tokens), BF),
            pltpu.VMEM((count, tokens, chunk), BF),
            pltpu.SemaphoreType.DMA((8,)),
            pltpu.SemaphoreType.DMA((count,)),
        ],
        compiler_params=params(24),
        cost_estimate=cost(8 * rows * width * tokens, 2 * (4 * rows + tokens) * width),
        name="project",
    )(place, plane, normed, *[far(value) for value, _ in pieces])


def finish_kernel(
    spots, rows, at_ref, planes_ref, lens_ref, live_ref, n_ref, lat_ref, p0, k0, p1, k1, p2, k2, *rest
):
    pieces, rest = rest[:-15], rest[-15:]
    out_ref, w_ref, q_ref, k_ref, v_ref, mask_ref, e_ref, att_ref, wo_ref, done_ref = rest[:10]
    w_sems, part_sems, wo_sems, out_sems, base_sems = rest[10:]
    parts, chunk, tokens = q_ref.shape
    count = p0.shape[0]
    slots = wo_ref.shape[0]
    last = slots - 1
    x, y, core = at_ref[0], at_ref[1], at_ref[2]

    start_columns(at_ref, pieces[8 * last :], spots[8 * last :], rows, w_ref, w_sems)
    for part in range(parts):
        for kind, to in ((0, q_ref), (1, k_ref), (2, v_ref)):
            which = parts * kind + part
            for s, (p, k) in enumerate(((p0, k0), (p1, k1), (p2, k2))):

                @pl.when(planes_ref[which // count] == s)
                def _():
                    src = (k if kind == 1 else p).at[which % count]
                    pltpu.make_async_copy(src, to.at[part], part_sems.at[which]).start()

    cols, lanes = wo_ref.shape[1], wo_ref.shape[2] // 2
    ours = cols // 4
    skip = pieces[0].shape[-2] - ours
    copies = []
    for s in range(slots):
        for owner, c in ((0, core), (1, 1 - core)):
            for i, (px, py) in enumerate(places(x, y)):
                at = 8 * s + 4 * owner + i
                row = pl.multiple_of((2 * py + c) * ours, 16)
                lane = pl.multiple_of(px * lanes, 128)
                copies.append(
                    pltpu.make_async_copy(
                        piece_rows(pieces[at], spots[at], skip, ours),
                        wo_ref.at[s, pl.ds(row, ours), pl.ds(lane, lanes)],
                        wo_sems.at[at],
                    )
                )
    bases = []
    for s in range(slots):
        spot = pl.ds(pl.multiple_of(planes_ref[s] * cols, 128), cols)
        bases.append(pltpu.make_async_copy(lat_ref.at[:, spot], done_ref.at[s], base_sems.at[s]))
    blocks = tokens // 128
    key = lax.broadcasted_iota(jnp.int32, (128, 256), 0)
    query = lax.broadcasted_iota(jnp.int32, (128, 256), 1) % 128
    for b in range(blocks):
        first = (key < WIN_TOK) & (query < WIN_TOK) & (key < lens_ref[2 * b])
        second = (key >= WIN_TOK) & (query >= WIN_TOK) & (key - WIN_TOK < lens_ref[2 * b + 1])
        mask_ref[b] = jnp.where(first | second, 1.0, 0.0).astype(F32)

    for m in range(count):
        if m < 2:
            wait_columns(m, pieces[8 * last :], spots[8 * last :], rows, w_ref, w_sems)
        which = planes_ref[last] * count + m
        for c in (copies + bases)[m::count]:
            c.start()
        out = project_chunk(m, which, parts, w_ref, n_ref)
        for kind, to in ((0, q_ref), (1, k_ref), (2, v_ref)):

            @pl.when(which // parts == kind)
            def _():
                to[which % parts] = out.T if kind == 1 else out

    ones = jnp.ones((16, 128), BF)
    blank = jnp.zeros((HEAD_DIM, 128), BF)
    pairs = chunk // 128

    @pl.loop(0, parts)
    def _(part):
        for kind in range(3):
            which = parts * kind + part

            @pl.when(planes_ref[which // count] != last)
            def _():
                pltpu.make_async_copy(p0.at[0], q_ref.at[0], part_sems.at[which]).wait()

        @pl.loop(0, pairs)
        def _(i):
            at = pl.ds(pl.multiple_of(i * 128, 128), 128)
            out_at = pl.ds(pl.multiple_of(part * chunk + i * 128, 128), 128)
            for b in range(blocks):
                tok = pl.ds(b * 128, 128)
                q = q_ref[part, at, tok]
                k = k_ref[part, tok, at]
                q0 = jnp.concatenate([q[:HEAD_DIM], blank], axis=0)
                q1 = jnp.concatenate([blank, q[HEAD_DIM:]], axis=0)
                scores = jnp.dot(k, jnp.concatenate([q0, q1], axis=1), preferred_element_type=F32)
                e_ref[b] = (jnp.exp(scores) * mask_ref[b]).astype(BF)
            for b in range(blocks):
                tok = pl.ds(b * 128, 128)
                v = v_ref[part, at, tok]
                got = jnp.dot(
                    jnp.concatenate([v, ones], axis=0), e_ref[b], preferred_element_type=F32
                )
                token = lax.broadcasted_iota(jnp.int32, (1, 256), 1) % 128
                first = (token < WIN_TOK) & (token < lens_ref[2 * b])
                second = (token >= WIN_TOK) & (token - WIN_TOK < lens_ref[2 * b + 1])
                keep = (first | second) & (b < live_ref[0])
                share = jnp.where(keep, 1.0 / got[128:129, :], 0.0)
                o0 = got[:HEAD_DIM, :128] * share[:, :128]
                o1 = got[HEAD_DIM:128, 128:] * share[:, 128:]
                att_ref[tok, out_at] = jnp.concatenate([o0, o1], axis=0).astype(BF).T

    outs = []
    for s in range(slots):
        for c in copies[8 * s : 8 * s + 8] + [bases[s]]:
            c.wait()
        spot = pl.ds(pl.multiple_of(planes_ref[s] * cols, 128), cols)
        for h in range(2):
            part = pl.ds(h * tokens // 2, tokens // 2)
            update = lax.dot_general(
                att_ref[part, :], wo_ref[s], (((1,), (1,)), ((), ())), preferred_element_type=F32
            )
            done_ref[s, part, :] = (done_ref[s, part, :].astype(F32) + update).astype(BF)
            outs.append(
                pltpu.make_async_copy(
                    done_ref.at[s, part], out_ref.at[part, spot], out_sems.at[2 * s + h]
                )
            )
            outs[-1].start()
    for c in outs:
        c.wait()


def finish(place, planes, window_len, live_blocks, normed, latents, parts, pieces, rows):
    count, chunk, tokens = parts[0][0].shape
    width = normed.shape[0]
    slots = len(pieces) // 8
    return pl.pallas_call(
        functools.partial(finish_kernel, [spot for _, spot in pieces], rows),
        out_shape=jax.ShapeDtypeStruct((tokens, width), BF),
        in_specs=[sspec()] * 4 + [vspec()] + [hspec()] * (7 + len(pieces)),
        out_specs=hspec(),
        scratch_shapes=[
            pltpu.VMEM((4 * rows, width), BF),
            pltpu.VMEM((4, chunk, tokens), BF),
            pltpu.VMEM((4, tokens, chunk), BF),
            pltpu.VMEM((4, chunk, tokens), BF),
            pltpu.VMEM((tokens // 128, 128, 256), F32),
            pltpu.VMEM((tokens // 128, 128, 256), BF),
            pltpu.VMEM((tokens, width), BF),
            pltpu.VMEM((slots, width // slots, width), BF),
            pltpu.VMEM((slots, tokens, width // slots), BF),
            pltpu.SemaphoreType.DMA((8,)),
            pltpu.SemaphoreType.DMA((4 * count,)),
            pltpu.SemaphoreType.DMA((len(pieces),)),
            pltpu.SemaphoreType.DMA((2 * slots,)),
            pltpu.SemaphoreType.DMA((slots,)),
        ],
        compiler_params=params(44),
        cost_estimate=cost(6 * width * width * tokens, 8 * width * tokens),
        name="finish",
    )(
        place,
        planes,
        window_len,
        live_blocks,
        normed,
        far(latents),
        *[far(a) for pair in parts for a in pair],
        *[far(value) for value, _ in pieces[:-8]],
        *[value for value, _ in pieces[-8:]],
    )


def local(tile_count, latents, window_index, window_len, live_blocks, norm_gain, w_qkv, w_out):
    blocks, rows, width = latents.shape

    def along(axis, pairs):
        def move(value, name):
            with jax.named_scope(name):
                return lax.ppermute(value, axis, pairs)

        return move

    def across(bit):
        return along("tile", [(i, i ^ bit) for i in range(tile_count)])

    core, ys, z1, z2 = across(1), across(2), across(4), across(8)
    xs = along("group", [(0, 1), (1, 0)])
    xy = along(
        ("tile", "group"),
        [(2 * i + g, 2 * (i ^ 2) + 1 - g) for i in range(tile_count) for g in range(2)],
    )
    t = lax.axis_index("tile")
    x = lax.axis_index("group")
    z = t // 4
    place = jnp.stack([x, t // 2 % 2, t % 2]).astype(jnp.int32)
    planes = jnp.stack([z, z ^ 1, z ^ 2, z ^ 3]).astype(jnp.int32)

    nq = w_qkv.shape[1]

    def sync(*values):
        return lax.optimization_barrier(values)

    def share(**values):
        shared = []
        for name, value in values.items():
            if shared:
                value = sync(value, shared[-1])[0]
            shared.append(core(value, f"core_{name}"))
        return shared

    def slot(index, *values):
        return [(value, index if value.ndim == 3 else None) for value in values]

    u0 = jnp.concatenate([w_qkv.T, w_out.T], axis=0)
    u1, d0, x0, y0, u2 = z1(u0, "u1"), xy(u0, "d0"), xs(u0, "x0"), ys(u0, "y0"), z2(u0, "u2")
    normed = normed_columns(latents, window_index, norm_gain)
    cu0 = core(u0, "core_u0")
    u1, d0, x0, y0, u2, normed, cu0 = sync(u1, d0, x0, y0, u2, normed, cu0)
    u12 = jnp.stack([u1, u2])
    x2, y12, u3, d1 = xs(u2, "x2"), ys(u12, "y12"), z1(u2, "u3"), z1(d0, "d1")
    cx0, cy0 = core(x0, "core_x0"), core(y0, "core_y0")
    x2, y12, u3, d1, cx0, cy0, u12 = sync(x2, y12, u3, d1, cx0, cy0, u12)
    x1, d2 = xs(u1, "x1"), ys(x2, "d2")
    cd0, cx2, cy12, cu12 = (
        core(value, name) for value, name in ((d0, "core_d0"), (x2, "core_x2"), (y12, "core_y12"), (u12, "core_u12"))
    )
    s0 = slot(0, u0, x0, y0, d0, cu0, cx0, cy0, cd0)
    p0 = project(place, planes[0:1], normed, s0, nq)
    x1, d2, cx2, cy12, cu12, d1, u3, p0 = sync(x1, d2, cx2, cy12, cu12, d1, u3, p0)
    x3, y3, d3 = xs(u3, "x3"), ys(u3, "y3"), z1(d2, "d3")
    cd2, cx1, cd1 = core(d2, "core_d2"), core(x1, "core_x1"), core(d1, "core_d1")
    cu3 = core(u3, "core_u3")
    s2 = slot(1, u12, x2, y12, d2, cu12, cx2, cy12, cd2)
    p2 = project(place, planes[2:3], normed, s2, nq)
    s1 = slot(0, u12, x1, y12, d1, cu12, cx1, cy12, cd1)
    p1 = project(place, planes[1:2], normed, s1, nq)
    x3, y3, d3, u3, cu3, p2, p1 = sync(x3, y3, d3, u3, cu3, p2, p1)
    cx3, cy3, cd3 = core(x3, "core_x3"), core(y3, "core_y3"), core(d3, "core_d3")
    s3 = slot(0, u3, x3, y3, d3, cu3, cx3, cy3, cd3)
    flat = latents.reshape(blocks * rows, width)
    so = s0 + s1 + s2 + s3
    out = finish(place, planes, window_len, live_blocks, normed, flat, (p0, p1, p2), so, nq)
    return out.reshape(latents.shape)


def solution(mesh):
    in_specs = (
        P(("tile", "group"), None, None),
        P(("tile", "group")),
        P(("tile", "group")),
        P(("tile", "group")),
        P(),
        P("group", "tile"),
        P("group", "tile"),
    )
    out_specs = P(("tile", "group"), None, None)
    planes, chips, cores = 4, 2, 2
    if mesh.shape["group"] == 2 and mesh.shape["tile"] == planes * chips * cores:
        body = functools.partial(local, mesh.shape["tile"])
    else:
        body = general
    return jax.shard_map(body, mesh=mesh, in_specs=in_specs, out_specs=out_specs, check_vma=False)
```

```python
import functools
import math

import jax
import jax.numpy as jnp
from jax import lax
from jax.experimental import pallas as pl
from jax.experimental.pallas import tpu as pltpu
from jax.sharding import PartitionSpec as P

HEAD_DIM = 64
WIN_SIDE = 8
WIN_COLS = 60
WIN_TOK = 64
EPS = 1e-06
BF = jnp.bfloat16
F32 = jnp.float32


def position_table(window_ids, width):
    token_ids = jnp.arange(WIN_TOK, dtype=jnp.int32)
    row_pos = window_ids[:, None] // WIN_COLS * WIN_SIDE + token_ids[None, :] // WIN_SIDE
    col_pos = window_ids[:, None] % WIN_COLS * WIN_SIDE + token_ids[None, :] % WIN_SIDE
    quarter = width // 4
    frequency = jnp.exp(jnp.arange(quarter, dtype=F32) * (-math.log(10000.0) / quarter))
    row_angle = row_pos.astype(F32)[:, :, None] * frequency
    col_angle = col_pos.astype(F32)[:, :, None] * frequency
    return jnp.concatenate(
        [jnp.sin(row_angle), jnp.cos(row_angle), jnp.sin(col_angle), jnp.cos(col_angle)], axis=-1
    )


def head_norm(values):
    return (values * lax.rsqrt(jnp.mean(values * values, axis=-1, keepdims=True) + EPS)).astype(BF)


def window_layer(blocks_in, window_ids, window_lens, norm_gain, w_qkv, w_out):
    width = blocks_in.shape[-1]
    count = window_ids.shape[0]
    heads = width // HEAD_DIM
    stream = blocks_in.reshape(count, WIN_TOK, width).astype(F32) + position_table(window_ids, width)
    scale = lax.rsqrt(jnp.mean(stream * stream, axis=-1, keepdims=True) + EPS)
    normed = (stream * scale * norm_gain).astype(BF).reshape(count * WIN_TOK, width)
    full_rows = lax.all_gather(w_qkv, "group", axis=0, tiled=True)
    projected = jnp.dot(
        normed,
        lax.all_gather(full_rows, "tile", axis=1, tiled=True),
        preferred_element_type=F32,
    ).reshape(count, WIN_TOK, 3, heads, HEAD_DIM)
    queries = head_norm(projected[:, :, 0])
    keys = head_norm(projected[:, :, 1])
    values = projected[:, :, 2].astype(BF)
    scores = jnp.einsum("wqhd,wkhd->whqk", queries, keys, preferred_element_type=F32) * HEAD_DIM**-0.5
    key_mask = jnp.arange(WIN_TOK, dtype=jnp.int32)[None, :] < window_lens[:, None]
    weights = jnp.exp(scores) * key_mask[:, None, None, :].astype(F32)
    probs = (weights / jnp.sum(weights, axis=-1, keepdims=True)).astype(BF)
    attended = jnp.einsum("whqk,wkhd->wqhd", probs, values, preferred_element_type=F32)
    attended = attended.astype(BF).reshape(count * WIN_TOK, width)
    out_rows = lax.all_gather(w_out, "group", axis=0, tiled=True)
    update = jnp.dot(
        attended, lax.all_gather(out_rows, "tile", axis=1, tiled=True), preferred_element_type=F32
    )
    base = blocks_in.reshape(count * WIN_TOK, width).astype(F32)
    token_live = key_mask.reshape(count * WIN_TOK)[:, None]
    return jnp.where(token_live, base + update, base).astype(BF).reshape(blocks_in.shape)


def general(latents, window_index, window_len, live_blocks, norm_gain, w_qkv, w_out):
    slot_ids = jnp.arange(latents.shape[0], dtype=jnp.int32)
    live_mask = (slot_ids < live_blocks[0])[:, None, None]
    finished = window_layer(latents, window_index, window_len, norm_gain, w_qkv, w_out)
    return jnp.where(live_mask, finished, latents)


def hspec():
    return pl.BlockSpec(memory_space=pltpu.HBM)


def vspec():
    return pl.BlockSpec(memory_space=pltpu.VMEM)


def sspec():
    return pl.BlockSpec(memory_space=pltpu.SMEM)


def params(mib):
    return pltpu.CompilerParams(vmem_limit_bytes=mib * 1024 * 1024)


def far(value):
    return pltpu.with_memory_space_constraint(value, pltpu.HBM)


def cost(flops, moved):
    return pl.CostEstimate(flops=flops, bytes_accessed=moved, transcendentals=0)


def norm_kernel(ids_ref, lat_ref, gain_ref, freq_ref, out_ref, pos_ref):
    blocks, _, width = lat_ref.shape
    quarter = width // 4
    freq = freq_ref[...]
    step = lax.broadcasted_iota(jnp.int32, (WIN_SIDE, quarter), 0).astype(F32) * freq
    sin_step, cos_step = jnp.sin(step), jnp.cos(step)
    gain = gain_ref[...]

    @pl.loop(0, blocks)
    def _(b):
        for w in range(2):
            place = ids_ref[2 * b + w]
            row = (place // WIN_COLS * WIN_SIDE).astype(F32)
            col = (place % WIN_COLS * WIN_SIDE).astype(F32)
            for at, start in ((0, row), (2 * quarter, col)):
                base = start * freq
                sin_base, cos_base = jnp.sin(base), jnp.cos(base)
                sines = sin_base * cos_step + cos_base * sin_step
                cosines = cos_base * cos_step - sin_base * sin_step
                for more, table in ((0, sines), (quarter, cosines)):
                    where = pl.ds(at + more, quarter)
                    for i in range(WIN_SIDE):
                        rows = pl.ds(w * WIN_TOK + i * WIN_SIDE, WIN_SIDE)
                        if at == 0:
                            pos_ref[rows, where] = jnp.broadcast_to(
                                table[i : i + 1, :], (WIN_SIDE, quarter)
                            )
                        else:
                            pos_ref[rows, where] = table
        stream = lat_ref[b].astype(F32) + pos_ref[...]
        scale = lax.rsqrt(jnp.mean(stream * stream, axis=-1, keepdims=True) + EPS)
        normed = (stream * scale * gain).astype(BF)
        out_ref[:, pl.ds(pl.multiple_of(b * 128, 128), 128)] = normed.T


def normed_columns(latents, window_index, norm_gain):
    blocks, rows, width = latents.shape
    quarter = width // 4
    freq = jnp.exp(jnp.arange(quarter, dtype=F32) * (-math.log(10000.0) / quarter))
    return pl.pallas_call(
        norm_kernel,
        out_shape=jax.ShapeDtypeStruct((width, blocks * rows), BF),
        in_specs=[sspec(), vspec(), vspec(), vspec()],
        out_specs=vspec(),
        scratch_shapes=[pltpu.VMEM((rows, width), F32)],
        compiler_params=params(24),
        cost_estimate=cost(40 * blocks * rows * width, 4 * blocks * rows * width),
        name="norm",
    )(window_index, latents, norm_gain.reshape(1, width), freq.reshape(1, quarter))


def places(x, y):
    return ((x, y), (1 - x, y), (x, 1 - y), (1 - x, 1 - y))


def piece_rows(ref, spot, start, rows):
    part = pl.ds(start, rows)
    return ref.at[part, :] if spot is None else ref.at[spot, part, :]


def start_columns(at_ref, pieces, spots, rows, w_ref, sems):
    x, y, core = at_ref[0], at_ref[1], at_ref[2]
    lanes = w_ref.shape[1] // 2
    for i, (px, py) in enumerate(places(x, y)):
        for owner, c in ((0, core), (1, 1 - core)):
            row = pl.multiple_of((2 * py + c) * rows, 16)
            lane = pl.multiple_of(px * lanes, 128)
            pltpu.make_async_copy(
                piece_rows(pieces[4 * owner + i], spots[4 * owner + i], 0, rows),
                w_ref.at[pl.ds(row, rows), pl.ds(lane, lanes)],
                sems.at[py * 4 + 2 * owner + i % 2],
            ).start()


def wait_columns(half, pieces, spots, rows, w_ref, sems):
    lanes = w_ref.shape[1] // 2
    for i in range(4):
        pltpu.make_async_copy(
            piece_rows(pieces[0], spots[0], 0, rows),
            w_ref.at[pl.ds(0, rows), pl.ds(0, lanes)],
            sems.at[4 * half + i],
        ).wait()


def project_chunk(m, which, parts, w_ref, n_ref):
    tokens = n_ref.shape[1]
    chunk = n_ref.shape[0] // parts
    got = jnp.dot(w_ref[m * chunk : (m + 1) * chunk, :], n_ref[...], preferred_element_type=F32)
    got = got.reshape(chunk // HEAD_DIM, HEAD_DIM, tokens)
    ms = jnp.mean(got * got, axis=1, keepdims=True)
    scale = jnp.where(which < 2 * parts, lax.rsqrt(ms + EPS), 1.0)
    scale = jnp.where(which < parts, scale * HEAD_DIM**-0.5, scale)
    return (got * scale).astype(BF).reshape(chunk, tokens)


def project_kernel(spots, parts, at_ref, plane_ref, n_ref, *rest):
    pieces, (p_ref, k_ref, w_ref, rows_ref, cols_ref, sems, out_sems) = rest[:8], rest[8:]
    rows = w_ref.shape[0] // 4
    start_columns(at_ref, pieces, spots, rows, w_ref, sems)
    count = p_ref.shape[0]
    for m in range(count):
        if m < 2:
            wait_columns(m, pieces, spots, rows, w_ref, sems)
        which = plane_ref[0] * count + m
        out = project_chunk(m, which, parts, w_ref, n_ref)
        rows_ref[m] = out
        cols_ref[m] = out.T
        is_key = (which >= parts) & (which < 2 * parts)

        @pl.when(is_key)
        def _():
            pltpu.make_async_copy(cols_ref.at[m], k_ref.at[m], out_sems.at[m]).start()

        @pl.when(jnp.logical_not(is_key))
        def _():
            pltpu.make_async_copy(rows_ref.at[m], p_ref.at[m], out_sems.at[m]).start()

    for m in range(count):
        pltpu.make_async_copy(rows_ref.at[m], p_ref.at[m], out_sems.at[m]).wait()


def project(place, plane, normed, pieces, rows):
    width, tokens = normed.shape
    parts = 4
    chunk = width // parts
    count = 4 * rows // chunk
    return pl.pallas_call(
        functools.partial(project_kernel, [spot for _, spot in pieces], parts),
        out_shape=(
            pltpu.HBM((count, chunk, tokens), BF),
            pltpu.HBM((count, tokens, chunk), BF),
        ),
        in_specs=[sspec(), sspec(), vspec()] + [hspec()] * 8,
        out_specs=(hspec(), hspec()),
        scratch_shapes=[
            pltpu.VMEM((4 * rows, width), BF),
            pltpu.VMEM((count, chunk, tokens), BF),
            pltpu.VMEM((count, tokens, chunk), BF),
            pltpu.SemaphoreType.DMA((8,)),
            pltpu.SemaphoreType.DMA((count,)),
        ],
        compiler_params=params(24),
        cost_estimate=cost(8 * rows * width * tokens, 2 * (4 * rows + tokens) * width),
        name="project",
    )(place, plane, normed, *[far(value) for value, _ in pieces])


def finish_kernel(
    spots, rows, at_ref, planes_ref, lens_ref, live_ref, n_ref, lat_ref, p0, k0, p1, k1, p2, k2, *rest
):
    pieces, rest = rest[:-15], rest[-15:]
    out_ref, w_ref, q_ref, k_ref, v_ref, mask_ref, e_ref, att_ref, wo_ref, done_ref = rest[:10]
    w_sems, part_sems, wo_sems, out_sems, base_sems = rest[10:]
    parts, chunk, tokens = q_ref.shape
    count = p0.shape[0]
    slots = wo_ref.shape[0]
    last = slots - 1
    x, y, core = at_ref[0], at_ref[1], at_ref[2]

    start_columns(at_ref, pieces[8 * last :], spots[8 * last :], rows, w_ref, w_sems)
    for part in range(parts):
        for kind, to in ((0, q_ref), (1, k_ref), (2, v_ref)):
            which = parts * kind + part
            for s, (p, k) in enumerate(((p0, k0), (p1, k1), (p2, k2))):

                @pl.when(planes_ref[which // count] == s)
                def _():
                    src = (k if kind == 1 else p).at[which % count]
                    pltpu.make_async_copy(src, to.at[part], part_sems.at[which]).start()

    cols, lanes = wo_ref.shape[1], wo_ref.shape[2] // 2
    ours = cols // 4
    skip = pieces[0].shape[-2] - ours
    copies = []
    for s in range(slots):
        for owner, c in ((0, core), (1, 1 - core)):
            for i, (px, py) in enumerate(places(x, y)):
                at = 8 * s + 4 * owner + i
                row = pl.multiple_of((2 * py + c) * ours, 16)
                lane = pl.multiple_of(px * lanes, 128)
                copies.append(
                    pltpu.make_async_copy(
                        piece_rows(pieces[at], spots[at], skip, ours),
                        wo_ref.at[s, pl.ds(row, ours), pl.ds(lane, lanes)],
                        wo_sems.at[at],
                    )
                )
    bases = []
    for s in range(slots):
        spot = pl.ds(pl.multiple_of(planes_ref[s] * cols, 128), cols)
        bases.append(pltpu.make_async_copy(lat_ref.at[:, spot], done_ref.at[s], base_sems.at[s]))
    blocks = tokens // 128
    key = lax.broadcasted_iota(jnp.int32, (128, 256), 0)
    query = lax.broadcasted_iota(jnp.int32, (128, 256), 1) % 128
    for b in range(blocks):
        first = (key < WIN_TOK) & (query < WIN_TOK) & (key < lens_ref[2 * b])
        second = (key >= WIN_TOK) & (query >= WIN_TOK) & (key - WIN_TOK < lens_ref[2 * b + 1])
        mask_ref[b] = jnp.where(first | second, 1.0, 0.0).astype(F32)

    for m in range(count):
        if m < 2:
            wait_columns(m, pieces[8 * last :], spots[8 * last :], rows, w_ref, w_sems)
        which = planes_ref[last] * count + m
        for c in (copies + bases)[m::count]:
            c.start()
        out = project_chunk(m, which, parts, w_ref, n_ref)
        for kind, to in ((0, q_ref), (1, k_ref), (2, v_ref)):

            @pl.when(which // parts == kind)
            def _():
                to[which % parts] = out.T if kind == 1 else out

    ones = jnp.ones((16, 128), BF)
    blank = jnp.zeros((HEAD_DIM, 128), BF)
    pairs = chunk // 128

    for which in range(3 * parts):

        @pl.when(planes_ref[which // count] != last)
        def _():
            pltpu.make_async_copy(p0.at[0], q_ref.at[0], part_sems.at[which]).wait()

    def weigh(pair):
        part = pair // pairs
        at = pl.ds(pl.multiple_of(pair % pairs * 128, 128), 128)
        for b in range(blocks):
            tok = pl.ds(b * 128, 128)
            q = q_ref[part, at, tok]
            k = k_ref[part, tok, at]
            q0 = jnp.concatenate([q[:HEAD_DIM], blank], axis=0)
            q1 = jnp.concatenate([blank, q[HEAD_DIM:]], axis=0)
            scores = jnp.dot(k, jnp.concatenate([q0, q1], axis=1), preferred_element_type=F32)
            e_ref[pair % 2, b] = (jnp.exp(scores) * mask_ref[b]).astype(BF)

    def gather(pair):
        part = pair // pairs
        at = pl.ds(pl.multiple_of(pair % pairs * 128, 128), 128)
        out_at = pl.ds(pl.multiple_of(pair * 128, 128), 128)
        for b in range(blocks):
            tok = pl.ds(b * 128, 128)
            v = v_ref[part, at, tok]
            got = jnp.dot(
                jnp.concatenate([v, ones], axis=0), e_ref[pair % 2, b], preferred_element_type=F32
            )
            token = lax.broadcasted_iota(jnp.int32, (1, 256), 1) % 128
            first = (token < WIN_TOK) & (token < lens_ref[2 * b])
            second = (token >= WIN_TOK) & (token - WIN_TOK < lens_ref[2 * b + 1])
            keep = (first | second) & (b < live_ref[0])
            share = jnp.where(keep, 1.0 / got[128:129, :], 0.0)
            o0 = got[:HEAD_DIM, :128] * share[:, :128]
            o1 = got[HEAD_DIM:128, 128:] * share[:, 128:]
            att_ref[tok, out_at] = jnp.concatenate([o0, o1], axis=0).astype(BF).T

    weigh(0)

    @pl.loop(0, parts * pairs)
    def _(pair):
        gather(pair)
        weigh(jnp.minimum(pair + 1, parts * pairs - 1))

    outs = []
    for s in range(slots):
        for c in copies[8 * s : 8 * s + 8] + [bases[s]]:
            c.wait()
        spot = pl.ds(pl.multiple_of(planes_ref[s] * cols, 128), cols)
        for h in range(2):
            part = pl.ds(h * tokens // 2, tokens // 2)
            update = lax.dot_general(
                att_ref[part, :], wo_ref[s], (((1,), (1,)), ((), ())), preferred_element_type=F32
            )
            done_ref[s, part, :] = (done_ref[s, part, :].astype(F32) + update).astype(BF)
            outs.append(
                pltpu.make_async_copy(
                    done_ref.at[s, part], out_ref.at[part, spot], out_sems.at[2 * s + h]
                )
            )
            outs[-1].start()
    for c in outs:
        c.wait()


def finish(place, planes, window_len, live_blocks, normed, latents, parts, pieces, rows):
    count, chunk, tokens = parts[0][0].shape
    width = normed.shape[0]
    slots = len(pieces) // 8
    return pl.pallas_call(
        functools.partial(finish_kernel, [spot for _, spot in pieces], rows),
        out_shape=jax.ShapeDtypeStruct((tokens, width), BF),
        in_specs=[sspec()] * 4 + [vspec()] + [hspec()] * (7 + len(pieces)),
        out_specs=hspec(),
        scratch_shapes=[
            pltpu.VMEM((4 * rows, width), BF),
            pltpu.VMEM((4, chunk, tokens), BF),
            pltpu.VMEM((4, tokens, chunk), BF),
            pltpu.VMEM((4, chunk, tokens), BF),
            pltpu.VMEM((tokens // 128, 128, 256), F32),
            pltpu.VMEM((2, tokens // 128, 128, 256), BF),
            pltpu.VMEM((tokens, width), BF),
            pltpu.VMEM((slots, width // slots, width), BF),
            pltpu.VMEM((slots, tokens, width // slots), BF),
            pltpu.SemaphoreType.DMA((8,)),
            pltpu.SemaphoreType.DMA((4 * count,)),
            pltpu.SemaphoreType.DMA((len(pieces),)),
            pltpu.SemaphoreType.DMA((2 * slots,)),
            pltpu.SemaphoreType.DMA((slots,)),
        ],
        compiler_params=params(44),
        cost_estimate=cost(6 * width * width * tokens, 8 * width * tokens),
        name="finish",
    )(
        place,
        planes,
        window_len,
        live_blocks,
        normed,
        far(latents),
        *[far(a) for pair in parts for a in pair],
        *[far(value) for value, _ in pieces[:-8]],
        *[value for value, _ in pieces[-8:]],
    )


def local(tile_count, latents, window_index, window_len, live_blocks, norm_gain, w_qkv, w_out):
    blocks, rows, width = latents.shape

    def along(axis, pairs):
        def move(value, name):
            with jax.named_scope(name):
                return lax.ppermute(value, axis, pairs)

        return move

    def across(bit):
        return along("tile", [(i, i ^ bit) for i in range(tile_count)])

    core, ys, z1, z2 = across(1), across(2), across(4), across(8)
    xs = along("group", [(0, 1), (1, 0)])
    xy = along(
        ("tile", "group"),
        [(2 * i + g, 2 * (i ^ 2) + 1 - g) for i in range(tile_count) for g in range(2)],
    )
    t = lax.axis_index("tile")
    x = lax.axis_index("group")
    z = t // 4
    place = jnp.stack([x, t // 2 % 2, t % 2]).astype(jnp.int32)
    planes = jnp.stack([z, z ^ 1, z ^ 2, z ^ 3]).astype(jnp.int32)

    nq = w_qkv.shape[1]

    def sync(*values):
        return lax.optimization_barrier(values)

    def share(**values):
        shared = []
        for name, value in values.items():
            if shared:
                value = sync(value, shared[-1])[0]
            shared.append(core(value, f"core_{name}"))
        return shared

    def slot(index, *values):
        return [(value, index if value.ndim == 3 else None) for value in values]

    u0 = jnp.concatenate([w_qkv.T, w_out.T], axis=0)
    u1, d0, x0, y0, u2 = z1(u0, "u1"), xy(u0, "d0"), xs(u0, "x0"), ys(u0, "y0"), z2(u0, "u2")
    normed = normed_columns(latents, window_index, norm_gain)
    cu0 = core(u0, "core_u0")
    u1, d0, x0, y0, u2, normed, cu0 = sync(u1, d0, x0, y0, u2, normed, cu0)
    u12 = jnp.stack([u1, u2])
    x2, y12, u3, d1 = xs(u2, "x2"), ys(u12, "y12"), z1(u2, "u3"), z1(d0, "d1")
    cx0, cy0 = core(x0, "core_x0"), core(y0, "core_y0")
    x2, y12, u3, d1, cx0, cy0, u12 = sync(x2, y12, u3, d1, cx0, cy0, u12)
    x1, d2 = xs(u1, "x1"), ys(x2, "d2")
    cd0, cx2, cy12, cu12 = (
        core(value, name) for value, name in ((d0, "core_d0"), (x2, "core_x2"), (y12, "core_y12"), (u12, "core_u12"))
    )
    s0 = slot(0, u0, x0, y0, d0, cu0, cx0, cy0, cd0)
    p0 = project(place, planes[0:1], normed, s0, nq)
    x1, d2, cx2, cy12, cu12, d1, u3, p0 = sync(x1, d2, cx2, cy12, cu12, d1, u3, p0)
    x3, y3, d3 = xs(u3, "x3"), ys(u3, "y3"), z1(d2, "d3")
    cd2, cx1, cd1 = core(d2, "core_d2"), core(x1, "core_x1"), core(d1, "core_d1")
    cu3 = core(u3, "core_u3")
    s2 = slot(1, u12, x2, y12, d2, cu12, cx2, cy12, cd2)
    p2 = project(place, planes[2:3], normed, s2, nq)
    s1 = slot(0, u12, x1, y12, d1, cu12, cx1, cy12, cd1)
    p1 = project(place, planes[1:2], normed, s1, nq)
    x3, y3, d3, u3, cu3, p2, p1 = sync(x3, y3, d3, u3, cu3, p2, p1)
    cx3, cy3, cd3 = core(x3, "core_x3"), core(y3, "core_y3"), core(d3, "core_d3")
    s3 = slot(0, u3, x3, y3, d3, cu3, cx3, cy3, cd3)
    flat = latents.reshape(blocks * rows, width)
    so = s0 + s1 + s2 + s3
    out = finish(place, planes, window_len, live_blocks, normed, flat, (p0, p1, p2), so, nq)
    return out.reshape(latents.shape)


def solution(mesh):
    in_specs = (
        P(("tile", "group"), None, None),
        P(("tile", "group")),
        P(("tile", "group")),
        P(("tile", "group")),
        P(),
        P("group", "tile"),
        P("group", "tile"),
    )
    out_specs = P(("tile", "group"), None, None)
    planes, chips, cores = 4, 2, 2
    if mesh.shape["group"] == 2 and mesh.shape["tile"] == planes * chips * cores:
        body = functools.partial(local, mesh.shape["tile"])
    else:
        body = general
    return jax.shard_map(body, mesh=mesh, in_specs=in_specs, out_specs=out_specs, check_vma=False)
```

```python
import functools
import math

import jax
import jax.numpy as jnp
from jax import lax
from jax.experimental import pallas as pl
from jax.experimental.pallas import tpu as pltpu
from jax.sharding import PartitionSpec as P

HEAD_DIM = 64
WIN_SIDE = 8
WIN_COLS = 60
WIN_TOK = 64
EPS = 1e-06
BF = jnp.bfloat16
F32 = jnp.float32


def position_table(window_ids, width):
    token_ids = jnp.arange(WIN_TOK, dtype=jnp.int32)
    row_pos = window_ids[:, None] // WIN_COLS * WIN_SIDE + token_ids[None, :] // WIN_SIDE
    col_pos = window_ids[:, None] % WIN_COLS * WIN_SIDE + token_ids[None, :] % WIN_SIDE
    quarter = width // 4
    frequency = jnp.exp(jnp.arange(quarter, dtype=F32) * (-math.log(10000.0) / quarter))
    row_angle = row_pos.astype(F32)[:, :, None] * frequency
    col_angle = col_pos.astype(F32)[:, :, None] * frequency
    return jnp.concatenate(
        [jnp.sin(row_angle), jnp.cos(row_angle), jnp.sin(col_angle), jnp.cos(col_angle)], axis=-1
    )


def head_norm(values):
    return (values * lax.rsqrt(jnp.mean(values * values, axis=-1, keepdims=True) + EPS)).astype(BF)


def window_layer(blocks_in, window_ids, window_lens, norm_gain, w_qkv, w_out):
    width = blocks_in.shape[-1]
    count = window_ids.shape[0]
    heads = width // HEAD_DIM
    stream = blocks_in.reshape(count, WIN_TOK, width).astype(F32) + position_table(window_ids, width)
    scale = lax.rsqrt(jnp.mean(stream * stream, axis=-1, keepdims=True) + EPS)
    normed = (stream * scale * norm_gain).astype(BF).reshape(count * WIN_TOK, width)
    full_rows = lax.all_gather(w_qkv, "group", axis=0, tiled=True)
    projected = jnp.dot(
        normed,
        lax.all_gather(full_rows, "tile", axis=1, tiled=True),
        preferred_element_type=F32,
    ).reshape(count, WIN_TOK, 3, heads, HEAD_DIM)
    queries = head_norm(projected[:, :, 0])
    keys = head_norm(projected[:, :, 1])
    values = projected[:, :, 2].astype(BF)
    scores = jnp.einsum("wqhd,wkhd->whqk", queries, keys, preferred_element_type=F32) * HEAD_DIM**-0.5
    key_mask = jnp.arange(WIN_TOK, dtype=jnp.int32)[None, :] < window_lens[:, None]
    weights = jnp.exp(scores) * key_mask[:, None, None, :].astype(F32)
    probs = (weights / jnp.sum(weights, axis=-1, keepdims=True)).astype(BF)
    attended = jnp.einsum("whqk,wkhd->wqhd", probs, values, preferred_element_type=F32)
    attended = attended.astype(BF).reshape(count * WIN_TOK, width)
    out_rows = lax.all_gather(w_out, "group", axis=0, tiled=True)
    update = jnp.dot(
        attended, lax.all_gather(out_rows, "tile", axis=1, tiled=True), preferred_element_type=F32
    )
    base = blocks_in.reshape(count * WIN_TOK, width).astype(F32)
    token_live = key_mask.reshape(count * WIN_TOK)[:, None]
    return jnp.where(token_live, base + update, base).astype(BF).reshape(blocks_in.shape)


def general(latents, window_index, window_len, live_blocks, norm_gain, w_qkv, w_out):
    slot_ids = jnp.arange(latents.shape[0], dtype=jnp.int32)
    live_mask = (slot_ids < live_blocks[0])[:, None, None]
    finished = window_layer(latents, window_index, window_len, norm_gain, w_qkv, w_out)
    return jnp.where(live_mask, finished, latents)


def hspec():
    return pl.BlockSpec(memory_space=pltpu.HBM)


def vspec():
    return pl.BlockSpec(memory_space=pltpu.VMEM)


def sspec():
    return pl.BlockSpec(memory_space=pltpu.SMEM)


def params(mib):
    return pltpu.CompilerParams(vmem_limit_bytes=mib * 1024 * 1024)


def far(value):
    return pltpu.with_memory_space_constraint(value, pltpu.HBM)


def cost(flops, moved):
    return pl.CostEstimate(flops=flops, bytes_accessed=moved, transcendentals=0)


def norm_kernel(ids_ref, lat_ref, gain_ref, freq_ref, out_ref, pos_ref):
    blocks, _, width = lat_ref.shape
    quarter = width // 4
    freq = freq_ref[...]
    step = lax.broadcasted_iota(jnp.int32, (WIN_SIDE, quarter), 0).astype(F32) * freq
    sin_step, cos_step = jnp.sin(step), jnp.cos(step)
    gain = gain_ref[...]

    @pl.loop(0, blocks)
    def _(b):
        for w in range(2):
            place = ids_ref[2 * b + w]
            row = (place // WIN_COLS * WIN_SIDE).astype(F32)
            col = (place % WIN_COLS * WIN_SIDE).astype(F32)
            for at, start in ((0, row), (2 * quarter, col)):
                base = start * freq
                sin_base, cos_base = jnp.sin(base), jnp.cos(base)
                sines = sin_base * cos_step + cos_base * sin_step
                cosines = cos_base * cos_step - sin_base * sin_step
                for more, table in ((0, sines), (quarter, cosines)):
                    where = pl.ds(at + more, quarter)
                    for i in range(WIN_SIDE):
                        rows = pl.ds(w * WIN_TOK + i * WIN_SIDE, WIN_SIDE)
                        if at == 0:
                            pos_ref[rows, where] = jnp.broadcast_to(
                                table[i : i + 1, :], (WIN_SIDE, quarter)
                            )
                        else:
                            pos_ref[rows, where] = table
        stream = lat_ref[b].astype(F32) + pos_ref[...]
        scale = lax.rsqrt(jnp.mean(stream * stream, axis=-1, keepdims=True) + EPS)
        normed = (stream * scale * gain).astype(BF)
        out_ref[:, pl.ds(pl.multiple_of(b * 128, 128), 128)] = normed.T


def normed_columns(latents, window_index, norm_gain):
    blocks, rows, width = latents.shape
    quarter = width // 4
    freq = jnp.exp(jnp.arange(quarter, dtype=F32) * (-math.log(10000.0) / quarter))
    return pl.pallas_call(
        norm_kernel,
        out_shape=jax.ShapeDtypeStruct((width, blocks * rows), BF),
        in_specs=[sspec(), vspec(), vspec(), vspec()],
        out_specs=vspec(),
        scratch_shapes=[pltpu.VMEM((rows, width), F32)],
        compiler_params=params(24),
        cost_estimate=cost(40 * blocks * rows * width, 4 * blocks * rows * width),
        name="norm",
    )(window_index, latents, norm_gain.reshape(1, width), freq.reshape(1, quarter))


def places(x, y):
    return ((x, y), (1 - x, y), (x, 1 - y), (1 - x, 1 - y))


def piece_rows(ref, spot, start, rows):
    part = pl.ds(start, rows)
    return ref.at[part, :] if spot is None else ref.at[spot, part, :]


def start_columns(at_ref, pieces, spots, rows, w_ref, sems):
    x, y, core = at_ref[0], at_ref[1], at_ref[2]
    lanes = w_ref.shape[1] // 2
    for i, (px, py) in enumerate(places(x, y)):
        for owner, c in ((0, core), (1, 1 - core)):
            row = pl.multiple_of((2 * py + c) * rows, 16)
            lane = pl.multiple_of(px * lanes, 128)
            pltpu.make_async_copy(
                piece_rows(pieces[4 * owner + i], spots[4 * owner + i], 0, rows),
                w_ref.at[pl.ds(row, rows), pl.ds(lane, lanes)],
                sems.at[py * 4 + 2 * owner + i % 2],
            ).start()


def wait_columns(half, pieces, spots, rows, w_ref, sems):
    lanes = w_ref.shape[1] // 2
    for i in range(4):
        pltpu.make_async_copy(
            piece_rows(pieces[0], spots[0], 0, rows),
            w_ref.at[pl.ds(0, rows), pl.ds(0, lanes)],
            sems.at[4 * half + i],
        ).wait()


def project_chunk(m, which, parts, w_ref, n_ref):
    tokens = n_ref.shape[1]
    chunk = n_ref.shape[0] // parts
    got = jnp.dot(w_ref[m * chunk : (m + 1) * chunk, :], n_ref[...], preferred_element_type=F32)
    got = got.reshape(chunk // HEAD_DIM, HEAD_DIM, tokens)
    ms = jnp.mean(got * got, axis=1, keepdims=True)
    scale = jnp.where(which < 2 * parts, lax.rsqrt(ms + EPS), 1.0)
    scale = jnp.where(which < parts, scale * HEAD_DIM**-0.5, scale)
    return (got * scale).astype(BF).reshape(chunk, tokens)


def project_kernel(spots, parts, at_ref, plane_ref, n_ref, *rest):
    pieces, (p_ref, k_ref, w_ref, rows_ref, cols_ref, sems, out_sems) = rest[:8], rest[8:]
    rows = w_ref.shape[0] // 4
    start_columns(at_ref, pieces, spots, rows, w_ref, sems)
    count = p_ref.shape[0]
    for m in range(count):
        if m < 2:
            wait_columns(m, pieces, spots, rows, w_ref, sems)
        which = plane_ref[0] * count + m
        out = project_chunk(m, which, parts, w_ref, n_ref)
        rows_ref[m] = out
        cols_ref[m] = out.T
        is_key = (which >= parts) & (which < 2 * parts)

        @pl.when(is_key)
        def _():
            pltpu.make_async_copy(cols_ref.at[m], k_ref.at[m], out_sems.at[m]).start()

        @pl.when(jnp.logical_not(is_key))
        def _():
            pltpu.make_async_copy(rows_ref.at[m], p_ref.at[m], out_sems.at[m]).start()

    for m in range(count):
        pltpu.make_async_copy(rows_ref.at[m], p_ref.at[m], out_sems.at[m]).wait()


def project(place, plane, normed, pieces, rows):
    width, tokens = normed.shape
    parts = 4
    chunk = width // parts
    count = 4 * rows // chunk
    return pl.pallas_call(
        functools.partial(project_kernel, [spot for _, spot in pieces], parts),
        out_shape=(
            pltpu.HBM((count, chunk, tokens), BF),
            pltpu.HBM((count, tokens, chunk), BF),
        ),
        in_specs=[sspec(), sspec(), vspec()] + [hspec()] * 8,
        out_specs=(hspec(), hspec()),
        scratch_shapes=[
            pltpu.VMEM((4 * rows, width), BF),
            pltpu.VMEM((count, chunk, tokens), BF),
            pltpu.VMEM((count, tokens, chunk), BF),
            pltpu.SemaphoreType.DMA((8,)),
            pltpu.SemaphoreType.DMA((count,)),
        ],
        compiler_params=params(24),
        cost_estimate=cost(8 * rows * width * tokens, 2 * (4 * rows + tokens) * width),
        name="project",
    )(place, plane, normed, *[far(value) for value, _ in pieces])


def finish_kernel(
    spots, rows, at_ref, planes_ref, lens_ref, live_ref, n_ref, lat_ref, p0, k0, p1, k1, p2, k2, *rest
):
    pieces, rest = rest[:-15], rest[-15:]
    out_ref, w_ref, q_ref, k_ref, v_ref, mask_ref, e_ref, att_ref, wo_ref, done_ref = rest[:10]
    w_sems, part_sems, wo_sems, out_sems, base_sems = rest[10:]
    parts, chunk, tokens = q_ref.shape
    count = p0.shape[0]
    slots = wo_ref.shape[0]
    last = slots - 1
    x, y, core = at_ref[0], at_ref[1], at_ref[2]

    start_columns(at_ref, pieces[8 * last :], spots[8 * last :], rows, w_ref, w_sems)
    for s, (p, k) in enumerate(((p0, k0), (p1, k1), (p2, k2))):
        for m in range(count):
            which = planes_ref[s] * count + m
            for kind, (src, to) in enumerate(((p, q_ref), (k, k_ref), (p, v_ref))):

                @pl.when(which // parts == kind)
                def _():
                    pltpu.make_async_copy(src.at[m], to.at[which % parts], part_sems.at[which]).start()

    cols, lanes = wo_ref.shape[1], wo_ref.shape[2] // 2
    ours = cols // 4
    skip = pieces[0].shape[-2] - ours
    copies = []
    for s in range(slots):
        for owner, c in ((0, core), (1, 1 - core)):
            for i, (px, py) in enumerate(places(x, y)):
                at = 8 * s + 4 * owner + i
                row = pl.multiple_of((2 * py + c) * ours, 16)
                lane = pl.multiple_of(px * lanes, 128)
                copies.append(
                    pltpu.make_async_copy(
                        piece_rows(pieces[at], spots[at], skip, ours),
                        wo_ref.at[s, pl.ds(row, ours), pl.ds(lane, lanes)],
                        wo_sems.at[at],
                    )
                )
    bases = []
    for s in range(slots):
        spot = pl.ds(pl.multiple_of(planes_ref[s] * cols, 128), cols)
        bases.append(pltpu.make_async_copy(lat_ref.at[:, spot], done_ref.at[s], base_sems.at[s]))
    blocks = tokens // 128
    key = lax.broadcasted_iota(jnp.int32, (128, 256), 0)
    query = lax.broadcasted_iota(jnp.int32, (128, 256), 1) % 128
    for b in range(blocks):
        first = (key < WIN_TOK) & (query < WIN_TOK) & (key < lens_ref[2 * b])
        second = (key >= WIN_TOK) & (query >= WIN_TOK) & (key - WIN_TOK < lens_ref[2 * b + 1])
        mask_ref[b] = jnp.where(first | second, 1.0, 0.0).astype(F32)

    for m in range(count):
        if m < 2:
            wait_columns(m, pieces[8 * last :], spots[8 * last :], rows, w_ref, w_sems)
        which = planes_ref[last] * count + m
        for c in (copies + bases)[m::count]:
            c.start()
        out = project_chunk(m, which, parts, w_ref, n_ref)
        for kind, to in ((0, q_ref), (1, k_ref), (2, v_ref)):

            @pl.when(which // parts == kind)
            def _():
                to[which % parts] = out.T if kind == 1 else out

    ones = jnp.ones((16, 128), BF)
    blank = jnp.zeros((HEAD_DIM, 128), BF)
    pairs = chunk // 128

    for which in range(3 * parts):

        @pl.when(planes_ref[which // count] != last)
        def _():
            pltpu.make_async_copy(p0.at[0], q_ref.at[0], part_sems.at[which]).wait()

    def weigh(pair):
        part = pair // pairs
        at = pl.ds(pl.multiple_of(pair % pairs * 128, 128), 128)
        for b in range(blocks):
            tok = pl.ds(b * 128, 128)
            q = q_ref[part, at, tok]
            k = k_ref[part, tok, at]
            q0 = jnp.concatenate([q[:HEAD_DIM], blank], axis=0)
            q1 = jnp.concatenate([blank, q[HEAD_DIM:]], axis=0)
            scores = jnp.dot(k, jnp.concatenate([q0, q1], axis=1), preferred_element_type=F32)
            e_ref[pair % 2, b] = (jnp.exp(scores) * mask_ref[b]).astype(BF)

    def gather(pair):
        part = pair // pairs
        at = pl.ds(pl.multiple_of(pair % pairs * 128, 128), 128)
        out_at = pl.ds(pl.multiple_of(pair * 128, 128), 128)
        for b in range(blocks):
            tok = pl.ds(b * 128, 128)
            v = v_ref[part, at, tok]
            got = jnp.dot(
                jnp.concatenate([v, ones], axis=0), e_ref[pair % 2, b], preferred_element_type=F32
            )
            token = lax.broadcasted_iota(jnp.int32, (1, 256), 1) % 128
            first = (token < WIN_TOK) & (token < lens_ref[2 * b])
            second = (token >= WIN_TOK) & (token - WIN_TOK < lens_ref[2 * b + 1])
            keep = (first | second) & (b < live_ref[0])
            share = jnp.where(keep, 1.0 / got[128:129, :], 0.0)
            o0 = got[:HEAD_DIM, :128] * share[:, :128]
            o1 = got[HEAD_DIM:128, 128:] * share[:, 128:]
            att_ref[tok, out_at] = jnp.concatenate([o0, o1], axis=0).astype(BF).T

    weigh(0)

    @pl.loop(0, parts)
    def _(part):
        for i in range(pairs):
            pair = part * pairs + i
            gather(pair)
            weigh(jnp.minimum(pair + 1, parts * pairs - 1))

    outs = []
    for s in range(slots):
        for c in copies[8 * s : 8 * s + 8] + [bases[s]]:
            c.wait()
        spot = pl.ds(pl.multiple_of(planes_ref[s] * cols, 128), cols)
        for h in range(2):
            part = pl.ds(h * tokens // 2, tokens // 2)
            update = lax.dot_general(
                att_ref[part, :], wo_ref[s], (((1,), (1,)), ((), ())), preferred_element_type=F32
            )
            done_ref[s, part, :] = (done_ref[s, part, :].astype(F32) + update).astype(BF)
            outs.append(
                pltpu.make_async_copy(
                    done_ref.at[s, part], out_ref.at[part, spot], out_sems.at[2 * s + h]
                )
            )
            outs[-1].start()
    for c in outs:
        c.wait()


def finish(place, planes, window_len, live_blocks, normed, latents, parts, pieces, rows):
    count, chunk, tokens = parts[0][0].shape
    width = normed.shape[0]
    slots = len(pieces) // 8
    return pl.pallas_call(
        functools.partial(finish_kernel, [spot for _, spot in pieces], rows),
        out_shape=jax.ShapeDtypeStruct((tokens, width), BF),
        in_specs=[sspec()] * 4 + [vspec()] + [hspec()] * (7 + len(pieces)),
        out_specs=hspec(),
        scratch_shapes=[
            pltpu.VMEM((4 * rows, width), BF),
            pltpu.VMEM((4, chunk, tokens), BF),
            pltpu.VMEM((4, tokens, chunk), BF),
            pltpu.VMEM((4, chunk, tokens), BF),
            pltpu.VMEM((tokens // 128, 128, 256), F32),
            pltpu.VMEM((2, tokens // 128, 128, 256), BF),
            pltpu.VMEM((tokens, width), BF),
            pltpu.VMEM((slots, width // slots, width), BF),
            pltpu.VMEM((slots, tokens, width // slots), BF),
            pltpu.SemaphoreType.DMA((8,)),
            pltpu.SemaphoreType.DMA((4 * count,)),
            pltpu.SemaphoreType.DMA((len(pieces),)),
            pltpu.SemaphoreType.DMA((2 * slots,)),
            pltpu.SemaphoreType.DMA((slots,)),
        ],
        compiler_params=params(44),
        cost_estimate=cost(6 * width * width * tokens, 8 * width * tokens),
        name="finish",
    )(
        place,
        planes,
        window_len,
        live_blocks,
        normed,
        far(latents),
        *[far(a) for pair in parts for a in pair],
        *[far(value) for value, _ in pieces[:-8]],
        *[value for value, _ in pieces[-8:]],
    )


def local(tile_count, latents, window_index, window_len, live_blocks, norm_gain, w_qkv, w_out):
    blocks, rows, width = latents.shape

    def along(axis, pairs):
        def move(value, name):
            with jax.named_scope(name):
                return lax.ppermute(value, axis, pairs)

        return move

    def across(bit):
        return along("tile", [(i, i ^ bit) for i in range(tile_count)])

    core, ys, z1, z2 = across(1), across(2), across(4), across(8)
    xs = along("group", [(0, 1), (1, 0)])
    xy = along(
        ("tile", "group"),
        [(2 * i + g, 2 * (i ^ 2) + 1 - g) for i in range(tile_count) for g in range(2)],
    )
    t = lax.axis_index("tile")
    x = lax.axis_index("group")
    z = t // 4
    place = jnp.stack([x, t // 2 % 2, t % 2]).astype(jnp.int32)
    planes = jnp.stack([z, z ^ 1, z ^ 2, z ^ 3]).astype(jnp.int32)

    nq = w_qkv.shape[1]

    def sync(*values):
        return lax.optimization_barrier(values)

    def share(**values):
        shared = []
        for name, value in values.items():
            if shared:
                value = sync(value, shared[-1])[0]
            shared.append(core(value, f"core_{name}"))
        return shared

    def slot(index, *values):
        return [(value, index if value.ndim == 3 else None) for value in values]

    u0 = jnp.concatenate([w_qkv.T, w_out.T], axis=0)
    u1, d0, x0, y0, u2 = z1(u0, "u1"), xy(u0, "d0"), xs(u0, "x0"), ys(u0, "y0"), z2(u0, "u2")
    normed = normed_columns(latents, window_index, norm_gain)
    cu0 = core(u0, "core_u0")
    u1, d0, x0, y0, u2, normed, cu0 = sync(u1, d0, x0, y0, u2, normed, cu0)
    u12 = jnp.stack([u1, u2])
    x2, y12, u3, d1 = xs(u2, "x2"), ys(u12, "y12"), z1(u2, "u3"), z1(d0, "d1")
    cx0, cy0 = core(x0, "core_x0"), core(y0, "core_y0")
    x2, y12, u3, d1, cx0, cy0, u12 = sync(x2, y12, u3, d1, cx0, cy0, u12)
    x1, d2 = xs(u1, "x1"), ys(x2, "d2")
    cd0, cx2, cy12, cu12 = (
        core(value, name) for value, name in ((d0, "core_d0"), (x2, "core_x2"), (y12, "core_y12"), (u12, "core_u12"))
    )
    s0 = slot(0, u0, x0, y0, d0, cu0, cx0, cy0, cd0)
    p0 = project(place, planes[0:1], normed, s0, nq)
    x1, d2, cx2, cy12, cu12, d1, u3, p0 = sync(x1, d2, cx2, cy12, cu12, d1, u3, p0)
    x3, y3, d3 = xs(u3, "x3"), ys(u3, "y3"), z1(d2, "d3")
    cd2, cx1, cd1 = core(d2, "core_d2"), core(x1, "core_x1"), core(d1, "core_d1")
    cu3 = core(u3, "core_u3")
    s2 = slot(1, u12, x2, y12, d2, cu12, cx2, cy12, cd2)
    p2 = project(place, planes[2:3], normed, s2, nq)
    s1 = slot(0, u12, x1, y12, d1, cu12, cx1, cy12, cd1)
    p1 = project(place, planes[1:2], normed, s1, nq)
    x3, y3, d3, u3, cu3, p2, p1 = sync(x3, y3, d3, u3, cu3, p2, p1)
    cx3, cy3, cd3 = core(x3, "core_x3"), core(y3, "core_y3"), core(d3, "core_d3")
    s3 = slot(0, u3, x3, y3, d3, cu3, cx3, cy3, cd3)
    flat = latents.reshape(blocks * rows, width)
    so = s0 + s1 + s2 + s3
    out = finish(place, planes, window_len, live_blocks, normed, flat, (p0, p1, p2), so, nq)
    return out.reshape(latents.shape)


def solution(mesh):
    in_specs = (
        P(("tile", "group"), None, None),
        P(("tile", "group")),
        P(("tile", "group")),
        P(("tile", "group")),
        P(),
        P("group", "tile"),
        P("group", "tile"),
    )
    out_specs = P(("tile", "group"), None, None)
    planes, chips, cores = 4, 2, 2
    if mesh.shape["group"] == 2 and mesh.shape["tile"] == planes * chips * cores:
        body = functools.partial(local, mesh.shape["tile"])
    else:
        body = general
    return jax.shard_map(body, mesh=mesh, in_specs=in_specs, out_specs=out_specs, check_vma=False)
```

```python
import functools
import math

import jax
import jax.numpy as jnp
from jax import lax
from jax.experimental import pallas as pl
from jax.experimental.pallas import tpu as pltpu
from jax.sharding import PartitionSpec as P

HEAD_DIM = 64
WIN_SIDE = 8
WIN_COLS = 60
WIN_TOK = 64
EPS = 1e-06
BF = jnp.bfloat16
F32 = jnp.float32


def position_table(window_ids, width):
    token_ids = jnp.arange(WIN_TOK, dtype=jnp.int32)
    row_pos = window_ids[:, None] // WIN_COLS * WIN_SIDE + token_ids[None, :] // WIN_SIDE
    col_pos = window_ids[:, None] % WIN_COLS * WIN_SIDE + token_ids[None, :] % WIN_SIDE
    quarter = width // 4
    frequency = jnp.exp(jnp.arange(quarter, dtype=F32) * (-math.log(10000.0) / quarter))
    row_angle = row_pos.astype(F32)[:, :, None] * frequency
    col_angle = col_pos.astype(F32)[:, :, None] * frequency
    return jnp.concatenate(
        [jnp.sin(row_angle), jnp.cos(row_angle), jnp.sin(col_angle), jnp.cos(col_angle)], axis=-1
    )


def head_norm(values):
    return (values * lax.rsqrt(jnp.mean(values * values, axis=-1, keepdims=True) + EPS)).astype(BF)


def window_layer(blocks_in, window_ids, window_lens, norm_gain, w_qkv, w_out):
    width = blocks_in.shape[-1]
    count = window_ids.shape[0]
    heads = width // HEAD_DIM
    stream = blocks_in.reshape(count, WIN_TOK, width).astype(F32) + position_table(window_ids, width)
    scale = lax.rsqrt(jnp.mean(stream * stream, axis=-1, keepdims=True) + EPS)
    normed = (stream * scale * norm_gain).astype(BF).reshape(count * WIN_TOK, width)
    full_rows = lax.all_gather(w_qkv, "group", axis=0, tiled=True)
    projected = jnp.dot(
        normed,
        lax.all_gather(full_rows, "tile", axis=1, tiled=True),
        preferred_element_type=F32,
    ).reshape(count, WIN_TOK, 3, heads, HEAD_DIM)
    queries = head_norm(projected[:, :, 0])
    keys = head_norm(projected[:, :, 1])
    values = projected[:, :, 2].astype(BF)
    scores = jnp.einsum("wqhd,wkhd->whqk", queries, keys, preferred_element_type=F32) * HEAD_DIM**-0.5
    key_mask = jnp.arange(WIN_TOK, dtype=jnp.int32)[None, :] < window_lens[:, None]
    weights = jnp.exp(scores) * key_mask[:, None, None, :].astype(F32)
    probs = (weights / jnp.sum(weights, axis=-1, keepdims=True)).astype(BF)
    attended = jnp.einsum("whqk,wkhd->wqhd", probs, values, preferred_element_type=F32)
    attended = attended.astype(BF).reshape(count * WIN_TOK, width)
    out_rows = lax.all_gather(w_out, "group", axis=0, tiled=True)
    update = jnp.dot(
        attended, lax.all_gather(out_rows, "tile", axis=1, tiled=True), preferred_element_type=F32
    )
    base = blocks_in.reshape(count * WIN_TOK, width).astype(F32)
    token_live = key_mask.reshape(count * WIN_TOK)[:, None]
    return jnp.where(token_live, base + update, base).astype(BF).reshape(blocks_in.shape)


def general(latents, window_index, window_len, live_blocks, norm_gain, w_qkv, w_out):
    slot_ids = jnp.arange(latents.shape[0], dtype=jnp.int32)
    live_mask = (slot_ids < live_blocks[0])[:, None, None]
    finished = window_layer(latents, window_index, window_len, norm_gain, w_qkv, w_out)
    return jnp.where(live_mask, finished, latents)


def hspec():
    return pl.BlockSpec(memory_space=pltpu.HBM)


def vspec():
    return pl.BlockSpec(memory_space=pltpu.VMEM)


def sspec():
    return pl.BlockSpec(memory_space=pltpu.SMEM)


def params(mib):
    return pltpu.CompilerParams(vmem_limit_bytes=mib * 1024 * 1024)


def far(value):
    return pltpu.with_memory_space_constraint(value, pltpu.HBM)


def cost(flops, moved):
    return pl.CostEstimate(flops=flops, bytes_accessed=moved, transcendentals=0)


def norm_kernel(ids_ref, lat_ref, gain_ref, freq_ref, out_ref, pos_ref):
    blocks, _, width = lat_ref.shape
    quarter = width // 4
    freq = freq_ref[...]
    step = lax.broadcasted_iota(jnp.int32, (WIN_SIDE, quarter), 0).astype(F32) * freq
    sin_step, cos_step = jnp.sin(step), jnp.cos(step)
    gain = gain_ref[...]

    @pl.loop(0, blocks)
    def _(b):
        for w in range(2):
            place = ids_ref[2 * b + w]
            row = (place // WIN_COLS * WIN_SIDE).astype(F32)
            col = (place % WIN_COLS * WIN_SIDE).astype(F32)
            for at, start in ((0, row), (2 * quarter, col)):
                base = start * freq
                sin_base, cos_base = jnp.sin(base), jnp.cos(base)
                sines = sin_base * cos_step + cos_base * sin_step
                cosines = cos_base * cos_step - sin_base * sin_step
                for more, table in ((0, sines), (quarter, cosines)):
                    where = pl.ds(at + more, quarter)
                    for i in range(WIN_SIDE):
                        rows = pl.ds(w * WIN_TOK + i * WIN_SIDE, WIN_SIDE)
                        if at == 0:
                            pos_ref[rows, where] = jnp.broadcast_to(
                                table[i : i + 1, :], (WIN_SIDE, quarter)
                            )
                        else:
                            pos_ref[rows, where] = table
        stream = lat_ref[b].astype(F32) + pos_ref[...]
        scale = lax.rsqrt(jnp.mean(stream * stream, axis=-1, keepdims=True) + EPS)
        normed = (stream * scale * gain).astype(BF)
        out_ref[:, pl.ds(pl.multiple_of(b * 128, 128), 128)] = normed.T


def normed_columns(latents, window_index, norm_gain):
    blocks, rows, width = latents.shape
    quarter = width // 4
    freq = jnp.exp(jnp.arange(quarter, dtype=F32) * (-math.log(10000.0) / quarter))
    return pl.pallas_call(
        norm_kernel,
        out_shape=jax.ShapeDtypeStruct((width, blocks * rows), BF),
        in_specs=[sspec(), vspec(), vspec(), vspec()],
        out_specs=vspec(),
        scratch_shapes=[pltpu.VMEM((rows, width), F32)],
        compiler_params=params(24),
        cost_estimate=cost(40 * blocks * rows * width, 4 * blocks * rows * width),
        name="norm",
    )(window_index, latents, norm_gain.reshape(1, width), freq.reshape(1, quarter))


def places(x, y):
    return ((x, y), (1 - x, y), (x, 1 - y), (1 - x, 1 - y))


def piece_rows(ref, spot, start, rows):
    part = pl.ds(start, rows)
    return ref.at[part, :] if spot is None else ref.at[spot, part, :]


def start_columns(at_ref, pieces, spots, rows, w_ref, sems):
    x, y, core = at_ref[0], at_ref[1], at_ref[2]
    lanes = w_ref.shape[1] // 2
    for i, (px, py) in enumerate(places(x, y)):
        for owner, c in ((0, core), (1, 1 - core)):
            row = pl.multiple_of((2 * py + c) * rows, 16)
            lane = pl.multiple_of(px * lanes, 128)
            pltpu.make_async_copy(
                piece_rows(pieces[4 * owner + i], spots[4 * owner + i], 0, rows),
                w_ref.at[pl.ds(row, rows), pl.ds(lane, lanes)],
                sems.at[py * 4 + 2 * owner + i % 2],
            ).start()


def wait_columns(half, pieces, spots, rows, w_ref, sems):
    lanes = w_ref.shape[1] // 2
    for i in range(4):
        pltpu.make_async_copy(
            piece_rows(pieces[0], spots[0], 0, rows),
            w_ref.at[pl.ds(0, rows), pl.ds(0, lanes)],
            sems.at[4 * half + i],
        ).wait()


def project_chunk(m, which, parts, w_ref, n_ref):
    tokens = n_ref.shape[1]
    chunk = n_ref.shape[0] // parts
    got = jnp.dot(w_ref[m * chunk : (m + 1) * chunk, :], n_ref[...], preferred_element_type=F32)
    got = got.reshape(chunk // HEAD_DIM, HEAD_DIM, tokens)
    ms = jnp.mean(got * got, axis=1, keepdims=True)
    scale = jnp.where(which < 2 * parts, lax.rsqrt(ms + EPS), 1.0)
    scale = jnp.where(which < parts, scale * HEAD_DIM**-0.5, scale)
    return (got * scale).astype(BF).reshape(chunk, tokens)


def project_kernel(spots, parts, at_ref, plane_ref, n_ref, *rest):
    pieces, (p_ref, k_ref, w_ref, rows_ref, cols_ref, sems, out_sems) = rest[:8], rest[8:]
    rows = w_ref.shape[0] // 4
    start_columns(at_ref, pieces, spots, rows, w_ref, sems)
    count = p_ref.shape[0]
    for m in range(count):
        if m < 2:
            wait_columns(m, pieces, spots, rows, w_ref, sems)
        which = plane_ref[0] * count + m
        out = project_chunk(m, which, parts, w_ref, n_ref)
        rows_ref[m] = out
        cols_ref[m] = out.T
        is_key = (which >= parts) & (which < 2 * parts)

        @pl.when(is_key)
        def _():
            pltpu.make_async_copy(cols_ref.at[m], k_ref.at[m], out_sems.at[m]).start()

        @pl.when(jnp.logical_not(is_key))
        def _():
            pltpu.make_async_copy(rows_ref.at[m], p_ref.at[m], out_sems.at[m]).start()

    for m in range(count):
        pltpu.make_async_copy(rows_ref.at[m], p_ref.at[m], out_sems.at[m]).wait()


def project(place, plane, normed, pieces, rows):
    width, tokens = normed.shape
    parts = 4
    chunk = width // parts
    count = 4 * rows // chunk
    return pl.pallas_call(
        functools.partial(project_kernel, [spot for _, spot in pieces], parts),
        out_shape=(
            pltpu.HBM((count, chunk, tokens), BF),
            pltpu.HBM((count, tokens, chunk), BF),
        ),
        in_specs=[sspec(), sspec(), vspec()] + [hspec()] * 8,
        out_specs=(hspec(), hspec()),
        scratch_shapes=[
            pltpu.VMEM((4 * rows, width), BF),
            pltpu.VMEM((count, chunk, tokens), BF),
            pltpu.VMEM((count, tokens, chunk), BF),
            pltpu.SemaphoreType.DMA((8,)),
            pltpu.SemaphoreType.DMA((count,)),
        ],
        compiler_params=params(24),
        cost_estimate=cost(8 * rows * width * tokens, 2 * (4 * rows + tokens) * width),
        name="project",
    )(place, plane, normed, *[far(value) for value, _ in pieces])


def finish_kernel(
    spots, rows, at_ref, planes_ref, lens_ref, live_ref, n_ref, lat_ref, p0, k0, p1, k1, p2, k2, *rest
):
    pieces, rest = rest[:-15], rest[-15:]
    out_ref, w_ref, q_ref, k_ref, v_ref, mask_ref, e_ref, att_ref, wo_ref, done_ref = rest[:10]
    w_sems, part_sems, wo_sems, out_sems, base_sems = rest[10:]
    parts, chunk, tokens = q_ref.shape
    count = p0.shape[0]
    slots = wo_ref.shape[0]
    last = slots - 1
    x, y, core = at_ref[0], at_ref[1], at_ref[2]

    start_columns(at_ref, pieces[8 * last :], spots[8 * last :], rows, w_ref, w_sems)
    for s, (p, k) in enumerate(((p0, k0), (p1, k1), (p2, k2))):
        for m in range(count):
            which = planes_ref[s] * count + m
            for kind, (src, to) in enumerate(((p, q_ref), (k, k_ref), (p, v_ref))):

                @pl.when(which // parts == kind)
                def _():
                    pltpu.make_async_copy(src.at[m], to.at[which % parts], part_sems.at[which]).start()

    cols, lanes = wo_ref.shape[1], wo_ref.shape[2] // 2
    ours = cols // 4
    skip = pieces[0].shape[-2] - ours
    copies = []
    for s in range(slots):
        for owner, c in ((0, core), (1, 1 - core)):
            for i, (px, py) in enumerate(places(x, y)):
                at = 8 * s + 4 * owner + i
                row = pl.multiple_of((2 * py + c) * ours, 16)
                lane = pl.multiple_of(px * lanes, 128)
                copies.append(
                    pltpu.make_async_copy(
                        piece_rows(pieces[at], spots[at], skip, ours),
                        wo_ref.at[s, pl.ds(row, ours), pl.ds(lane, lanes)],
                        wo_sems.at[at],
                    )
                )
    bases = []
    for s in range(slots):
        spot = pl.ds(pl.multiple_of(planes_ref[s] * cols, 128), cols)
        bases.append(pltpu.make_async_copy(lat_ref.at[:, spot], done_ref.at[s], base_sems.at[s]))
    blocks = tokens // 128
    key = lax.broadcasted_iota(jnp.int32, (128, 256), 0)
    query = lax.broadcasted_iota(jnp.int32, (128, 256), 1) % 128
    for b in range(blocks):
        first = (key < WIN_TOK) & (query < WIN_TOK) & (key < lens_ref[2 * b])
        second = (key >= WIN_TOK) & (query >= WIN_TOK) & (key - WIN_TOK < lens_ref[2 * b + 1])
        mask_ref[b] = jnp.where(first | second, 1.0, 0.0).astype(F32)

    for m in range(count):
        if m < 2:
            wait_columns(m, pieces[8 * last :], spots[8 * last :], rows, w_ref, w_sems)
        which = planes_ref[last] * count + m
        for c in (copies + bases)[m::count]:
            c.start()
        out = project_chunk(m, which, parts, w_ref, n_ref)
        for kind, to in ((0, q_ref), (1, k_ref), (2, v_ref)):

            @pl.when(which // parts == kind)
            def _():
                to[which % parts] = out.T if kind == 1 else out

    ones = jnp.ones((16, 128), BF)
    blank = jnp.zeros((HEAD_DIM, 128), BF)
    pairs = chunk // 128

    for which in range(3 * parts):

        @pl.when(planes_ref[which // count] != last)
        def _():
            pltpu.make_async_copy(p0.at[0], q_ref.at[0], part_sems.at[which]).wait()

    def weigh(pair):
        part = pair // pairs
        at = pl.ds(pl.multiple_of(pair % pairs * 128, 128), 128)
        for b in range(blocks):
            tok = pl.ds(b * 128, 128)
            q = q_ref[part, at, tok]
            k = k_ref[part, tok, at]
            q0 = jnp.concatenate([q[:HEAD_DIM], blank], axis=0)
            q1 = jnp.concatenate([blank, q[HEAD_DIM:]], axis=0)
            scores = jnp.dot(k, jnp.concatenate([q0, q1], axis=1), preferred_element_type=F32)
            e_ref[pair % 2, b] = (jnp.exp(scores) * mask_ref[b]).astype(BF)

    def gather(pair):
        part = pair // pairs
        at = pl.ds(pl.multiple_of(pair % pairs * 128, 128), 128)
        out_at = pl.ds(pl.multiple_of(pair * 128, 128), 128)
        for b in range(blocks):
            tok = pl.ds(b * 128, 128)
            v = v_ref[part, at, tok]
            got = jnp.dot(
                jnp.concatenate([v, ones], axis=0), e_ref[pair % 2, b], preferred_element_type=F32
            )
            token = lax.broadcasted_iota(jnp.int32, (1, 256), 1) % 128
            first = (token < WIN_TOK) & (token < lens_ref[2 * b])
            second = (token >= WIN_TOK) & (token - WIN_TOK < lens_ref[2 * b + 1])
            keep = (first | second) & (b < live_ref[0])
            share = jnp.where(keep, 1.0 / got[128:129, :], 0.0)
            o0 = got[:HEAD_DIM, :128] * share[:, :128]
            o1 = got[HEAD_DIM:128, 128:] * share[:, 128:]
            att_ref[tok, out_at] = jnp.concatenate([o0, o1], axis=0).astype(BF).T

    weigh(0)

    @pl.loop(0, parts)
    def _(part):
        for i in range(pairs):
            pair = part * pairs + i
            gather(pair)
            weigh(jnp.minimum(pair + 1, parts * pairs - 1))

    outs = []
    for s in range(slots):
        for c in copies[8 * s : 8 * s + 8] + [bases[s]]:
            c.wait()
        spot = pl.ds(pl.multiple_of(planes_ref[s] * cols, 128), cols)
        for h in range(2):
            part = pl.ds(h * tokens // 2, tokens // 2)
            update = lax.dot_general(
                att_ref[part, :], wo_ref[s], (((1,), (1,)), ((), ())), preferred_element_type=F32
            )
            done_ref[s, part, :] = (done_ref[s, part, :].astype(F32) + update).astype(BF)
            outs.append(
                pltpu.make_async_copy(
                    done_ref.at[s, part], out_ref.at[part, spot], out_sems.at[2 * s + h]
                )
            )
            outs[-1].start()
    for c in outs:
        c.wait()


def finish(place, planes, window_len, live_blocks, normed, latents, parts, pieces, rows):
    count, chunk, tokens = parts[0][0].shape
    width = normed.shape[0]
    slots = len(pieces) // 8
    return pl.pallas_call(
        functools.partial(finish_kernel, [spot for _, spot in pieces], rows),
        out_shape=jax.ShapeDtypeStruct((tokens, width), BF),
        in_specs=[sspec()] * 4 + [vspec()] + [hspec()] * (7 + len(pieces)),
        out_specs=hspec(),
        scratch_shapes=[
            pltpu.VMEM((4 * rows, width), BF),
            pltpu.VMEM((4, chunk, tokens), BF),
            pltpu.VMEM((4, tokens, chunk), BF),
            pltpu.VMEM((4, chunk, tokens), BF),
            pltpu.VMEM((tokens // 128, 128, 256), F32),
            pltpu.VMEM((2, tokens // 128, 128, 256), BF),
            pltpu.VMEM((tokens, width), BF),
            pltpu.VMEM((slots, width // slots, width), BF),
            pltpu.VMEM((slots, tokens, width // slots), BF),
            pltpu.SemaphoreType.DMA((8,)),
            pltpu.SemaphoreType.DMA((4 * count,)),
            pltpu.SemaphoreType.DMA((len(pieces),)),
            pltpu.SemaphoreType.DMA((2 * slots,)),
            pltpu.SemaphoreType.DMA((slots,)),
        ],
        compiler_params=params(44),
        cost_estimate=cost(6 * width * width * tokens, 8 * width * tokens),
        name="finish",
    )(
        place,
        planes,
        window_len,
        live_blocks,
        normed,
        far(latents),
        *[far(a) for pair in parts for a in pair],
        *[far(value) for value, _ in pieces[:-8]],
        *[value for value, _ in pieces[-8:]],
    )


def local(tile_count, latents, window_index, window_len, live_blocks, norm_gain, w_qkv, w_out):
    blocks, rows, width = latents.shape

    def along(axis, pairs):
        def move(value, name):
            with jax.named_scope(name):
                return lax.ppermute(value, axis, pairs)

        return move

    def across(bit):
        return along("tile", [(i, i ^ bit) for i in range(tile_count)])

    core, ys, z1, z2 = across(1), across(2), across(4), across(8)
    xs = along("group", [(0, 1), (1, 0)])
    xy = along(
        ("tile", "group"),
        [(2 * i + g, 2 * (i ^ 2) + 1 - g) for i in range(tile_count) for g in range(2)],
    )
    t = lax.axis_index("tile")
    x = lax.axis_index("group")
    z = t // 4
    place = jnp.stack([x, t // 2 % 2, t % 2]).astype(jnp.int32)
    planes = jnp.stack([z, z ^ 1, z ^ 2, z ^ 3]).astype(jnp.int32)

    nq = w_qkv.shape[1]

    def sync(*values):
        return lax.optimization_barrier(values)

    def share(**values):
        shared = []
        for name, value in values.items():
            if shared:
                value = sync(value, shared[-1])[0]
            shared.append(core(value, f"core_{name}"))
        return shared

    def slot(index, *values):
        return [(value, index if value.ndim == 3 else None) for value in values]

    u0 = jnp.concatenate([w_qkv.T, w_out.T], axis=0)
    u1, d0, x0, y0, u2 = z1(u0, "u1"), xy(u0, "d0"), xs(u0, "x0"), ys(u0, "y0"), z2(u0, "u2")
    normed = normed_columns(latents, window_index, norm_gain)
    cu0 = core(u0, "core_u0")
    u1, d0, x0, y0, u2, normed, cu0 = sync(u1, d0, x0, y0, u2, normed, cu0)
    u12 = jnp.stack([u1, u2])
    x2, y12, u3, d1 = xs(u2, "x2"), ys(u12, "y12"), z1(u2, "u3"), z1(d0, "d1")
    cx0, cy0 = core(x0, "core_x0"), core(y0, "core_y0")
    x2, y12, u3, d1, cx0, cy0, u12 = sync(x2, y12, u3, d1, cx0, cy0, u12)
    x1, d2 = xs(u1, "x1"), ys(x2, "d2")
    cd0, cx2, cy12, cu12 = (
        core(value, name) for value, name in ((d0, "core_d0"), (x2, "core_x2"), (y12, "core_y12"), (u12, "core_u12"))
    )
    cu3 = core(sync(u3, cd0)[0], "core_u3")
    s0 = slot(0, u0, x0, y0, d0, cu0, cx0, cy0, cd0)
    p0 = project(place, planes[0:1], normed, s0, nq)
    x1, d2, cx2, cy12, cu12, cu3, d1, u3, p0 = sync(x1, d2, cx2, cy12, cu12, cu3, d1, u3, p0)
    x3, y3, d3 = xs(u3, "x3"), ys(u3, "y3"), z1(d2, "d3")
    cd2, cx1, cd1 = core(d2, "core_d2"), core(x1, "core_x1"), core(d1, "core_d1")
    s2 = slot(1, u12, x2, y12, d2, cu12, cx2, cy12, cd2)
    p2 = project(place, planes[2:3], normed, s2, nq)
    s1 = slot(0, u12, x1, y12, d1, cu12, cx1, cy12, cd1)
    p1 = project(place, planes[1:2], normed, s1, nq)
    x3, y3, d3, u3, cu3, p2, p1 = sync(x3, y3, d3, u3, cu3, p2, p1)
    cx3, cy3, cd3 = core(x3, "core_x3"), core(y3, "core_y3"), core(d3, "core_d3")
    s3 = slot(0, u3, x3, y3, d3, cu3, cx3, cy3, cd3)
    flat = latents.reshape(blocks * rows, width)
    so = s0 + s1 + s2 + s3
    out = finish(place, planes, window_len, live_blocks, normed, flat, (p0, p1, p2), so, nq)
    return out.reshape(latents.shape)


def solution(mesh):
    in_specs = (
        P(("tile", "group"), None, None),
        P(("tile", "group")),
        P(("tile", "group")),
        P(("tile", "group")),
        P(),
        P("group", "tile"),
        P("group", "tile"),
    )
    out_specs = P(("tile", "group"), None, None)
    planes, chips, cores = 4, 2, 2
    if mesh.shape["group"] == 2 and mesh.shape["tile"] == planes * chips * cores:
        body = functools.partial(local, mesh.shape["tile"])
    else:
        body = general
    return jax.shard_map(body, mesh=mesh, in_specs=in_specs, out_specs=out_specs, check_vma=False)
```
